32 devices in a mesh: dp: 4 (over z), blk: 8 (over y, x, core).
Axes of the slice: x: 2, y: 2, z: 4, core: 2. Of those that a mesh axis runs over, the one named last changes fastest.
Arguments:
- latents: bfloat16 [32, 64, 1536], P('dp', 'blk'), may hold values from -6 to 6
- media: bfloat16 [32, 256, 1536], P('dp', 'blk'), may hold values from -6 to 6
- media_lengths: int32 [32], P('dp'), may hold values from 1 to 256, as said below
- cotangent: bfloat16 [32, 64, 1536], P('dp', 'blk'), may hold values from -6 to 6
- query_weight: bfloat16 [1536, 1536], P(('dp', 'blk')), may hold values from -0.15625 to 0.15625
- kv_weight: bfloat16 [1536, 3072], P(('dp', 'blk')), may hold values from -0.15625 to 0.15625
- out_weight: bfloat16 [1536, 1536], P(('dp', 'blk')), may hold values from -1.25 to 1.25
- in_weight: bfloat16 [1536, 6144], P(('dp', 'blk')), may hold values from -0.15625 to 0.15625
- down_weight: bfloat16 [1536, 6144], P(('dp', 'blk')), may hold values from -0.078125 to 0.078125
- media_gain: bfloat16 [1536], P(('dp', 'blk')), may hold values from 0.5 to 1.5
- latent_gain: bfloat16 [1536], P(('dp', 'blk')), may hold values from 0.5 to 1.5
- ffn_gain: bfloat16 [1536], P(('dp', 'blk')), may hold values from 0.5 to 1.5
Outputs:
- resampled: bfloat16 [32, 64, 1536], P('dp', 'blk')
- latents_grad: float32 [32, 64, 1536], P('dp', 'blk')
- media_grad: float32 [32, 256, 1536], P('dp', 'blk')
- query_grad: float32 [1536, 1536], P(('dp', 'blk'))
- kv_grad: float32 [1536, 3072], P(('dp', 'blk'))
- out_grad: float32 [1536, 1536], P(('dp', 'blk'))
- in_grad: float32 [1536, 6144], P(('dp', 'blk'))
- down_grad: float32 [1536, 6144], P(('dp', 'blk'))
- media_gain_grad: float32 [1536], P(('dp', 'blk'))
- latent_gain_grad: float32 [1536], P(('dp', 'blk'))
- ffn_gain_grad: float32 [1536], P(('dp', 'blk'))
The draws below stay inside these ranges and needn't reach their ends.
Inputs may be any that keep to these rules, and one draw needn't show every extreme that they name: `media_lengths`: a prefix of each image's patch rows is valid; in each aligned block of 8 images one image has all 256.
All inputs are finite; a program needn't handle non-finite values.
Results may differ from the reference program's by a relative error of at most 0.04.
Values may be sent and summed in bfloat16 or wider, within the bound.
No kernel may reach another device: no remote copies, remote signals or barrier semaphores. Data moves between devices by JAX's collectives and lax.ppermute only.
A program may use at most 256 MiB of HBM per device.

```python
import math
import jax
import jax.numpy as jnp
from jax import lax

D = 1536
HEADS = 16
FF = 6144
PATCH = 256
LAT = 64
IMG_DEV = 8
IMAGES = 32


def draw_media_lengths(key, part):
    key = jax.random.fold_in(key, 7)
    key_len, key_pick = jax.random.split(key)
    lengths = jax.random.randint(key_len, (IMAGES,), 1, PATCH + 1)
    groups = IMAGES // IMG_DEV
    chosen = jax.random.randint(key_pick, (groups, 1), 0, IMG_DEV)
    full_spot = jnp.arange(IMG_DEV)[None, :] == chosen
    return jnp.where(full_spot, PATCH, lengths.reshape(groups, IMG_DEV)).reshape(IMAGES).astype(jnp.int32)


def raised(values, key, source, target, parts, factor):
    owner, partner = [(jnp.arange(values.shape[dim]) // (values.shape[dim] // parts)).reshape([-1 if axis == dim else 1 for axis in range(values.ndim)]) for dim in (source, target)]
    chosen = jax.random.permutation(key, parts)[partner]
    strong = (owner == chosen) | (owner == (partner + parts // 2) % parts)
    return jnp.where(strong, factor * values, values)


def level_of(rng, shape, shards, least, top_value):
    factor_of = 1.0
    for dim, parts in shards:
        draws = jax.random.uniform(jax.random.fold_in(jax.random.fold_in(rng, 6), dim), (parts,), jnp.float32, least / len(shards), top_value / len(shards))
        factor_of = factor_of * jnp.repeat(jnp.exp(draws), shape[dim] // parts).reshape((-1,) + (1,) * (len(shape) - 1 - dim))
    return factor_of


def centred(rng, shape, scale, bound, pieces=(), kind=jnp.bfloat16):
    level = level_of(rng, shape, pieces, -0.22, 0.18) if pieces else 1.0
    values = jax.random.normal(rng, shape, jnp.float32) * scale * level
    return jnp.minimum(jnp.maximum(values, -bound), bound).astype(kind)


def heavy_noise(own_key, shape, width, limit, shards, heavy, held_as=jnp.bfloat16):
    values = width * jax.random.normal(own_key, shape, jnp.float32)
    if shards:
        values = values * level_of(own_key, shape, shards, -0.22, 0.18)
    return jnp.clip(raised(values, jax.random.fold_in(own_key, 3), *heavy), -limit, limit).astype(held_as)


def setup_inputs(seed: int = 0) -> dict:
    streams_of = jax.random.split(jax.random.key(seed), 13)
    latents = centred(streams_of[0], (IMAGES, LAT, D), 1.0, 6.0, ((0, 4), (1, 8)))
    media = heavy_noise(streams_of[1], (IMAGES, PATCH, D), 1.0, 6.0, ((0, 4), (1, 8)), (0, 2, 4, 2.0))
    media_lengths = draw_media_lengths(jax.random.fold_in(streams_of[12], 71), 0)
    cotangent = heavy_noise(streams_of[3], (IMAGES, LAT, D), 1.0, 6.0, ((0, 4), (1, 8)), (0, 2, 4, 2.0))
    query_weight = centred(streams_of[4], (D, D), D ** -0.5, 0.15625, ((0, 32),))
    kv_weight = centred(streams_of[5], (D, 2 * D), D ** -0.5, 0.15625, ((0, 32),))
    out_weight = centred(streams_of[6], (D, D), (D // 64) ** -0.5, 1.25, ((0, 32),))
    in_weight = centred(streams_of[7], (D, FF), D ** -0.5, 0.15625, ((0, 32),))
    down_weight = centred(streams_of[8], (D, FF), FF ** -0.5, 0.078125, ((0, 32),))
    media_gain = jnp.clip(1.0 + 0.1 * jax.random.normal(streams_of[9], (D,), jnp.float32), 0.5, 1.5).astype(jnp.bfloat16)
    latent_gain = jnp.clip(1.0 + 0.1 * jax.random.normal(streams_of[10], (D,), jnp.float32), 0.5, 1.5).astype(jnp.bfloat16)
    ffn_gain = jnp.clip(1.0 + 0.1 * jax.random.normal(streams_of[11], (D,), jnp.float32), 0.5, 1.5).astype(jnp.bfloat16)
    return {"latents": latents, "media": media, "media_lengths": media_lengths, "cotangent": cotangent, "query_weight": query_weight, "kv_weight": kv_weight, "out_weight": out_weight, "in_weight": in_weight, "down_weight": down_weight, "media_gain": media_gain, "latent_gain": latent_gain, "ffn_gain": ffn_gain}


NORM_EPS = 1e-05
MASKED = -1e+30

@jax.custom_vjp
def low(v):
    return lax.optimization_barrier(v.astype(jnp.bfloat16)).astype(jnp.float32)

@jax.custom_vjp
def low_back(v):
    return v

def low_keep(v):
    return (low(v), None)

def low_pass(kept, grad):
    return (grad,)

def back_keep(v):
    return (v, None)

def back_low(kept, grad):
    return (low(grad),)
low.defvjp(low_keep, low_pass)
low_back.defvjp(back_keep, back_low)

def product(form, left, right):
    return jnp.einsum(form, left, right, precision=lax.Precision.HIGHEST)

def normalize(values):
    center = values - lax.optimization_barrier(jnp.mean(values, -1, keepdims=True))
    return center * lax.rsqrt(lax.optimization_barrier(jnp.mean(center * center, -1, keepdims=True)) + NORM_EPS)

def reference(latents, media, media_lengths, cotangent, query_weight, kv_weight, out_weight, in_weight, down_weight, media_gain, latent_gain, ffn_gain):
    block_images = IMG_DEV // 2
    block_count = IMAGES // block_images
    head_size = D // HEADS
    score_scale = 1.0 / math.sqrt(head_size)
    length_blocks = media_lengths.reshape(block_count, block_images)

    def blocks(array):
        return array.astype(jnp.float32).reshape((block_count, block_images) + array.shape[1:])

    def forward(lat_all, med_all, w_query, w_kv, w_out, w_in, w_down, g_media, g_latent, g_ffn):

        def one_block(inputs):
            lat_block, med_block, lengths = inputs
            media_in = low(normalize(med_block) * g_media)
            latent_in = low(normalize(lat_block) * g_latent)
            queries = low_back(low(product('bld,de->ble', latent_in, w_query)))
            kv_in = jnp.concatenate([media_in, latent_in], 1)
            kv_proj = product('brd,de->bre', kv_in, w_kv)
            keys = low_back(low(kv_proj[..., :D]))
            values = low_back(low(kv_proj[..., D:]))
            query_heads = queries.reshape(block_images, LAT, HEADS, head_size)
            key_heads = keys.reshape(block_images, PATCH + LAT, HEADS, head_size)
            value_heads = values.reshape(block_images, PATCH + LAT, HEADS, head_size)
            scores = low_back(product('blhe,brhe->bhlr', query_heads, key_heads) * score_scale)
            position = jnp.arange(PATCH + LAT, dtype=jnp.int32)
            allowed = (position[None, :] >= PATCH) | (position[None, :] < lengths[:, None])
            scores = jnp.where(allowed[:, None, None, :], scores, MASKED)
            top_score = lax.optimization_barrier(jnp.max(scores, -1, keepdims=True))
            weights = jnp.exp(scores - top_score)
            attended = product('bhlr,brhe->bhle', low(weights), value_heads) / lax.optimization_barrier(jnp.sum(weights, -1, keepdims=True))
            attn_rows = low_back(low(attended.transpose(0, 2, 1, 3).reshape(block_images, LAT, D)))
            mixed = lat_block + low_back(product('ble,ed->bld', attn_rows, w_out))
            ffn_input = low(normalize(mixed) * g_ffn)
            pre_act = low_back(product('bld,df->blf', ffn_input, w_in))
            hidden = low(jax.nn.gelu(pre_act, approximate=False))
            return mixed + low_back(product('blf,df->bld', hidden, w_down))
        return lax.map(jax.checkpoint(one_block), (lat_all, med_all, length_blocks))
    primal = (blocks(latents), blocks(media), query_weight.astype(jnp.float32), kv_weight.astype(jnp.float32), out_weight.astype(jnp.float32), in_weight.astype(jnp.float32), down_weight.astype(jnp.float32), media_gain.astype(jnp.float32), latent_gain.astype(jnp.float32), ffn_gain.astype(jnp.float32))
    result, pull = jax.vjp(forward, *primal)
    grads = pull(blocks(cotangent))
    return (result.reshape(IMAGES, LAT, D).astype(jnp.bfloat16), grads[0].reshape(IMAGES, LAT, D), grads[1].reshape(IMAGES, PATCH, D), grads[2], grads[3], grads[4], grads[5], grads[6], grads[7], grads[8], grads[9])
```

```python
from functools import partial
import math

import jax
import jax.numpy as jnp
from jax import lax
from jax.experimental import pallas as pl
from jax.experimental.pallas import tpu as pltpu
from jax.sharding import PartitionSpec as P

HEADS = 16
NORM_EPS = 1e-05
MASKED = -1e30
GAUSS_DENSITY = 0.3989422804014327
BF = jnp.bfloat16
F32 = jnp.float32
MIB = 1 << 20


def swap(array, bit, axis="blk"):
    return lax.ppermute(array, axis, [(i, i ^ bit) for i in range(lax.axis_size(axis))])


def gather_slots(block):
    count = lax.axis_size("blk")
    half = block.shape[0] // 2
    slots = {0: block}
    for offset in range(2, count, 2):
        low = offset & -offset
        high = 1 << (offset.bit_length() - 1)
        if low == high:
            slots[offset] = swap(block, offset)
    for offset in range(2, count, 2):
        low = offset & -offset
        high = 1 << (offset.bit_length() - 1)
        if low != high:
            slots[offset] = jnp.concatenate(
                [swap(slots[offset ^ low][:half], low), swap(slots[offset ^ high][half:], high)], 0
            )
    for offset in range(0, count, 2):
        slots[offset + 1] = swap(slots[offset], 1)
    return [slots[k] for k in range(count)]


def scatter_sum(even, odd):
    total = even.astype(F32) + swap(odd, 1).astype(F32)
    pairs, rows, width = total.shape
    bits = pairs.bit_length() - 1
    half = rows // 2
    shaped = total.reshape((2,) * bits + (rows, width))
    first, second = shaped[..., :half, :], shaped[..., half:, :]
    for step in range(bits):
        send = first[..., 1, :, :]
        got = swap(send.astype(BF), 2 << step)
        keep = first[..., 0, :, :]
        send_b = second[1]
        got_b = swap(send_b.astype(BF), 2 << (bits - 1 - step))
        keep_b = second[0]
        if step == bits - 1:
            return (keep, got), (keep_b, got_b)
        first = keep + got.astype(F32)
        second = keep_b + got_b.astype(F32)


def joined(halves):
    return jnp.concatenate([keep + got.astype(F32) for keep, got in halves], 0)


def normalize(values):
    center = values - jnp.mean(values, -1, keepdims=True)
    inverse = lax.rsqrt(jnp.mean(center * center, -1, keepdims=True) + NORM_EPS)
    return (center * inverse, inverse)


def norm_back(grad_norm, normed, inverse):
    return inverse * (
        grad_norm
        - jnp.mean(grad_norm, -1, keepdims=True)
        - normed * jnp.mean(grad_norm * normed, -1, keepdims=True)
    )


def dot(left, right, dims=((1,), (0,))):
    return lax.dot_general(left, right, (dims, ((), ())), preferred_element_type=F32)


NT = ((1,), (1,))
TN = ((0,), (0,))


def call(kernel, out_shapes, smem=0, vmem=48):
    def run(*operands):
        specs = [
            pl.BlockSpec(memory_space=pltpu.SMEM if i < smem else pltpu.VMEM)
            for i in range(len(operands))
        ]
        outs = [jax.ShapeDtypeStruct(shape, kind) for shape, kind in out_shapes]
        return pl.pallas_call(
            kernel,
            out_shape=outs,
            in_specs=specs,
            out_specs=[pl.BlockSpec(memory_space=pltpu.VMEM)] * len(outs),
            compiler_params=pltpu.CompilerParams(vmem_limit_bytes=vmem * MIB),
        )(*operands)

    return run


def project_kernel(count, *refs):
    media, lats = refs[:count], refs[count : 2 * count]
    w_media, w_lat, kv_out, lat_out = refs[2 * count :]
    rows, lat_rows = media[0].shape[0], lats[0].shape[0]
    for k in range(count):
        kv_out[k * rows : (k + 1) * rows, :] = dot(media[k][...], w_media[...]).astype(BF)
    for k in range(count):
        lat_out[k * lat_rows : (k + 1) * lat_rows, :] = dot(lats[k][...], w_lat[...])


def head_masks(rows, width, heads, size):
    lane = lax.broadcasted_iota(jnp.int32, (rows, width), 1)
    return [(lane >= h * size) & (lane < (h + 1) * size) for h in range(heads)]


def stacked(values, masks):
    return jnp.concatenate([jnp.where(m, values, jnp.zeros_like(values)) for m in masks], 0)


def unstacked(values, masks):
    rows = values.shape[0] // len(masks)
    total = jnp.zeros((rows, values.shape[1]), F32)
    for h, m in enumerate(masks):
        total = jnp.where(m, values[h * rows : (h + 1) * rows], total)
    return total


def media_allowed(me, length, count, media_rows, rows):
    column = lax.broadcasted_iota(jnp.int32, (rows, count * media_rows), 1)
    slot = column // media_rows
    index = (slot ^ me) * media_rows + column % media_rows
    return index < length


def attend_kernel(
    count, heads, size, me_ref, len_ref, kv_ref, lat_ref, wo_ref, att_ref, lse_ref, even_ref, odd_ref
):
    images, pad = kv_ref.shape[1], wo_ref.shape[0]
    media_rows = kv_ref.shape[2]
    lat_rows = lat_ref.shape[2]
    rows = count * lat_rows
    scale = 1.0 / math.sqrt(size)
    masks = head_masks(rows, pad, heads, size)
    me = me_ref[0]
    for i in range(images):
        keys = kv_ref[:, i, :, :pad].reshape(count * media_rows, pad)
        values = kv_ref[:, i, :, pad:].reshape(count * media_rows, pad)
        lat = lat_ref[:, i].reshape(rows, 3 * pad).astype(BF)
        lat_keys, lat_values = lat[:, :pad], lat[:, pad : 2 * pad]
        queries = stacked(lat[:, 2 * pad :], masks)
        allowed = media_allowed(me, len_ref[i], count, media_rows, heads * rows)
        scores = jnp.where(allowed, dot(queries, keys, NT) * scale, MASKED)
        lat_scores = dot(queries, lat_keys, NT) * scale
        top = jnp.maximum(
            jnp.max(scores, -1, keepdims=True), jnp.max(lat_scores, -1, keepdims=True)
        )
        probs = jnp.where(allowed, jnp.exp(scores - top), 0.0)
        lat_probs = jnp.exp(lat_scores - top)
        denominator = jnp.sum(probs, -1, keepdims=True) + jnp.sum(lat_probs, -1, keepdims=True)
        weighted = dot(probs.astype(BF), values) + dot(lat_probs.astype(BF), lat_values)
        attended = unstacked(weighted / denominator, masks)
        att_ref[:, i] = attended.reshape(count, lat_rows, pad)
        lse_ref[i] = jnp.broadcast_to(top + jnp.log(denominator), (heads * rows, 128))
    flat = att_ref[...].reshape(count * images * lat_rows, pad).astype(BF)
    part = dot(flat, wo_ref[...]).astype(BF)
    block = images * lat_rows
    for k in range(count):
        out = odd_ref if k % 2 else even_ref
        out[k // 2] = part[k * block : (k + 1) * block]


def attend_back_kernel(
    count,
    heads,
    size,
    me_ref,
    len_ref,
    kv_ref,
    lat_ref,
    wo_ref,
    att_ref,
    lse_ref,
    *refs,
):
    branch = refs[:count]
    dkv_ref, dlat_ref, dlat_wide, datt_wide = refs[count:]
    images, pad = kv_ref.shape[1], wo_ref.shape[0]
    media_rows = kv_ref.shape[2]
    lat_rows = lat_ref.shape[2]
    rows = count * lat_rows
    scale = 1.0 / math.sqrt(size)
    masks = head_masks(rows, pad, heads, size)
    me = me_ref[0]
    for k in range(count):
        part = dot(branch[k][...], wo_ref[...], NT)
        datt_wide[k] = part.reshape(images, lat_rows, pad)
    for i in range(images):
        keys = kv_ref[:, i, :, :pad].reshape(count * media_rows, pad)
        values = kv_ref[:, i, :, pad:].reshape(count * media_rows, pad)
        lat = lat_ref[:, i].reshape(rows, 3 * pad).astype(BF)
        lat_keys, lat_values = lat[:, :pad], lat[:, pad : 2 * pad]
        queries = stacked(lat[:, 2 * pad :], masks)
        grads = datt_wide[:, i].reshape(rows, pad).astype(BF)
        attended = att_ref[:, i].reshape(rows, pad)
        grad_heads = stacked(grads, masks)
        product = stacked(grads.astype(F32) * attended, masks)
        delta = jnp.sum(product, -1, keepdims=True)
        total = lse_ref[i][:, :1]
        allowed = media_allowed(me, len_ref[i], count, media_rows, heads * rows)
        scores = jnp.where(allowed, dot(queries, keys, NT) * scale, MASKED)
        lat_scores = dot(queries, lat_keys, NT) * scale
        probs = jnp.where(allowed, jnp.exp(scores - total), 0.0)
        lat_probs = jnp.exp(lat_scores - total)
        score_grad = (probs * (dot(grad_heads, values, NT) - delta)).astype(BF)
        lat_score_grad = (lat_probs * (dot(grad_heads, lat_values, NT) - delta)).astype(BF)
        query_grad = scale * unstacked(dot(score_grad, keys) + dot(lat_score_grad, lat_keys), masks)
        dkv_ref[:, i, :, :pad] = (
            (scale * dot(score_grad, queries, TN)).astype(BF).reshape(count, media_rows, pad)
        )
        dkv_ref[:, i, :, pad:] = (
            dot(probs.astype(BF), grad_heads, TN).astype(BF).reshape(count, media_rows, pad)
        )
        lat_grad = jnp.concatenate(
            [
                scale * dot(lat_score_grad, queries, TN),
                dot(lat_probs.astype(BF), grad_heads, TN),
                query_grad,
            ],
            1,
        )
        dlat_wide[:, i] = lat_grad.reshape(count, lat_rows, 3 * pad)
    block = images * lat_rows
    dlat_ref[...] = dlat_wide[...].reshape(count * block, 3 * pad).astype(BF)


def input_grad_kernel(count, dkv_ref, dlat_ref, w_media, w_lat, even, odd, even_lat, odd_lat):
    rows = dkv_ref.shape[0] // count
    lat_rows = dlat_ref.shape[0] // count
    for k in range(count):
        out, out_lat = (odd, odd_lat) if k % 2 else (even, even_lat)
        out[k // 2] = dot(dkv_ref[k * rows : (k + 1) * rows, :], w_media[...], NT).astype(BF)
        out_lat[k // 2] = dot(
            dlat_ref[k * lat_rows : (k + 1) * lat_rows, :], w_lat[...], NT
        ).astype(BF)


def erf_parts(values):
    cdf = 0.5 * (1.0 + lax.erf(values * 0.7071067811865476))
    return cdf, cdf + values * jnp.exp(-0.5 * values * values) * GAUSS_DENSITY


def ffn_kernel(count, *refs):
    rows_in, cots = refs[:count], refs[count : 2 * count]
    w_in, w_down, hidden_ref, pre_ref, even, odd = refs[2 * count :]
    rows = rows_in[0].shape[0]
    for k in range(count):
        pre = dot(rows_in[k][...], w_in[...])
        cdf, slope = erf_parts(pre)
        hidden_ref[k * rows : (k + 1) * rows, :] = (pre * cdf).astype(BF)
        back = dot(cots[k][...], w_down[...])
        pre_grad = (back * slope).astype(BF)
        pre_ref[k * rows : (k + 1) * rows, :] = pre_grad
        out = odd if k % 2 else even
        out[k // 2] = dot(pre_grad, w_in[...], NT).astype(BF)


def down_kernel(count, hidden_ref, w_down, even, odd):
    rows = hidden_ref.shape[0] // count
    for k in range(count):
        out = odd if k % 2 else even
        out[k // 2] = dot(hidden_ref[k * rows : (k + 1) * rows, :], w_down[...], NT).astype(BF)


def weight_grad_kernel(count, *refs):
    lefts, right, out = refs[:count], refs[count], refs[count + 1]
    left = jnp.concatenate([r[...] for r in lefts], 0)
    out[...] = dot(left, right[...], TN).astype(out.dtype)


def body(
    latents,
    media,
    media_lengths,
    cotangent,
    query_weight,
    kv_weight,
    out_weight,
    in_weight,
    down_weight,
    media_gain,
    latent_gain,
    ffn_gain,
):
    images, lat_rows, width = latents.shape
    media_rows = media.shape[1]
    nb, nd = lax.axis_size("blk"), lax.axis_size("dp")
    size = width // HEADS
    heads = HEADS // nb
    own = query_weight.shape[0]
    span = heads * size
    pad = -(-span // 128) * 128
    hidden_width = in_weight.shape[1]
    part_hidden = hidden_width // nb
    me = lax.axis_index("blk").astype(jnp.int32).reshape(1)
    ring = size // own
    per_ring = nd // ring
    groups = nb // ring

    def by_owner(weight):
        shaped = weight.reshape(own, ring, per_ring, groups, size)
        return shaped.transpose(3, 1, 0, 2, 4).reshape(nb, own, span)

    def from_owner(slots):
        shaped = slots.reshape(groups, ring, own, per_ring, size)
        return shaped.transpose(2, 1, 3, 0, 4).reshape(own, width)

    g_media, g_lat, g_ffn = (g.astype(F32)[:, None] for g in (media_gain, latent_gain, ffn_gain))
    q_scaled = (query_weight * g_lat).astype(BF)
    in_scaled = (in_weight * g_ffn).astype(BF)
    extra = (-(3 * span + 2)) % 128 + 2
    gain_columns = jnp.concatenate(
        [media_gain[:, None], latent_gain[:, None], jnp.zeros((own, extra - 2), BF)], 1
    )
    attn_parts = jnp.concatenate(
        [
            by_owner(kv_weight[:, :width]),
            by_owner(kv_weight[:, width:]),
            by_owner(q_scaled),
            jnp.broadcast_to(gain_columns, (nb, own, extra)),
        ],
        2,
    )
    ffn_parts = jnp.concatenate(
        [
            in_scaled.reshape(own, nb, part_hidden).transpose(1, 0, 2),
            down_weight.reshape(own, nb, part_hidden).transpose(1, 0, 2),
        ],
        2,
    )

    def columns(parts):
        mine = lax.all_to_all(parts, "blk", 0, 0, tiled=True)
        return lax.all_gather(mine.reshape(nb * own, -1), "dp", axis=0, tiled=True)

    attn_w = columns(attn_parts)
    ffn_w = columns(ffn_parts)
    all_out = lax.all_gather(out_weight, "dp", axis=0, tiled=False)
    ring_groups = [[g * ring + i for i in range(ring)] for g in range(groups)]
    out_w = lax.all_to_all(
        all_out.reshape(ring, per_ring, own, width), "blk", 0, 0, axis_index_groups=ring_groups
    )
    out_w = out_w.transpose(1, 0, 2, 3).reshape(span, width)
    out_w = jnp.pad(out_w, ((0, pad - span), (0, 0)))

    lat_float = latents.astype(F32).reshape(images * lat_rows, width)
    media_float = media.astype(F32).reshape(images * media_rows, width)
    media_norm, media_inverse = normalize(media_float)
    lat_norm, lat_inverse = normalize(lat_float)
    media_slots = gather_slots(media_norm.astype(BF))
    lat_slots = gather_slots(lat_norm.astype(BF))
    cot_flat = cotangent.reshape(images * lat_rows, width)
    cot_slots = gather_slots(cot_flat)

    def padded(block):
        return jnp.pad(block, ((0, 0), (0, pad - span)))

    w_k, w_v = attn_w[:, :span].astype(F32), attn_w[:, span : 2 * span].astype(F32)
    w_q = attn_w[:, 2 * span : 3 * span]
    row_media = attn_w[:, 3 * span : 3 * span + 1].astype(F32)
    row_lat = attn_w[:, 3 * span + 1 : 3 * span + 2].astype(F32)
    w_media = jnp.concatenate(
        [padded((w_k * row_media).astype(BF)), padded((w_v * row_media).astype(BF))], 1
    )
    w_lat = jnp.concatenate(
        [padded((w_k * row_lat).astype(BF)), padded((w_v * row_lat).astype(BF)), padded(w_q)], 1
    )
    all_media, all_lat = nb * images * media_rows, nb * images * lat_rows
    kv, lat_proj = call(
        partial(project_kernel, nb),
        [((all_media, 2 * pad), BF), ((all_lat, 3 * pad), F32)],
    )(*media_slots, *lat_slots, w_media, w_lat)
    kv4 = kv.reshape(nb, images, media_rows, 2 * pad)
    lat4 = lat_proj.reshape(nb, images, lat_rows, 3 * pad)
    half_shape = (nb // 2, images * lat_rows, width)
    attended, totals, even, odd = call(
        partial(attend_kernel, nb, heads, size),
        [
            ((nb, images, lat_rows, pad), F32),
            ((images, heads * nb * lat_rows, 128), F32),
            (half_shape, BF),
            (half_shape, BF),
        ],
        smem=2,
    )(me, media_lengths, kv4, lat4, out_w)
    mixed = lat_float + joined(scatter_sum(even, odd))
    ffn_norm, ffn_inverse = normalize(mixed)
    ffn_slots = gather_slots(ffn_norm.astype(BF))
    w_in, w_down = ffn_w[:, :part_hidden], ffn_w[:, part_hidden:]
    hidden, pre_grad, even, odd = call(
        partial(ffn_kernel, nb),
        [((all_lat, part_hidden), BF), ((all_lat, part_hidden), BF), (half_shape, BF), (half_shape, BF)],
    )(*ffn_slots, *cot_slots, w_in, w_down)
    ffn_back = joined(scatter_sum(even, odd))
    even, odd = call(partial(down_kernel, nb), [(half_shape, BF), (half_shape, BF)])(hidden, w_down)
    resampled = (mixed + joined(scatter_sum(even, odd))).astype(BF).reshape(latents.shape)
    mixed_grad = cot_flat.astype(F32) + norm_back(ffn_back, ffn_norm, ffn_inverse)
    branch_slots = gather_slots(mixed_grad.astype(BF))
    kv_grad, lat_grad = pl.pallas_call(
        partial(attend_back_kernel, nb, heads, size),
        out_shape=[
            jax.ShapeDtypeStruct(kv4.shape, BF),
            jax.ShapeDtypeStruct((all_lat, 3 * pad), BF),
        ],
        in_specs=[pl.BlockSpec(memory_space=pltpu.SMEM)] * 2
        + [pl.BlockSpec(memory_space=pltpu.VMEM)] * (5 + nb),
        out_specs=[pl.BlockSpec(memory_space=pltpu.VMEM)] * 2,
        scratch_shapes=[
            pltpu.VMEM((nb, images, lat_rows, 3 * pad), F32),
            pltpu.VMEM((nb, images, lat_rows, pad), F32),
        ],
        compiler_params=pltpu.CompilerParams(vmem_limit_bytes=48 * MIB),
    )(me, media_lengths, kv4, lat4, out_w, attended, totals, *branch_slots)
    kv_grad = kv_grad.reshape(all_media, 2 * pad)
    media_half = (nb // 2, images * media_rows, width)
    even, odd, even_lat, odd_lat = call(
        partial(input_grad_kernel, nb),
        [(media_half, BF), (media_half, BF), (half_shape, BF), (half_shape, BF)],
    )(kv_grad, lat_grad, w_media, w_lat)
    media_back = joined(scatter_sum(even, odd))
    lat_back = joined(scatter_sum(even_lat, odd_lat))
    media_grad = norm_back(media_back, media_norm, media_inverse).reshape(media.shape)
    latents_grad = (mixed_grad + norm_back(lat_back, lat_norm, lat_inverse)).reshape(latents.shape)

    grad_of = partial(weight_grad_kernel, nb)
    (g_in,) = call(grad_of, [((width, part_hidden), BF)])(*ffn_slots, pre_grad)
    (g_down,) = call(grad_of, [((width, part_hidden), BF)])(*cot_slots, hidden)
    att_flat = attended.reshape(all_lat, pad).astype(BF)
    branch_all = jnp.concatenate(branch_slots, 0)
    g_out = dot(att_flat, branch_all, TN)[:span].astype(BF)
    (g_media_kv,) = call(grad_of, [((width, 2 * pad), F32)])(*media_slots, kv_grad)
    (g_lat_qkv,) = call(grad_of, [((width, 3 * pad), F32)])(*lat_slots, lat_grad)
    gm_k, gm_v = g_media_kv[:, :span], g_media_kv[:, pad : pad + span]
    gl_k, gl_v = g_lat_qkv[:, :span], g_lat_qkv[:, pad : pad + span]
    gl_q = g_lat_qkv[:, 2 * pad : 2 * pad + span]
    gain_media = jnp.sum(gm_k * w_k + gm_v * w_v, 1, keepdims=True)
    gain_lat = jnp.sum(gl_k * w_k + gl_v * w_v, 1, keepdims=True)
    attn_grads = jnp.concatenate(
        [
            gm_k * row_media + gl_k * row_lat,
            gm_v * row_media + gl_v * row_lat,
            gl_q,
            gain_media,
            gain_lat,
            jnp.zeros((width, extra - 2), F32),
        ],
        1,
    ).astype(BF)

    def rows_of(grads):
        summed = lax.psum_scatter(grads, "dp", scatter_dimension=0, tiled=True)
        return lax.all_to_all(summed.reshape(nb, own, -1), "blk", 0, 0, tiled=True)

    in_slots = rows_of(g_in).astype(F32)
    down_slots = rows_of(g_down).astype(F32)
    attn_slots = rows_of(attn_grads).astype(F32)
    out_slots = lax.all_to_all(
        g_out.reshape(per_ring, ring, own, width).transpose(1, 0, 2, 3),
        "blk",
        0,
        0,
        axis_index_groups=ring_groups,
    )
    out_grad = lax.psum_scatter(
        out_slots.reshape(nd * own, width), "dp", scatter_dimension=0, tiled=True
    ).astype(F32)
    in_raw = in_slots.transpose(1, 0, 2).reshape(own, hidden_width)
    down_grad = down_slots.transpose(1, 0, 2).reshape(own, hidden_width)
    kv_out = jnp.concatenate(
        [from_owner(attn_slots[..., :span]), from_owner(attn_slots[..., span : 2 * span])], 1
    )
    q_raw = from_owner(attn_slots[..., 2 * span : 3 * span])
    gains = jnp.sum(attn_slots[..., 3 * span : 3 * span + 2], 0)
    media_gain_grad = gains[:, 0]
    latent_gain_grad = gains[:, 1] + jnp.sum(q_raw * query_weight.astype(F32), 1)
    ffn_gain_grad = jnp.sum(in_raw * in_weight.astype(F32), 1)
    return (
        resampled,
        latents_grad,
        media_grad,
        q_raw * g_lat,
        kv_out,
        out_grad,
        in_raw * g_ffn,
        down_grad,
        media_gain_grad,
        latent_gain_grad,
        ffn_gain_grad,
    )


def solution(mesh):
    rows = P("dp", "blk", None)
    weight = P(("dp", "blk"), None)
    gain = P(("dp", "blk"))
    return jax.shard_map(
        body,
        mesh=mesh,
        in_specs=(rows, rows, P("dp"), rows) + (weight,) * 5 + (gain,) * 3,
        out_specs=(rows,) * 3 + (weight,) * 5 + (gain,) * 3,
        check_vma=False,
    )
```

```python
from functools import partial
import math

import jax
import jax.numpy as jnp
from jax import lax
from jax.experimental import pallas as pl
from jax.experimental.pallas import tpu as pltpu
from jax.sharding import PartitionSpec as P

HEADS = 16
NORM_EPS = 1e-05
MASKED = -1e30
GAUSS_DENSITY = 0.3989422804014327
BF = jnp.bfloat16
F32 = jnp.float32
MIB = 1 << 20
NT = ((1,), (1,))
TN = ((0,), (0,))


def swap(array, bit, axis="blk"):
    return lax.ppermute(array, axis, [(i, i ^ bit) for i in range(lax.axis_size(axis))])


def gather_first(block):
    slots = {0: block}
    for offset in range(2, lax.axis_size("blk"), 2):
        if offset & (offset - 1) == 0:
            slots[offset] = swap(block, offset)
    return slots


def gather_rest(slots, *before):
    count = lax.axis_size("blk")
    half = slots[0].shape[0] // 2
    slots = dict(slots)
    if before:
        slots[2] = after(slots[2], *before)
    for offset in range(2, count, 2):
        low = offset & -offset
        high = 1 << (offset.bit_length() - 1)
        if low != high:
            slots[offset] = jnp.concatenate(
                [swap(slots[offset ^ low][:half], low), swap(slots[offset ^ high][half:], high)], 0
            )
    for offset in range(0, count, 2):
        slots[offset + 1] = swap(slots[offset], 1)
    return [slots[k] for k in range(count)]


def gather_slots(block):
    return gather_rest(gather_first(block))


def fold_kernel(terms, lowest, *refs):
    ins, outs = refs[: 2 * terms], refs[2 * terms : 2 * terms + 4]
    held, made, sems, out_sems = (
        refs[2 * terms + 4 : 4 * terms + 4],
        refs[4 * terms + 4 : 4 * terms + 8],
        refs[-2],
        refs[-1],
    )
    slots = ins[0].shape[0]
    pairs = [(ins[t].at[m], held[t].at[m]) for m in range(slots) for t in range(2 * terms)]
    copies = begin(pairs, sems)
    rows = outs[0].shape[1]
    written = []
    for m in range(slots):
        for t in range(2 * terms):
            copies[2 * terms * m + t].wait()
        for i in range(2):
            if terms == 1:
                left, right, here = held[0], held[1], slice(i * rows, (i + 1) * rows)
            else:
                left, right, here = held[2 * i], held[2 * i + 1], slice(0, rows)
            total = left[m, here, :].astype(F32) + right[m, here, :].astype(F32)
            half = slots // 2
            side, place = (m % 2, m // 2) if lowest[i] else (m // half, m % half)
            made[2 * i + side][place] = total.astype(outs[2 * i + side].dtype)
            copy = pltpu.make_async_copy(
                made[2 * i + side].at[place], outs[2 * i + side].at[place], out_sems.at[len(written)]
            )
            copy.start()
            written.append(copy)
    for copy in written:
        copy.wait()


def fold(*terms):
    flat = [t for pair in terms for t in pair]
    slots, rows, width = flat[0].shape
    if len(terms) == 1:
        rows //= 2
    half = (slots // 2, rows, width)
    scratch = [pltpu.VMEM(t.shape, t.dtype) for t in flat]
    scratch += [pltpu.VMEM(half, kind) for kind in (F32, BF, F32, BF)]
    scratch += [
        pltpu.SemaphoreType.DMA((slots * len(flat),)),
        pltpu.SemaphoreType.DMA((2 * slots,)),
    ]
    return call(
        partial(fold_kernel, len(terms), (True, False)),
        [(half, kind, "h") for kind in (F32, BF, F32, BF)],
        "h" * len(flat),
        scratch,
    )(*flat)


def scatter_sum(even, odd, hooks=()):
    hooks = list(hooks)
    got = swap(odd, 1)
    if hooks:
        got = after(got, *hooks.pop(0)(odd))
    keep_a, send_a, keep_b, send_b = fold((even, got))
    low, high = 2, lax.axis_size("blk") // 2
    while True:
        got_a, got_b = swap(send_a, low), swap(send_b, high)
        if hooks:
            got_a = after(got_a, *hooks.pop(0)(send_a))
        if low * 2 >= lax.axis_size("blk"):
            return keep_a[0], got_a[0], keep_b[0], got_b[0]
        keep_a, send_a, keep_b, send_b = fold((keep_a, got_a), (keep_b, got_b))
        low, high = low * 2, high // 2


def after(array, *others):
    return lax.optimization_barrier((array, *others))[0]


def dot(left, right, dims=((1,), (0,))):
    return lax.dot_general(left, right, (dims, ((), ())), preferred_element_type=F32)


def call(kernel, outs, spaces, scratch=(), vmem=56, cost=2):
    kinds = {"s": pltpu.SMEM, "v": pltpu.VMEM, "h": pl.ANY, "d": pl.ANY}
    fetched = [i for i, letter in enumerate(spaces) if letter == "d"]
    count = len(spaces) + len(outs) + len(scratch)

    def fetching(*refs):
        refs, held = list(refs[:count]), refs[count:]
        copies = begin([(refs[i], held[j]) for j, i in enumerate(fetched)], held[-1])
        for j, i in enumerate(fetched):
            copies[j].wait()
            refs[i] = held[j]
        kernel(*refs)

    def run(*operands):
        held = [pltpu.VMEM(operands[i].shape, operands[i].dtype) for i in fetched]
        if fetched:
            held.append(pltpu.SemaphoreType.DMA((len(fetched),)))
        return pl.pallas_call(
            fetching if fetched else kernel,
            out_shape=[jax.ShapeDtypeStruct(shape, kind) for shape, kind, _ in outs],
            in_specs=[pl.BlockSpec(memory_space=kinds[s]) for s in spaces],
            out_specs=[pl.BlockSpec(memory_space=kinds[s]) for _, _, s in outs],
            scratch_shapes=[*scratch, *held],
            compiler_params=pltpu.CompilerParams(vmem_limit_bytes=vmem * MIB),
            cost_estimate=pl.CostEstimate(
                flops=int(cost * 1.15e9), bytes_accessed=int(cost * 3.6e6), transcendentals=0
            ),
        )(*operands)

    return run


def begin(pairs, sems):
    copies = [pltpu.make_async_copy(s, d, sems.at[i]) for i, (s, d) in enumerate(pairs)]
    for copy in copies:
        copy.start()
    return copies


def normalize(values):
    center = values - jnp.mean(values, -1, keepdims=True)
    inverse = lax.rsqrt(jnp.mean(center * center, -1, keepdims=True) + NORM_EPS)
    return (center * inverse, inverse)


def norm_back(grad_norm, normed, inverse):
    return inverse * (
        grad_norm
        - jnp.mean(grad_norm, -1, keepdims=True)
        - normed * jnp.mean(grad_norm * normed, -1, keepdims=True)
    )


def owned_heads(count, ring, per_ring, b):
    groups = count // ring
    return [((b % ring) * per_ring + j) * groups + b // ring for j in range(per_ring)]


def split_attn_kernel(lay, ring, per_ring, kv, query, gains, out):
    count, own, _ = out.shape
    width = query.shape[1]
    size = lay.size
    scaled = (query[...].astype(F32) * gains[:, 1:2]).astype(BF)
    both = kv[...]
    lane = lax.broadcasted_iota(jnp.int32, (own, lay.width - lay.gain_at), 1)
    tail = jnp.where(lane == 0, gains[:, 0:1], jnp.where(lane == 1, gains[:, 1:2], 0.0))
    tail = tail.astype(BF)
    for b in range(count):
        heads = owned_heads(count, ring, per_ring, b)
        pieces = []
        for source, base in ((both, 0), (both, width), (scaled, 0)):
            pieces += [source[:, base + h * size : base + (h + 1) * size] for h in heads]
            if lay.step > lay.span:
                pieces.append(jnp.zeros((own, lay.step - lay.span), BF))
        out[b] = jnp.concatenate(pieces + [tail], 1)


def split_ffn_kernel(count, w_in, w_down, gains, out):
    part = out.shape[2] // 2
    planes = out.shape[0] // count
    for b in range(count):
        for p in range(2):
            cols = slice((2 * b + p) * part, (2 * b + p + 1) * part)
            scaled = (w_in[:, cols].astype(F32) * gains[:, 2:3]).astype(BF)
            down = w_down[:, cols]
            for d in range(p, planes, 2):
                out[d * count + b, :, :part] = scaled
                out[d * count + b, :, part:] = down


def finish_ffn_kernel(count, of_in, of_down, w_in, gains, in_grad, down_grad, gain_grad):
    planes = of_in.shape[0] // count
    part = of_in.shape[2]
    gain = gains[:, 2:3]
    total = jnp.zeros((w_in.shape[0], 1), F32)
    for b in range(count):
        for p in range(2):
            cols = slice((2 * b + p) * part, (2 * b + p + 1) * part)
            raw = of_in[p * count + b].astype(F32)
            down = of_down[p * count + b].astype(F32)
            for d in range(p + 2, planes, 2):
                raw = raw + of_in[d * count + b].astype(F32)
                down = down + of_down[d * count + b].astype(F32)
            total = total + jnp.sum(raw * w_in[:, cols].astype(F32), 1, keepdims=True)
            in_grad[:, cols] = raw * gain
            down_grad[:, cols] = down
    gain_grad[...] = jnp.broadcast_to(total, gain_grad.shape)


def finish_attn_kernel(lay, ring, per_ring, slots, query, gains, q_grad, kv_grad, gain_grad):
    count, own, _ = slots.shape
    width = query.shape[1]
    size = lay.size
    place = {}
    tail = jnp.zeros((own, lay.width - lay.gain_at), F32)
    for b in range(count):
        block = slots[b].astype(F32)
        for j, h in enumerate(owned_heads(count, ring, per_ring, b)):
            for i, at in enumerate((0, lay.step, lay.q_at)):
                place[i, h] = block[:, at + j * size : at + (j + 1) * size]
        tail = tail + block[:, lay.gain_at :]
    heads = width // size
    kv_grad[:, :width] = jnp.concatenate([place[0, h] for h in range(heads)], 1)
    kv_grad[:, width:] = jnp.concatenate([place[1, h] for h in range(heads)], 1)
    raw = jnp.concatenate([place[2, h] for h in range(heads)], 1)
    q_grad[...] = raw * gains[:, 1:2]
    of_query = jnp.sum(raw * query[...].astype(F32), 1, keepdims=True)
    lane = lax.broadcasted_iota(jnp.int32, gain_grad.shape, 1)
    gain_grad[...] = jnp.where(lane == 0, tail[:, 0:1], tail[:, 1:2] + of_query)


def prepare_kernel(media, lats, out):
    rows = media.shape[0]
    out[:rows, :] = normalize(media[...].astype(F32))[0].astype(BF)
    out[rows:, :] = normalize(lats[...].astype(F32))[0].astype(BF)


class Layout:
    def __init__(self, span, size):
        self.span, self.size = span, size
        pad = -(-span // 128) * 128
        if (2 * span) % 128 == 0:
            self.step, self.v_at = span, span // 128 * 128
        else:
            self.step, self.v_at = pad, pad
        self.block = pad
        self.v_off = self.step - self.v_at
        self.q_at = 2 * self.step
        self.gain_at = self.q_at + span if self.step == span else 3 * pad
        self.width = -(-(self.gain_at + 2) // 128) * 128
        self.heads = span // size

    def keys(self, values):
        return values[..., : self.block]

    def values(self, values):
        return values[..., self.v_at : self.v_at + self.block]

    def queries(self, values):
        return values[..., self.q_at : self.q_at + self.block]

    def pack(self, keys, values):
        shared = self.block - self.v_at
        if not shared:
            return jnp.concatenate([keys, values], 1)
        return jnp.concatenate(
            [keys[:, : self.v_at], keys[:, self.v_at :] + values[:, :shared], values[:, shared:]], 1
        )

    def masks(self, rows, offset):
        lane = lax.broadcasted_iota(jnp.int32, (rows, self.block), 1) - offset
        return [
            (lane >= h * self.size) & (lane < (h + 1) * self.size) for h in range(self.heads)
        ]


def stacked(values, masks):
    return jnp.concatenate([jnp.where(m, values, jnp.zeros_like(values)) for m in masks], 0)


def unstacked(values, masks):
    rows = values.shape[0] // len(masks)
    total = jnp.zeros((rows, values.shape[1]), F32)
    for h, m in enumerate(masks):
        total = jnp.where(m, values[h * rows : (h + 1) * rows], total)
    return total


def media_allowed(me, length, count, media_rows, rows):
    column = lax.broadcasted_iota(jnp.int32, (rows, count * media_rows), 1)
    index = ((column // media_rows) ^ me) * media_rows + column % media_rows
    return index < length


def scale_weights(lay, w, wm, wl):
    row_media = w[:, lay.gain_at : lay.gain_at + 1].astype(F32)
    row_lat = w[:, lay.gain_at + 1 : lay.gain_at + 2].astype(F32)
    base = w[:, : lay.q_at].astype(F32)
    wm[...] = (base * row_media).astype(BF)
    wl[:, : lay.q_at] = (base * row_lat).astype(BF)
    wl[:, lay.q_at :] = w[:, lay.q_at :]


def put_slots(part, count, even, odd):
    rows = part.shape[0] // count
    for k in range(count):
        (odd if k % 2 else even)[k // 2] = part[k * rows : (k + 1) * rows]


def own_rows(lay, ring, me, wo_all, wo):
    at = pl.multiple_of((me % ring) * lay.span, lay.span)
    wo[...] = jnp.zeros(wo.shape, wo.dtype)
    wo[lay.v_off : lay.v_off + lay.span, :] = wo_all[pl.ds(at, lay.span), :]


def forward_kernel(count, lay, ring, me_ref, len_ref, *refs):
    slots = refs[:count]
    w_hbm, wo_hbm, kv_ref, lat_ref, att_ref, lse_ref = refs[count : count + 6]
    even, odd = refs[count + 6 : count + 8]
    xm, xl, w, wm, wl, wo_all, wo, sems = refs[count + 8 :]
    images, media_rows = kv_ref.shape[1:3]
    lat_rows = lat_ref.shape[2]
    rows = count * lat_rows
    block_m, block_l = images * media_rows, images * lat_rows
    pairs = [(w_hbm, w), (wo_hbm, wo_all)]
    for k in range(count):
        pairs.append((slots[k].at[pl.ds(0, block_m)], xm.at[pl.ds(k * block_m, block_m)]))
        pairs.append((slots[k].at[pl.ds(block_m, block_l)], xl.at[pl.ds(k * block_l, block_l)]))
    copies = begin(pairs, sems)
    copies[0].wait()
    scale_weights(lay, w, wm, wl)
    for k in range(count):
        copies[2 + 2 * k].wait()
        proj = dot(xm[k * block_m : (k + 1) * block_m, :], wm[...]).astype(BF)
        kv_ref[k] = proj.reshape(images, media_rows, lay.q_at)
    for k in range(count):
        copies[3 + 2 * k].wait()
    lat_ref[...] = dot(xl[...], wl[...]).reshape(lat_ref.shape)

    scale = 1.0 / math.sqrt(lay.size)
    q_masks, v_masks = lay.masks(rows, 0), lay.masks(rows, lay.v_off)
    me = me_ref[0]
    for i in range(images):
        kv = kv_ref[:, i].reshape(count * media_rows, lay.q_at)
        lat = lat_ref[:, i].reshape(rows, lay.width).astype(BF)
        queries = stacked(lay.queries(lat), q_masks)
        allowed = media_allowed(me, len_ref[i], count, media_rows, lay.heads * rows)
        scores = jnp.where(allowed, dot(queries, lay.keys(kv), NT) * scale, MASKED)
        lat_scores = dot(queries, lay.keys(lat), NT) * scale
        top = jnp.maximum(
            jnp.max(scores, -1, keepdims=True), jnp.max(lat_scores, -1, keepdims=True)
        )
        probs = jnp.where(allowed, jnp.exp(scores - top), 0.0)
        lat_probs = jnp.exp(lat_scores - top)
        denominator = jnp.sum(probs, -1, keepdims=True) + jnp.sum(lat_probs, -1, keepdims=True)
        weighted = dot(probs.astype(BF), lay.values(kv)) + dot(
            lat_probs.astype(BF), lay.values(lat)
        )
        attended = unstacked(weighted / denominator, v_masks)
        att_ref[:, i] = attended.reshape(count, lat_rows, lay.block)
        lse_ref[i] = jnp.broadcast_to(top + jnp.log(denominator), (lay.heads * rows, 128))
    copies[1].wait()
    own_rows(lay, ring, me, wo_all, wo)
    flat = att_ref[...].reshape(count * block_l, lay.block).astype(BF)
    put_slots(dot(flat, wo[...]).astype(BF), count, even, odd)


def backward_kernel(count, lay, ring, me_ref, len_ref, *refs):
    branch = refs[:count]
    kv_hbm, lat_hbm, wo_hbm, att_hbm, lse_hbm, dkv_ref, dlat_ref = refs[count : count + 7]
    br, kv_ref, lat_ref, wo_all, wo, att_ref, lse_ref, dwide, datt, sems = refs[count + 7 :]
    images, media_rows = kv_ref.shape[1:3]
    lat_rows = lat_ref.shape[2]
    rows = count * lat_rows
    block_m, block_l = images * media_rows, images * lat_rows
    pairs = [(branch[k], br.at[pl.ds(k * block_l, block_l)]) for k in range(count)]
    pairs += [
        (wo_hbm, wo_all),
        (lat_hbm, lat_ref),
        (att_hbm, att_ref),
        (lse_hbm, lse_ref),
        (kv_hbm, kv_ref),
    ]
    copies = begin(pairs, sems)
    for k in range(count + 1):
        copies[k].wait()
    own_rows(lay, ring, me_ref[0], wo_all, wo)
    datt[...] = dot(br[...], wo[...], NT).reshape(datt.shape)
    for copy in copies[count + 1 :]:
        copy.wait()

    scale = 1.0 / math.sqrt(lay.size)
    q_masks, v_masks = lay.masks(rows, 0), lay.masks(rows, lay.v_off)
    me = me_ref[0]
    for i in range(images):
        kv = kv_ref[:, i].reshape(count * media_rows, lay.q_at)
        lat = lat_ref[:, i].reshape(rows, lay.width).astype(BF)
        queries = stacked(lay.queries(lat), q_masks)
        grads = datt[:, i].reshape(rows, lay.block).astype(BF)
        attended = att_ref[:, i].reshape(rows, lay.block)
        grad_heads = stacked(grads, v_masks)
        delta = jnp.sum(stacked(grads.astype(F32) * attended, v_masks), -1, keepdims=True)
        total = lse_ref[i][:, :1]
        allowed = media_allowed(me, len_ref[i], count, media_rows, lay.heads * rows)
        scores = jnp.where(allowed, dot(queries, lay.keys(kv), NT) * scale, MASKED)
        lat_scores = dot(queries, lay.keys(lat), NT) * scale
        probs = jnp.where(allowed, jnp.exp(scores - total), 0.0)
        lat_probs = jnp.exp(lat_scores - total)
        score_grad = (probs * (dot(grad_heads, lay.values(kv), NT) - delta)).astype(BF)
        lat_score_grad = (lat_probs * (dot(grad_heads, lay.values(lat), NT) - delta)).astype(BF)
        query_grad = scale * unstacked(
            dot(score_grad, lay.keys(kv)) + dot(lat_score_grad, lay.keys(lat)), q_masks
        )
        dkv_ref[:, i] = (
            lay.pack(scale * dot(score_grad, queries, TN), dot(probs.astype(BF), grad_heads, TN))
            .astype(BF)
            .reshape(count, media_rows, lay.q_at)
        )
        dlat = jnp.concatenate(
            [
                lay.pack(
                    scale * dot(lat_score_grad, queries, TN),
                    dot(lat_probs.astype(BF), grad_heads, TN),
                ),
                query_grad,
            ],
            1,
        )
        dwide[:, i] = jnp.pad(dlat, ((0, 0), (0, lay.width - dlat.shape[1]))).reshape(
            count, lat_rows, lay.width
        )
    dlat_ref[...] = dwide[...].reshape(count * block_l, lay.width).astype(BF)


def input_grad_kernel(count, lay, dkv_ref, dlat_ref, w, even, odd, wm, wl):
    block_l = dlat_ref.shape[0] // count
    block_m = even.shape[1] - block_l
    scale_weights(lay, w, wm, wl)
    lat_back = dot(dlat_ref[...], wl[...], NT).astype(BF)
    for k in range(count):
        out = odd if k % 2 else even
        back = dot(dkv_ref[k].reshape(block_m, lay.q_at), wm[...], NT).astype(BF)
        out[k // 2, :block_m] = back
        out[k // 2, block_m:] = lat_back[k * block_l : (k + 1) * block_l]


def attn_weight_grad_kernel(count, lay, ring, me_ref, *refs):
    slots, branch = refs[:count], refs[count : 2 * count]
    dkv, dlat, w, att, grads, out_keep, out_send, xm, xl, br, out_all, sems = refs[2 * count :]
    images, media_rows = dkv.shape[1:3]
    block_m, block_l = images * media_rows, dlat.shape[0] // count
    pairs = []
    for k in range(count):
        pairs.append((slots[k].at[pl.ds(0, block_m)], xm.at[pl.ds(k * block_m, block_m)]))
        pairs.append((slots[k].at[pl.ds(block_m, block_l)], xl.at[pl.ds(k * block_l, block_l)]))
        pairs.append((branch[k], br.at[pl.ds(k * block_l, block_l)]))
    copies = begin(pairs, sems)
    for copy in copies:
        copy.wait()
    flat = att[...].reshape(count * block_l, lay.block).astype(BF)
    total = dot(flat, br[...], TN)[lay.v_off : lay.v_off + lay.span]
    per_ring, own = out_keep.shape[0], out_keep.shape[1]
    for q in range(per_ring * ring):
        out_all[q] = total[q * own : (q + 1) * own].astype(BF)
    me = me_ref[0]
    for j in range(per_ring):
        for r in range(ring):
            piece = out_all[j * ring + ((me % ring) ^ r)]
            if r:
                out_send[r - 1, j] = piece
            else:
                out_keep[j] = piece
    right = dkv[...].reshape(count * block_m, lay.q_at)
    width = xm.shape[1]
    step = 256 if width % 256 == 0 else 128
    for at in range(0, width, step):
        g_media = dot(xm[:, at : at + step], right, TN)
        g_lat = dot(xl[:, at : at + step], dlat[...], TN)
        block = w[at : at + step, :].astype(F32)
        base = block[:, : lay.q_at]
        row_media = block[:, lay.gain_at : lay.gain_at + 1]
        row_lat = block[:, lay.gain_at + 1 : lay.gain_at + 2]
        gain_media = jnp.sum(g_media * base, 1, keepdims=True)
        gain_lat = jnp.sum(g_lat[:, : lay.q_at] * base, 1, keepdims=True)
        rest = g_lat[:, lay.q_at :]
        lane = lax.broadcasted_iota(jnp.int32, rest.shape, 1) + lay.q_at
        rest = jnp.where(lane == lay.gain_at, gain_media, rest)
        rest = jnp.where(lane == lay.gain_at + 1, gain_lat, rest)
        grads[at : at + step, : lay.q_at] = (
            g_media * row_media + g_lat[:, : lay.q_at] * row_lat
        ).astype(BF)
        grads[at : at + step, lay.q_at :] = rest.astype(BF)


def mixed_kernel(keep_a, got_a, keep_b, got_b, lats, mixed, normed):
    half = keep_a.shape[0]
    for at, keep, got in ((0, keep_a, got_a), (half, keep_b, got_b)):
        value = keep[...] + got[...].astype(F32) + lats[at : at + half, :].astype(F32)
        mixed[at : at + half, :] = value
        normed[at : at + half, :] = normalize(value)[0].astype(BF)


def erf_parts(values):
    cdf = 0.5 * (1.0 + lax.erf(values * 0.7071067811865476))
    return cdf, cdf + values * jnp.exp(-0.5 * values * values) * GAUSS_DENSITY


def ffn_kernel(count, *refs):
    rows_in, cots = refs[:count], refs[count : 2 * count]
    w_hbm, hidden, pre_grad, even, odd, x, c, w, sems = refs[2 * count :]
    rows = rows_in[0].shape[0]
    part = w.shape[1] // 2
    pairs = [(w_hbm, w)]
    pairs += [(rows_in[k], x.at[pl.ds(k * rows, rows)]) for k in range(count)]
    pairs += [(cots[k], c.at[pl.ds(k * rows, rows)]) for k in range(count)]
    copies = begin(pairs, sems)
    copies[0].wait()
    step = 2
    for k in range(0, count, step):
        here = slice(k * rows, (k + step) * rows)
        for copy in copies[1 + k : 1 + k + step]:
            copy.wait()
        pre = dot(x[here, :], w[:, :part])
        cdf, slope = erf_parts(pre)
        hidden[here, :] = (pre * cdf).astype(BF)
        for copy in copies[1 + count + k : 1 + count + k + step]:
            copy.wait()
        grad = (dot(c[here, :], w[:, part:]) * slope).astype(BF)
        pre_grad[here, :] = grad
        back = dot(grad, w[:, :part], NT).astype(BF)
        even[k // 2] = back[:rows]
        odd[k // 2] = back[rows:]


def down_kernel(count, hidden, w, even, odd):
    part = hidden.shape[1]
    put_slots(dot(hidden[...], w[:, part:], NT).astype(BF), count, even, odd)


def ffn_weight_grad_kernel(count, *refs):
    rows_in, right = refs[:count], refs[count]
    total, x, sems = refs[count + 1 :]
    rows = rows_in[0].shape[0]
    copies = begin([(r, x.at[pl.ds(k * rows, rows)]) for k, r in enumerate(rows_in)], sems)
    for copy in copies:
        copy.wait()
    width = x.shape[1]
    step = 256 if width % 256 == 0 else 128
    for at in range(0, width, step):
        total[at : at + step, :] = dot(x[:, at : at + step], right[...], TN).astype(BF)


def add_kernel(left, right, out):
    out[...] = (left[...].astype(F32) + right[...].astype(F32)).astype(out.dtype)


def resampled_kernel(keep, got, far, mixed, out):
    total = mixed[...] + keep[...] + got[...].astype(F32) + far[...].astype(F32)
    out[...] = total.astype(out.dtype)


def ffn_back_kernel(keep, got, far, mixed, cot, mixed_grad, branch):
    normed, inverse = normalize(mixed[...])
    back = keep[...] + got[...].astype(F32) + far[...].astype(F32)
    grad = cot[...].astype(F32) + norm_back(back, normed, inverse)
    mixed_grad[...] = grad
    branch[...] = grad.astype(BF)


def final_kernel(keep_a, got_a, keep_b, got_b, media, lats, mixed_grad, media_grad, lat_grad):
    half, rows = keep_a.shape[0], media.shape[0]
    first = keep_a[...] + got_a[...].astype(F32)
    normed, inverse = normalize(media[:half, :].astype(F32))
    media_grad[:half, :] = norm_back(first, normed, inverse)
    second = keep_b[...] + got_b[...].astype(F32)
    normed, inverse = normalize(media[half:, :].astype(F32))
    media_grad[half:, :] = norm_back(second[: rows - half], normed, inverse)
    normed, inverse = normalize(lats[...].astype(F32))
    lat_grad[...] = mixed_grad[...] + norm_back(second[rows - half :], normed, inverse)


def body(
    latents,
    media,
    media_lengths,
    cotangent,
    query_weight,
    kv_weight,
    out_weight,
    in_weight,
    down_weight,
    media_gain,
    latent_gain,
    ffn_gain,
):
    images, lat_rows, width = latents.shape
    media_rows = media.shape[1]
    nb, nd = lax.axis_size("blk"), lax.axis_size("dp")
    size = width // HEADS
    heads = HEADS // nb
    own = query_weight.shape[0]
    plane = nb * own
    span = heads * size
    lay = Layout(span, size)
    hidden_width = in_weight.shape[1]
    part = hidden_width // nb // 2
    me = lax.axis_index("blk").astype(jnp.int32).reshape(1)
    dz = lax.axis_index("dp").astype(jnp.int32).reshape(1)
    ring = size // own
    per_ring = nd // ring
    groups = nb // ring
    block_m, block_l = images * media_rows, images * lat_rows
    block = block_m + block_l
    all_m, all_l = nb * block_m, nb * block_l

    sems = pltpu.SemaphoreType.DMA

    gains = jnp.stack([media_gain, latent_gain, ffn_gain], 1).astype(F32)
    (attn_parts,) = call(
        partial(split_attn_kernel, lay, ring, per_ring), [((nb, own, lay.width), BF, "v")], "vvv"
    )(kv_weight, query_weight, gains)
    quick = ring == 2 and own % 16 == 0
    if quick:
        out_near = [out_weight] + [swap(out_weight, k, "dp") for k in range(1, nd)]
    else:
        ring_groups = [[g * ring + i for i in range(ring)] for g in range(groups)]
        out_w = lax.all_gather(out_weight, "dp", axis=0, tiled=False)
        out_w = lax.all_gather(out_w, "blk", axis=0, tiled=False, axis_index_groups=ring_groups)
        out_w = out_w.transpose(1, 0, 2, 3).reshape(nd * ring * own, width)
        out_near = [out_w]

    cot_flat = cotangent.reshape(block_l, width)
    cot_far = swap(cot_flat, 1, "dp")
    mine = lax.all_to_all(attn_parts, "blk", 0, 0, tiled=True).reshape(plane, -1)
    attn_w = lax.all_gather(after(mine, cot_far, *out_near), "dp", axis=0, tiled=True)

    media_flat = media.reshape(block_m, width)
    lat_flat = latents.reshape(block_l, width)
    (normed,) = call(prepare_kernel, [((block, width), BF, "v")], "dd", cost=3)(
        after(media_flat, attn_parts), lat_flat
    )
    slots_first = gather_first(normed)
    (ffn_parts,) = call(
        partial(split_ffn_kernel, nb), [((nd * nb, own, 2 * part), BF, "v")], "ddv", cost=5
    )(after(in_weight, *slots_first.values()), down_weight, gains)
    slots = gather_rest(slots_first, ffn_parts, *out_near)
    ffn_w = lax.all_to_all(after(ffn_parts, attn_w), ("dp", "blk"), 0, 0, tiled=True)
    ffn_w = ffn_w.reshape(width, 2 * part)

    if quick:
        near = jnp.stack(out_near)
        far = swap(near, 1)
        core = lax.axis_index("blk") % 2
        both = jnp.where(core == 0, jnp.stack([near, far], 1), jnp.stack([far, near], 1))
        out_w = [lax.dynamic_index_in_dim(both, dz[0] ^ k, 0, False) for k in range(nd)]
        out_w = jnp.concatenate(out_w, 0).reshape(nd * ring * own, width)

    def pair(block):
        return jnp.concatenate([block, swap(block, 1, "dp")], 0)

    cot_first = gather_first(after(jnp.concatenate([cot_flat, cot_far], 0), *slots))

    half_l = (nb // 2, block_l, width)
    half_pair = (nb // 2, 2 * block_l, width)
    half_all = (nb // 2, block, width)
    kv, lat_proj, attended, totals, even, odd = call(
        partial(forward_kernel, nb, lay, ring),
        [
            ((nb, images, media_rows, lay.q_at), BF, "v"),
            ((nb, images, lat_rows, lay.width), F32, "v"),
            ((nb, images, lat_rows, lay.block), F32, "v"),
            ((images, heads * nb * lat_rows, 128), F32, "v"),
            (half_l, BF, "v"),
            (half_l, BF, "v"),
        ],
        "ss" + "h" * (nb + 2),
        [
            pltpu.VMEM((all_m, width), BF),
            pltpu.VMEM((all_l, width), BF),
            pltpu.VMEM((width, lay.width), BF),
            pltpu.VMEM((width, lay.q_at), BF),
            pltpu.VMEM((width, lay.width), BF),
            pltpu.VMEM((ring * span, width), BF),
            pltpu.VMEM((lay.block, width), BF),
            sems((2 + 2 * nb,)),
        ],
        cost=14,
    )(me, media_lengths, *slots, attn_w, out_w)
    mixed, ffn_in = call(
        mixed_kernel, [((block_l, width), F32, "v"), ((block_l, width), BF, "v")], "ddddd"
    )(*scatter_sum(even, after(odd, *cot_first.values())), lat_flat)
    cot_slots = gather_rest(cot_first)
    in_slots = gather_slots(pair(ffn_in))
    hidden, pre_grad, even, odd = call(
        partial(ffn_kernel, nb),
        [((2 * all_l, part), BF, "v")] * 2 + [(half_pair, BF, "v")] * 2,
        "h" * (2 * nb + 1),
        [
            pltpu.VMEM((2 * all_l, width), BF),
            pltpu.VMEM((2 * all_l, width), BF),
            pltpu.VMEM((width, 2 * part), BF),
            sems((2 * nb + 1,)),
        ],
        cost=11,
    )(*in_slots, *cot_slots, ffn_w)

    def both_planes(terms):
        keep, got, keep_far, got_far = terms
        (sent,) = call(add_kernel, [(keep_far.shape, BF, "v")], "dd")(keep_far, got_far)
        return keep, got, sent, swap(sent, 1, "dp")

    def ffn_weight_grad(rows, right):
        return call(
            partial(ffn_weight_grad_kernel, nb),
            [((width, part), BF, "v")],
            "h" * nb + "d",
            [pltpu.VMEM((2 * all_l, width), BF), sems((nb,))],
            cost=6,
        )(*rows, right)

    def to_rows(grads):
        return lax.all_to_all(
            grads.reshape(nd * nb, own, part), ("dp", "blk"), 0, 0, tiled=True
        )

    made = {}

    def beside_scatter(sent):
        made["down"] = ffn_weight_grad(cot_slots, after(hidden, sent))
        return made["down"]

    keep, got, sent, far = both_planes(scatter_sum(even, odd, [lambda sent: (), beside_scatter]))
    made["in"] = ffn_weight_grad(in_slots, after(pre_grad, sent))
    even_d, odd_d = call(partial(down_kernel, nb), [(half_pair, BF, "v")] * 2, "dd", cost=5)(
        after(hidden, *made["in"]), ffn_w
    )
    mixed_grad, branch = call(
        ffn_back_kernel, [((block_l, width), F32, "v"), ((block_l, width), BF, "v")], "d" * 5
    )(keep, got, after(far, even_d), mixed, cot_flat)
    down_terms = scatter_sum(even_d, odd_d)
    branch_slots = gather_slots(branch)
    ffn_sums = to_rows(made["in"][0]), to_rows(made["down"][0])

    dkv, dlat = call(
        partial(backward_kernel, nb, lay, ring),
        [(kv.shape, BF, "v"), ((all_l, lay.width), BF, "v")],
        "ss" + "h" * (nb + 5),
        [
            pltpu.VMEM((all_l, width), BF),
            pltpu.VMEM(kv.shape, BF),
            pltpu.VMEM(lat_proj.shape, F32),
            pltpu.VMEM((ring * span, width), BF),
            pltpu.VMEM((lay.block, width), BF),
            pltpu.VMEM(attended.shape, F32),
            pltpu.VMEM(totals.shape, F32),
            pltpu.VMEM(lat_proj.shape, F32),
            pltpu.VMEM(attended.shape, F32),
            sems((nb + 5,)),
        ],
        cost=9,
    )(me, media_lengths, *branch_slots, kv, lat_proj, out_w, attended, totals)

    attn_grads, out_keep, out_send = call(
        partial(attn_weight_grad_kernel, nb, lay, ring),
        [
            ((width, lay.width), BF, "v"),
            ((per_ring, own, width), BF, "v"),
            ((ring - 1, per_ring, own, width), BF, "v"),
        ],
        "s" + "h" * (2 * nb) + "dddd",
        [
            pltpu.VMEM((all_m, width), BF),
            pltpu.VMEM((all_l, width), BF),
            pltpu.VMEM((all_l, width), BF),
            pltpu.VMEM((per_ring * ring, own, width), BF),
            sems((3 * nb,)),
        ],
        cost=13,
    )(me, *slots, *branch_slots, dkv, dlat, attn_w, attended)

    keep, got, _, far = both_planes(down_terms)
    (resampled,) = call(resampled_kernel, [((block_l, width), BF, "v")], "dddd")(
        keep, got, far, mixed
    )
    attn_sum = lax.psum_scatter(attn_grads, "dp", scatter_dimension=0, tiled=True)

    even, odd = call(
        partial(input_grad_kernel, nb, lay),
        [(half_all, BF, "v"), (half_all, BF, "v")],
        "ddd",
        [pltpu.VMEM((width, lay.q_at), BF), pltpu.VMEM((width, lay.width), BF)],
        cost=10,
    )(after(dkv, attn_grads), dlat, attn_w)

    media_grad, latents_grad = call(
        final_kernel, [((block_m, width), F32, "v"), ((block_l, width), F32, "v")], "d" * 7, cost=5
    )(
        *scatter_sum(even, odd, [lambda sent: (), lambda sent: (attn_sum,)]),
        media_flat,
        lat_flat,
        mixed_grad,
    )

    in_grad, down_grad, ffn_gain_grad = call(
        partial(finish_ffn_kernel, nb),
        [((own, hidden_width), F32, "v")] * 2 + [((own, 128), F32, "v")],
        "dddv",
        cost=4,
    )(*ffn_sums, in_weight, gains)

    attn_slots = lax.all_to_all(attn_sum.reshape(nb, own, -1), "blk", 0, 0, tiled=True)
    query_grad, kv_grad, gain_grads = call(
        partial(finish_attn_kernel, lay, ring, per_ring),
        [((own, width), F32, "v"), ((own, 2 * width), F32, "v"), ((own, 128), F32, "v")],
        "ddv",
    )(attn_slots, query_weight, gains)

    out_send = after(out_send, attn_sum)
    pieces = [out_keep] + [swap(out_send[r - 1], r) for r in range(1, ring)]
    pieces = jnp.stack(pieces)
    rank = lax.axis_index("blk") % ring
    pieces = [lax.dynamic_index_in_dim(pieces, rank ^ r, 0, False) for r in range(ring)]
    out_rows = jnp.concatenate(pieces, 0).reshape(nd * own, width)
    out_grad = lax.psum_scatter(out_rows, "dp", scatter_dimension=0, tiled=True).astype(F32)
    return (
        resampled.reshape(latents.shape),
        latents_grad.reshape(latents.shape),
        media_grad.reshape(media.shape),
        query_grad,
        kv_grad,
        out_grad,
        in_grad,
        down_grad,
        gain_grads[:, 0],
        gain_grads[:, 1],
        ffn_gain_grad[:, 0],
    )


def solution(mesh):
    rows = P("dp", "blk", None)
    weight = P(("dp", "blk"), None)
    gain = P(("dp", "blk"))
    return jax.shard_map(
        body,
        mesh=mesh,
        in_specs=(rows, rows, P("dp"), rows) + (weight,) * 5 + (gain,) * 3,
        out_specs=(rows,) * 3 + (weight,) * 5 + (gain,) * 3,
        check_vma=False,
    )
```

```python
from functools import partial
import math

import jax
import jax.numpy as jnp
from jax import lax
from jax.experimental import pallas as pl
from jax.experimental.pallas import tpu as pltpu
from jax.sharding import PartitionSpec as P

HEADS = 16
NORM_EPS = 1e-05
MASKED = -1e30
GAUSS_DENSITY = 0.3989422804014327
BF = jnp.bfloat16
F32 = jnp.float32
MIB = 1 << 20
VMEM_MIB = 63
NT = ((1,), (1,))
TN = ((0,), (0,))


def chip_bits():
    return lax.axis_size("blk").bit_length() - 2


def hop_bit(j, core):
    return 2 << ((j + core) % chip_bits())


def hop(array, j):
    return lax.ppermute(
        array, "blk", [(i, i ^ hop_bit(j, i % 2)) for i in range(lax.axis_size("blk"))]
    )


def swap(array, bit, axis="blk"):
    return lax.ppermute(array, axis, [(i, i ^ bit) for i in range(lax.axis_size(axis))])


def gather_kind(block):
    blocks = [block]
    for j in range(chip_bits()):
        blocks = blocks + [hop(b, j) for b in blocks]
    return blocks


def gather_all(block):
    blocks = gather_kind(block)
    return blocks + [swap(b, 1) for b in blocks]


def owners(me):
    tables = []
    for core in range(2):
        steps = [hop_bit(j, core) for j in range(chip_bits())]
        tables.append(
            [sum(s for j, s in enumerate(steps) if m >> j & 1) for m in range(1 << len(steps))]
        )
    both = [tables[c] + [1 ^ k for k in tables[1 - c]] for c in range(2)]
    return me ^ jnp.where(me % 2 == 0, jnp.array(both[0]), jnp.array(both[1])).astype(jnp.int32)


def after(array, *others):
    return lax.optimization_barrier((array, *others))[0]


def dot(left, right, dims=((1,), (0,))):
    return lax.dot_general(left, right, (dims, ((), ())), preferred_element_type=F32)


def begin(pairs, sems, first=0):
    copies = [pltpu.make_async_copy(s, d, sems.at[first + i]) for i, (s, d) in enumerate(pairs)]
    for copy in copies:
        copy.start()
    return copies


def call(kernel, outs, spaces, scratch=(), cost=2):
    fetched = [i for i, letter in enumerate(spaces) if letter == "d"]
    stored = [i for i, out in enumerate(outs) if out[2] == "d"]
    first = len(spaces)
    last = first + len(outs)
    sems = pltpu.SemaphoreType.DMA

    def run(*operands):
        held = [pltpu.VMEM(operands[i].shape, operands[i].dtype) for i in fetched]
        made = [pltpu.VMEM(outs[i][0], outs[i][1]) for i in stored]
        def whole(*refs):
            at = last + len(scratch)
            own, extra = list(refs[:at]), list(refs[at:])
            out_sems, in_sems = extra.pop(), extra.pop()
            held_refs, made_refs = extra[: len(fetched)], extra[len(fetched) :]
            copies = begin([(own[i], r) for i, r in zip(fetched, held_refs)], in_sems)
            results = [(r, own[first + i]) for i, r in zip(stored, made_refs)]
            for i, r in zip(fetched, held_refs):
                own[i] = r
            for i, r in zip(stored, made_refs):
                own[first + i] = r
            for copy in copies:
                copy.wait()
            kernel(*own)
            for copy in begin(results, out_sems):
                copy.wait()

        return pl.pallas_call(
            whole,
            out_shape=[jax.ShapeDtypeStruct(shape, kind) for shape, kind, _ in outs],
            in_specs=[
                pl.BlockSpec(memory_space=pltpu.SMEM if s == "s" else pltpu.HBM) for s in spaces
            ],
            out_specs=[pl.BlockSpec(memory_space=pltpu.HBM)] * len(outs),
            scratch_shapes=[
                *scratch,
                *held,
                *made,
                sems((max(1, len(fetched)),)),
                sems((max(1, len(stored)),)),
            ],
            compiler_params=pltpu.CompilerParams(vmem_limit_bytes=VMEM_MIB * MIB),
            cost_estimate=pl.CostEstimate(
                flops=int(cost * 1.15e9), bytes_accessed=int(cost * 3.6e6), transcendentals=0
            ),
        )(*operands)

    return run


def column_steps(width, steps=3):
    step = width // steps if width % (128 * steps) == 0 else width
    return [(at, step) for at in range(0, width, step)]


def kept_and_sent(shape):
    return [(shape, BF, "h")] * 2, [
        pltpu.VMEM(shape, BF),
        pltpu.VMEM(shape, BF),
        pltpu.SemaphoreType.DMA((6,)),
    ]


def put_slots(parts, outs, at, step, values, written):
    kept, sent, sems = parts
    half = kept.shape[0]
    for m, value in enumerate(values):
        (sent if m // half else kept)[m % half, :, at : at + step] = value.astype(BF)
    for source, target in ((kept, outs[0]), (sent, outs[1])):
        cols = pl.ds(at, step)
        copy = pltpu.make_async_copy(
            source.at[:, :, cols], target.at[:, :, cols], sems.at[len(written)]
        )
        copy.start()
        written.append(copy)


def fold_kernel(kept, got, keep, send, left, right, low, high, sems):
    slots = left.shape[0]
    half = slots // 2
    order = [m for i in range(half) for m in (i + half, i)]
    pairs = [(r.at[m], h.at[m]) for m in order for r, h in ((kept, left), (got, right))]
    copies = begin(pairs, sems)
    written = []
    for i, m in enumerate(order):
        copies[2 * i].wait()
        copies[2 * i + 1].wait()
        total = (left[m].astype(F32) + right[m].astype(F32)).astype(BF)
        held, out = (high, send) if m >= half else (low, keep)
        held[m % half] = total
        copy = pltpu.make_async_copy(held.at[m % half], out.at[m % half], sems.at[2 * slots + i])
        copy.start()
        written.append(copy)
    for copy in written:
        copy.wait()


def fold(kept, got):
    slots, rows, width = kept.shape
    half = (slots // 2, rows, width)
    return call(
        fold_kernel,
        [(half, BF, "h")] * 2,
        "hh",
        [
            pltpu.VMEM(kept.shape, BF),
            pltpu.VMEM(kept.shape, BF),
            pltpu.VMEM(half, BF),
            pltpu.VMEM(half, BF),
            pltpu.SemaphoreType.DMA((3 * slots,)),
        ],
        cost=2,
    )(kept, got)


def scatter(parts, hooks=()):
    kept, sent = parts
    hooks = list(hooks)
    for j in reversed(range(chip_bits())):
        got = hop(sent, j)
        if hooks:
            got = after(got, *hooks.pop(0)(sent))
        if j:
            kept, sent = fold(kept, got)
    return kept[0], got[0]


def normalize(values):
    center = values - jnp.mean(values, -1, keepdims=True)
    inverse = lax.rsqrt(jnp.mean(center * center, -1, keepdims=True) + NORM_EPS)
    return (center * inverse, inverse)


def norm_back(grad_norm, normed, inverse):
    return inverse * (
        grad_norm
        - jnp.mean(grad_norm, -1, keepdims=True)
        - normed * jnp.mean(grad_norm * normed, -1, keepdims=True)
    )


class Layout:
    def __init__(self, span, size):
        self.span, self.size = span, size
        pad = -(-span // 128) * 128
        if (2 * span) % 128 == 0:
            self.step, self.v_at = span, span // 128 * 128
        else:
            self.step, self.v_at = pad, pad
        self.block = pad
        self.v_off = self.step - self.v_at
        self.q_at = 2 * self.step
        self.gain_at = self.q_at + span if self.step == span else 3 * pad
        self.width = -(-(self.gain_at + 2) // 128) * 128
        self.heads = span // size

    def keys(self, values):
        return values[..., : self.block]

    def values(self, values):
        return values[..., self.v_at : self.v_at + self.block]

    def queries(self, values):
        return values[..., self.q_at : self.q_at + self.block]

    def pack(self, keys, values):
        shared = self.block - self.v_at
        if not shared:
            return jnp.concatenate([keys, values], 1)
        return jnp.concatenate(
            [keys[:, : self.v_at], keys[:, self.v_at :] + values[:, :shared], values[:, shared:]], 1
        )

    def masks(self, rows, offset):
        lane = lax.broadcasted_iota(jnp.int32, (rows, self.block), 1) - offset
        return [
            (lane >= h * self.size) & (lane < (h + 1) * self.size) for h in range(self.heads)
        ]


def owned_heads(count, ring, per_ring, b):
    groups = count // ring
    return [((b % ring) * per_ring + j) * groups + b // ring for j in range(per_ring)]


def split_attn_kernel(lay, ring, per_ring, kv, query, gains, out):
    count, own, _ = out.shape
    width = query.shape[1]
    size = lay.size
    scaled = (query[...].astype(F32) * gains[:, 1:2]).astype(BF)
    both = kv[...]
    lane = lax.broadcasted_iota(jnp.int32, (own, lay.width - lay.gain_at), 1)
    tail = jnp.where(lane == 0, gains[:, 0:1], jnp.where(lane == 1, gains[:, 1:2], 0.0))
    tail = tail.astype(BF)
    for b in range(count):
        heads = owned_heads(count, ring, per_ring, b)
        pieces = []
        for source, base in ((both, 0), (both, width), (scaled, 0)):
            pieces += [source[:, base + h * size : base + (h + 1) * size] for h in heads]
            if lay.step > lay.span:
                pieces.append(jnp.zeros((own, lay.step - lay.span), BF))
        out[b] = jnp.concatenate(pieces + [tail], 1)


def split_ffn_kernel(w_in, w_down, gains, out):
    count, _, four = out.shape
    part = four // 4
    for b in range(count):
        for p in range(2):
            cols = slice((2 * b + p) * part, (2 * b + p + 1) * part)
            scaled = (w_in[:, cols].astype(F32) * gains[:, 2:3]).astype(BF)
            out[b, :, 2 * p * part : (2 * p + 1) * part] = scaled
            out[b, :, (2 * p + 1) * part : (2 * p + 2) * part] = w_down[:, cols]


def prepare_kernel(media, lats, out):
    rows = media.shape[0]
    out[:rows, :] = normalize(media[...].astype(F32))[0].astype(BF)
    out[rows:, :] = normalize(lats[...].astype(F32))[0].astype(BF)


def stacked(values, masks):
    return jnp.concatenate([jnp.where(m, values, jnp.zeros_like(values)) for m in masks], 0)


def unstacked(values, masks):
    rows = values.shape[0] // len(masks)
    total = jnp.zeros((rows, values.shape[1]), F32)
    for h, m in enumerate(masks):
        total = jnp.where(m, values[h * rows : (h + 1) * rows], total)
    return total


def patch_index(place_ref, count, media_rows, rows):
    column = lax.broadcasted_iota(jnp.int32, (rows, count * media_rows), 1)
    slot, row = column // media_rows, column % media_rows
    index = row
    for k in range(count):
        index = jnp.where(slot == k, place_ref[2 + k] * media_rows + row, index)
    return index


def scaled_columns(lay, w):
    row_media = w[:, lay.gain_at : lay.gain_at + 1].astype(F32)
    row_lat = w[:, lay.gain_at + 1 : lay.gain_at + 2].astype(F32)
    base = w[:, : lay.q_at].astype(F32)
    rest = w[:, lay.q_at :]
    return (base * row_media).astype(BF), jnp.concatenate([(base * row_lat).astype(BF), rest], 1)


def row_copies(slots, block_m, block_l, xm, xl):
    pairs = []
    for k, slot in enumerate(slots):
        pairs.append((slot.at[pl.ds(0, block_m)], xm.at[pl.ds(k * block_m, block_m)]))
        pairs.append((slot.at[pl.ds(block_m, block_l)], xl.at[pl.ds(k * block_l, block_l)]))
    return pairs


def out_copies(me, dz, near, far, held):
    planes, own, _ = near.shape
    core = me % 2
    pairs = []
    for source, which in ((near, core), (far, 1 - core)):
        for k in range(planes):
            at = pl.multiple_of(((dz ^ k) * 2 + which) * own, own)
            pairs.append((source.at[k], held.at[pl.ds(at, own)]))
    return pairs


def rows_of_heads(lay, member, wo_all, wo):
    at = pl.multiple_of(member * lay.span, lay.span)
    wo[...] = jnp.zeros(wo.shape, wo.dtype)
    wo[lay.v_off : lay.v_off + lay.span, :] = wo_all[pl.ds(at, lay.span), :]


def weight_copies(place_ref, weights, held):
    if len(weights) == 1:
        return [(weights[0], held)]
    return out_copies(place_ref[0], place_ref[1], *weights, held)


def forward_kernel(count, lay, place_ref, len_ref, *refs):
    slots, refs = refs[:count], refs[count:]
    w_hbm, kv_out, lat_out, att_out, lse_out, odd_out = refs[:6]
    xm, xl, w, wm, wl, kv_ref, lat_ref, att_ref, lse_ref, odd, sems, out_sems = refs[6:]
    images, media_rows = kv_ref.shape[1:3]
    lat_rows = lat_ref.shape[2]
    rows = count * lat_rows
    block_m, block_l = images * media_rows, images * lat_rows
    copies = begin([(w_hbm, w)] + row_copies(slots, block_m, block_l, xm, xl), sems)
    copies[0].wait()
    wm[...], wl[...] = scaled_columns(lay, w[...])
    step = max(1, count // 4)
    for k in range(0, count, step):
        for i in range(k, k + step):
            copies[1 + 2 * i].wait()
        proj = dot(xm[k * block_m : (k + step) * block_m, :], wm[...]).astype(BF)
        kv_ref[k : k + step] = proj.reshape(step, images, media_rows, lay.q_at)
    for k in range(count):
        copies[2 + 2 * k].wait()
    lat_ref[...] = dot(xl[...], wl[...]).reshape(lat_ref.shape)
    written = begin([(kv_ref, kv_out), (lat_ref, lat_out)], out_sems)

    scale = 1.0 / math.sqrt(lay.size)
    q_masks, v_masks = lay.masks(rows, 0), lay.masks(rows, lay.v_off)
    index = patch_index(place_ref, count, media_rows, lay.heads * rows)
    for i in range(images):
        kv = kv_ref[:, i].reshape(count * media_rows, lay.q_at)
        lat = lat_ref[:, i].reshape(rows, lay.width).astype(BF)
        queries = stacked(lay.queries(lat), q_masks)
        allowed = index < len_ref[i]
        scores = jnp.where(allowed, dot(queries, lay.keys(kv), NT) * scale, MASKED)
        lat_scores = dot(queries, lay.keys(lat), NT) * scale
        top = jnp.maximum(
            jnp.max(scores, -1, keepdims=True), jnp.max(lat_scores, -1, keepdims=True)
        )
        probs = jnp.where(allowed, jnp.exp(scores - top), 0.0)
        lat_probs = jnp.exp(lat_scores - top)
        denominator = jnp.sum(probs, -1, keepdims=True) + jnp.sum(lat_probs, -1, keepdims=True)
        weighted = dot(probs.astype(BF), lay.values(kv)) + dot(
            lat_probs.astype(BF), lay.values(lat)
        )
        attended = unstacked(weighted / denominator, v_masks)
        att_ref[:, i] = attended.reshape(count, lat_rows, lay.block)
        lse_ref[i] = jnp.broadcast_to(top + jnp.log(denominator), (lay.heads * rows, 128))
    half = count // 2
    for k in range(half):
        odd[k] = att_ref[half + k].reshape(block_l, lay.block).astype(BF)
    written += begin([(odd, odd_out), (att_ref, att_out), (lse_ref, lse_out)], out_sems, 2)
    for copy in written:
        copy.wait()


def out_kernel(lay, ring, weights, place_ref, att, got, *refs):
    sources, outs, refs = refs[:weights], refs[weights : weights + 2], refs[weights + 2 :]
    wo_all, wo, wo_far, sems, *parts = refs
    copies = begin(weight_copies(place_ref, sources, wo_all), sems)
    half, rows = got.shape[:2]
    here = [att[m].reshape(rows, lay.block).astype(BF) for m in range(half)]
    here = jnp.concatenate(here, 0)
    there = got[...].reshape(half * rows, lay.block)
    for copy in copies:
        copy.wait()
    member = place_ref[0] % ring
    rows_of_heads(lay, member, wo_all, wo)
    rows_of_heads(lay, member ^ 1, wo_all, wo_far)
    written = []
    for at, step in column_steps(wo.shape[1]):
        cols = slice(at, at + step)
        total = dot(here, wo[:, cols]) + dot(there, wo_far[:, cols])
        values = [total[m * rows : (m + 1) * rows] for m in range(half)]
        put_slots(parts, outs, at, step, values, written)
    for copy in written:
        copy.wait()


def backward_kernel(count, lay, ring, weights, place_ref, len_ref, *refs):
    branch, sources, refs = refs[:count], refs[count : count + weights], refs[count + weights :]
    kv_hbm, lat_hbm, att_hbm, lse_hbm, dkv_ref, dlat_ref, dkv_odd, dlat_odd = refs[:8]
    br, kv_ref, lat_ref, wo_all, wo, att_ref, lse_ref, dwide, datt, sems = refs[8:]
    images, media_rows = kv_ref.shape[1:3]
    lat_rows = lat_ref.shape[2]
    rows = count * lat_rows
    block_m, block_l = images * media_rows, images * lat_rows
    pairs = weight_copies(place_ref, sources, wo_all)
    pairs += [(branch[k], br.at[pl.ds(k * block_l, block_l)]) for k in range(count)]
    ready = len(pairs)
    pairs += [(lat_hbm, lat_ref), (att_hbm, att_ref), (lse_hbm, lse_ref), (kv_hbm, kv_ref)]
    copies = begin(pairs, sems)
    for copy in copies[:ready]:
        copy.wait()
    rows_of_heads(lay, place_ref[0] % ring, wo_all, wo)
    datt[...] = dot(br[...], wo[...], NT).reshape(datt.shape)
    for copy in copies[ready:]:
        copy.wait()

    scale = 1.0 / math.sqrt(lay.size)
    q_masks, v_masks = lay.masks(rows, 0), lay.masks(rows, lay.v_off)
    index = patch_index(place_ref, count, media_rows, lay.heads * rows)
    for i in range(images):
        kv = kv_ref[:, i].reshape(count * media_rows, lay.q_at)
        lat = lat_ref[:, i].reshape(rows, lay.width).astype(BF)
        queries = stacked(lay.queries(lat), q_masks)
        grads = datt[:, i].reshape(rows, lay.block).astype(BF)
        attended = att_ref[:, i].reshape(rows, lay.block)
        grad_heads = stacked(grads, v_masks)
        delta = jnp.sum(stacked(grads.astype(F32) * attended, v_masks), -1, keepdims=True)
        total = lse_ref[i][:, :1]
        allowed = index < len_ref[i]
        scores = jnp.where(allowed, dot(queries, lay.keys(kv), NT) * scale, MASKED)
        lat_scores = dot(queries, lay.keys(lat), NT) * scale
        probs = jnp.where(allowed, jnp.exp(scores - total), 0.0)
        lat_probs = jnp.exp(lat_scores - total)
        score_grad = (probs * (dot(grad_heads, lay.values(kv), NT) - delta)).astype(BF)
        lat_score_grad = (lat_probs * (dot(grad_heads, lay.values(lat), NT) - delta)).astype(BF)
        query_grad = scale * unstacked(
            dot(score_grad, lay.keys(kv)) + dot(lat_score_grad, lay.keys(lat)), q_masks
        )
        dkv_ref[:, i] = (
            lay.pack(scale * dot(score_grad, queries, TN), dot(probs.astype(BF), grad_heads, TN))
            .astype(BF)
            .reshape(count, media_rows, lay.q_at)
        )
        dlat = jnp.concatenate(
            [
                lay.pack(
                    scale * dot(lat_score_grad, queries, TN),
                    dot(lat_probs.astype(BF), grad_heads, TN),
                ),
                query_grad,
            ],
            1,
        )
        dwide[:, i] = jnp.pad(dlat, ((0, 0), (0, lay.width - dlat.shape[1]))).reshape(
            count, lat_rows, lay.width
        )
    dlat_ref[...] = dwide[...].reshape(count * block_l, lay.width).astype(BF)
    half = count // 2
    for k in range(half):
        dkv_odd[k] = dkv_ref[half + k]
        dlat_odd[k] = dlat_ref[(half + k) * block_l : (half + k + 1) * block_l, :]


def input_grad_kernel(lay, *refs):
    ins, outs, refs = refs[:6], refs[6:8], refs[8:]
    dkv, dlat, dkv_got, dlat_got, w, w_far, sems, *parts = refs
    half, block_l = dlat_got.shape[:2]
    block_m = dkv_got.shape[1] * dkv_got.shape[2]
    steps = column_steps(w.shape[0])
    pairs = [
        (ins[3], dlat_got),
        (ins[2], dkv_got),
        (ins[1].at[pl.ds(0, half * block_l)], dlat),
        (ins[0].at[pl.ds(0, half)], dkv),
    ]
    ready = len(pairs)
    for at, step in steps:
        here = pl.ds(at, step)
        pairs += [(ins[4].at[here], w.at[here]), (ins[5].at[here], w_far.at[here])]
    copies = begin(pairs, sems)
    for copy in copies[:ready]:
        copy.wait()
    media_near = dkv[...].reshape(half * block_m, lay.q_at)
    media_far = dkv_got[...].reshape(half * block_m, lay.q_at)
    lat_far = dlat_got[...].reshape(half * block_l, lay.width)
    written = []
    for i, (at, step) in enumerate(steps):
        here = slice(at, at + step)
        copies[ready + 2 * i].wait()
        copies[ready + 2 * i + 1].wait()
        wm, wl = scaled_columns(lay, w[here, :])
        wm_far, wl_far = scaled_columns(lay, w_far[here, :])
        back = dot(media_near, wm, NT) + dot(media_far, wm_far, NT)
        lat = dot(dlat[...], wl, NT) + dot(lat_far, wl_far, NT)
        values = []
        for m in range(half):
            rows = [back[m * block_m : (m + 1) * block_m], lat[m * block_l : (m + 1) * block_l]]
            values.append(jnp.concatenate(rows, 0))
        put_slots(parts, outs, at, step, values, written)
    for copy in written:
        copy.wait()


def attn_weight_grad_kernel(count, lay, ring, place_ref, *refs):
    slots, branch = refs[:count], refs[count : 2 * count]
    dkv, dlat, w, att, grads, out_keep, out_send, xm, xl, br, out_all, sems = refs[2 * count :]
    images, media_rows = dkv.shape[1:3]
    block_m, block_l = images * media_rows, dlat.shape[0] // count
    pairs = [(branch[k], br.at[pl.ds(k * block_l, block_l)]) for k in range(count)]
    pairs += row_copies(slots, block_m, block_l, xm, xl)
    copies = begin(pairs, sems)
    for copy in copies[:count]:
        copy.wait()
    flat = att[...].reshape(count * block_l, lay.block).astype(BF)
    total = dot(flat, br[...], TN)[lay.v_off : lay.v_off + lay.span]
    per_ring, own = out_keep.shape[0], out_keep.shape[1]
    for q in range(per_ring * ring):
        out_all[q] = total[q * own : (q + 1) * own].astype(BF)
    me = place_ref[0]
    for j in range(per_ring):
        for r in range(ring):
            piece = out_all[j * ring + ((me % ring) ^ r)]
            if r:
                out_send[r - 1, j] = piece
            else:
                out_keep[j] = piece
    for copy in copies[count:]:
        copy.wait()
    right = dkv[...].reshape(count * block_m, lay.q_at)
    width = xm.shape[1]
    for at, step in column_steps(width, 2):
        g_media = dot(xm[:, at : at + step], right, TN)
        g_lat = dot(xl[:, at : at + step], dlat[...], TN)
        block = w[at : at + step, :].astype(F32)
        base = block[:, : lay.q_at]
        row_media = block[:, lay.gain_at : lay.gain_at + 1]
        row_lat = block[:, lay.gain_at + 1 : lay.gain_at + 2]
        gain_media = jnp.sum(g_media * base, 1, keepdims=True)
        gain_lat = jnp.sum(g_lat[:, : lay.q_at] * base, 1, keepdims=True)
        rest = g_lat[:, lay.q_at :]
        lane = lax.broadcasted_iota(jnp.int32, rest.shape, 1) + lay.q_at
        rest = jnp.where(lane == lay.gain_at, gain_media, rest)
        rest = jnp.where(lane == lay.gain_at + 1, gain_lat, rest)
        grads[at : at + step, : lay.q_at] = (
            g_media * row_media + g_lat[:, : lay.q_at] * row_lat
        ).astype(BF)
        grads[at : at + step, lay.q_at :] = rest.astype(BF)


def mixed_kernel(keep, got, lats, mixed, normed):
    value = keep[...].astype(F32) + got[...].astype(F32) + lats[...].astype(F32)
    mixed[...] = value
    normed[...] = normalize(value)[0].astype(BF)


def erf_parts(values):
    cdf = 0.5 * (1.0 + lax.erf(values * 0.7071067811865476))
    return cdf, cdf + values * jnp.exp(-0.5 * values * values) * GAUSS_DENSITY


def side_copies(side, weights, held):
    part = held.shape[1] // 2
    if part % 128:
        return [(weights[side], held)]
    cols = pl.ds(side * part, part)
    return [(w.at[:, cols], held.at[:, pl.ds(i * part, part)]) for i, w in enumerate(weights)]


def ffn_kernel(half, *refs):
    rows_in, cots, weights = refs[:half], refs[half : 2 * half], refs[2 * half : 2 * half + 2]
    hidden_out, pre_out, *outs = refs[2 * half + 2 : 2 * half + 6]
    x, c, w_in, w_down, hidden, pre_grad, sems, out_sems, *parts = refs[2 * half + 6 :]
    rows = rows_in[0].shape[0]
    pairs = [(r, x.at[pl.ds(k * rows, rows)]) for k, r in enumerate(rows_in)]
    pairs += side_copies(0, weights, w_in)
    ready = len(pairs)
    pairs += [(r, c.at[pl.ds(k * rows, rows)]) for k, r in enumerate(cots)]
    pairs += side_copies(1, weights, w_down)
    copies = begin(pairs, sems)
    for copy in copies[:ready]:
        copy.wait()
    pre = dot(x[...], w_in[...])
    cdf, slope = erf_parts(pre)
    hidden[...] = (pre * cdf).astype(BF)
    stored = begin([(hidden, hidden_out)], out_sems)
    for copy in copies[ready:]:
        copy.wait()
    pre_grad[...] = (dot(c[...], w_down[...]) * slope).astype(BF)
    stored += begin([(pre_grad, pre_out)], out_sems, 1)
    back_through(pre_grad, w_in, half, outs, parts)
    for copy in stored:
        copy.wait()


def back_through(left, w, half, outs, parts):
    rows = left.shape[0] // half
    written = []
    for at, step in column_steps(w.shape[0]):
        total = dot(left[...], w[at : at + step, :], NT)
        values = [total[m * rows : (m + 1) * rows] for m in range(half)]
        put_slots(parts, outs, at, step, values, written)
    for copy in written:
        copy.wait()


def down_kernel(half, hidden, w, w_far, keep, send, w_down, sems, *parts):
    for copy in begin(side_copies(1, (w, w_far), w_down), sems):
        copy.wait()
    back_through(hidden, w_down, half, (keep, send), parts)


def ffn_weight_grad_kernel(half, *refs):
    rows_in, right, first = refs[:half], refs[half], refs[half + 1 : -4]
    own, far, x, sems = refs[-4:]
    part = right.shape[1] // 2
    rows = rows_in[0].shape[0]
    copies = begin([(r, x.at[pl.ds(k * rows, rows)]) for k, r in enumerate(rows_in)], sems)
    for copy in copies:
        copy.wait()
    for at, step in column_steps(x.shape[1], 2):
        here = slice(at, at + step)
        total = dot(x[:, here], right[...], TN).astype(BF)
        own[here, :part] = total[:, :part]
        far[here, :part] = total[:, part:]
    for out, other in zip((own, far), first):
        out[:, part:] = other[...]


def total_kernel(left, right, out):
    out[...] = (left[...].astype(F32) + right[...].astype(F32)).astype(out.dtype)


def sum_planes_kernel(grads, out):
    planes, _, width = grads.shape
    for p in range(2):
        total = grads[p].astype(F32)
        for d in range(p + 2, planes, 2):
            total = total + grads[d].astype(F32)
        out[:, p * width : (p + 1) * width] = total.astype(BF)


def resampled_kernel(near, far, mixed, out):
    out[...] = (mixed[...] + near[...].astype(F32) + far[...].astype(F32)).astype(out.dtype)


def ffn_back_kernel(near, far, mixed, cot, mixed_grad, branch):
    normed, inverse = normalize(mixed[...])
    back = near[...].astype(F32) + far[...].astype(F32)
    grad = cot[...].astype(F32) + norm_back(back, normed, inverse)
    mixed_grad[...] = grad
    branch[...] = grad.astype(BF)


def final_kernel(keep, got, media, lats, mixed_grad, media_grad, lat_grad):
    rows = media.shape[0]
    back = keep[...].astype(F32) + got[...].astype(F32)
    normed, inverse = normalize(media[...].astype(F32))
    media_grad[...] = norm_back(back[:rows], normed, inverse)
    normed, inverse = normalize(lats[...].astype(F32))
    lat_grad[...] = mixed_grad[...] + norm_back(back[rows:], normed, inverse)


def finish_ffn_kernel(grads, w_in, gains, in_grad, down_grad, gain_grad):
    part = grads.shape[2] // 4
    total = jnp.zeros((w_in.shape[0], 1), F32)
    for b in range(grads.shape[0]):
        for p in range(2):
            cols = slice((2 * b + p) * part, (2 * b + p + 1) * part)
            at = 2 * p * part
            raw = grads[b, :, at : at + part].astype(F32)
            total = total + jnp.sum(raw * w_in[:, cols].astype(F32), 1, keepdims=True)
            in_grad[:, cols] = raw * gains[:, 2:3]
            down_grad[:, cols] = grads[b, :, at + part : at + 2 * part].astype(F32)
    gain_grad[...] = jnp.broadcast_to(total, gain_grad.shape)


def finish_attn_kernel(lay, ring, per_ring, slots, query, gains, q_grad, kv_grad, gain_grad):
    count, own, _ = slots.shape
    width = query.shape[1]
    size = lay.size
    place = {}
    tail = jnp.zeros((own, lay.width - lay.gain_at), F32)
    for b in range(count):
        block = slots[b].astype(F32)
        for j, h in enumerate(owned_heads(count, ring, per_ring, b)):
            for i, at in enumerate((0, lay.step, lay.q_at)):
                place[i, h] = block[:, at + j * size : at + (j + 1) * size]
        tail = tail + block[:, lay.gain_at :]
    heads = width // size
    kv_grad[:, :width] = jnp.concatenate([place[0, h] for h in range(heads)], 1)
    kv_grad[:, width:] = jnp.concatenate([place[1, h] for h in range(heads)], 1)
    raw = jnp.concatenate([place[2, h] for h in range(heads)], 1)
    q_grad[...] = raw * gains[:, 1:2]
    of_query = jnp.sum(raw * query[...].astype(F32), 1, keepdims=True)
    lane = lax.broadcasted_iota(jnp.int32, gain_grad.shape, 1)
    gain_grad[...] = jnp.where(lane == 0, tail[:, 0:1], tail[:, 1:2] + of_query)


def body(
    latents,
    media,
    media_lengths,
    cotangent,
    query_weight,
    kv_weight,
    out_weight,
    in_weight,
    down_weight,
    media_gain,
    latent_gain,
    ffn_gain,
):
    images, lat_rows, width = latents.shape
    media_rows = media.shape[1]
    nb, nd = lax.axis_size("blk"), lax.axis_size("dp")
    half = nb // 2
    size = width // HEADS
    heads = HEADS // nb
    own = query_weight.shape[0]
    plane = nb * own
    span = heads * size
    lay = Layout(span, size)
    hidden_width = in_weight.shape[1]
    part = hidden_width // nb // 2
    me = lax.axis_index("blk").astype(jnp.int32)
    dz = lax.axis_index("dp").astype(jnp.int32)
    place = jnp.concatenate([jnp.stack([me, dz]), owners(me)])
    ring = size // own
    per_ring = nd // ring
    groups = nb // ring
    block_m, block_l = images * media_rows, images * lat_rows
    block = block_m + block_l
    all_m, all_l = nb * block_m, nb * block_l
    sems = pltpu.SemaphoreType.DMA

    gains = jnp.stack([media_gain, latent_gain, ffn_gain], 1).astype(F32)
    (attn_parts,) = call(
        partial(split_attn_kernel, lay, ring, per_ring), [((nb, own, lay.width), BF, "d")], "ddd"
    )(kv_weight, query_weight, gains)

    quick = ring == 2 and own % 16 == 0
    if quick:
        out_near = [out_weight] + [swap(out_weight, k, "dp") for k in range(1, nd)]
    else:
        ring_groups = [[g * ring + i for i in range(ring)] for g in range(groups)]
        out_w = lax.all_gather(out_weight, "dp", axis=0, tiled=False)
        out_w = lax.all_gather(out_w, "blk", axis=0, tiled=False, axis_index_groups=ring_groups)
        out_near = [out_w.transpose(1, 0, 2, 3).reshape(nd * ring * own, width)]

    mine = lax.all_to_all(attn_parts, "blk", 0, 0, tiled=True).reshape(plane, -1)
    attn_w = lax.all_gather(after(mine, *out_near), "dp", axis=0, tiled=True)

    media_flat = media.reshape(block_m, width)
    lat_flat = latents.reshape(block_l, width)
    cot_flat = cotangent.reshape(block_l, width)
    (normed,) = call(prepare_kernel, [((block, width), BF, "d")], "dd", cost=3)(
        after(media_flat, attn_parts), lat_flat
    )
    slots = gather_all(normed)
    cot_pair = jnp.concatenate([cot_flat, swap(cot_flat, 1, "dp")], 0)

    (ffn_parts,) = call(split_ffn_kernel, [((nb, own, 4 * part), BF, "d")], "ddd", cost=4)(
        after(in_weight, normed), down_weight, gains
    )
    ffn_mine = lax.all_to_all(after(ffn_parts, mine), "blk", 0, 0, tiled=True)
    ffn_mine = ffn_mine.reshape(plane, 4 * part)
    by_plane = jnp.stack(
        [ffn_mine[:, d % 2 * 2 * part : (d % 2 + 1) * 2 * part] for d in range(nd)]
    )
    ffn_w = lax.all_to_all(after(by_plane, *slots, attn_w, cot_pair), "dp", 0, 0, tiled=True)
    ffn_w = ffn_w.reshape(width, 2 * part)

    if quick:
        near = jnp.stack(out_near)
        out_w = [near, swap(near, 1)]
    else:
        out_w = out_near

    cot_kind = gather_kind(after(cot_pair, *slots))
    kv_shape = (nb, images, media_rows, lay.q_at)
    lat_shape = (nb, images, lat_rows, lay.width)
    att_shape = (nb, images, lat_rows, lay.block)
    lse_shape = (images, heads * nb * lat_rows, 128)
    odd_shape = (half, block_l, lay.block)
    shapes = [(kv_shape, BF), (lat_shape, F32), (att_shape, F32), (lse_shape, F32), (odd_shape, BF)]
    kv, lat_proj, attended, totals, att_odd = call(
        partial(forward_kernel, nb, lay),
        [(shape, kind, "h") for shape, kind in shapes],
        "ss" + "h" * (nb + 1),
        [
            pltpu.VMEM((all_m, width), BF),
            pltpu.VMEM((all_l, width), BF),
            pltpu.VMEM((width, lay.width), BF),
            pltpu.VMEM((width, lay.q_at), BF),
            pltpu.VMEM((width, lay.width), BF),
        ]
        + [pltpu.VMEM(shape, kind) for shape, kind in shapes]
        + [sems((1 + 2 * nb,)), sems((5,))],
        cost=11,
    )(place, media_lengths, *slots, attn_w)

    def exchange(rows):
        return kept_and_sent((half // 2, rows, width))

    outs, scratch = exchange(block_l)
    parts = call(
        partial(out_kernel, lay, ring, len(out_w)),
        outs,
        "sdd" + "h" * len(out_w),
        [
            pltpu.VMEM((nd * ring * own, width), BF),
            pltpu.VMEM((lay.block, width), BF),
            pltpu.VMEM((lay.block, width), BF),
            sems((2 * nd,)),
            *scratch,
        ],
        cost=3,
    )(place, attended, swap(after(att_odd, *cot_kind[1:3]), 1), *out_w)
    mixed, ffn_in = call(
        mixed_kernel, [((block_l, width), F32, "d"), ((block_l, width), BF, "d")], "ddd"
    )(*scatter(parts, [lambda sent: cot_kind[3:]]), lat_flat)

    mid = block_l // 2
    in_kind = gather_kind(
        jnp.concatenate([ffn_in, swap(ffn_in[:mid], 1, "dp"), swap(ffn_in[mid:], 1, "dp")], 0)
    )
    ffn_far = swap(after(ffn_w, *in_kind[1:3]), 1)
    if part % 128:
        ffn_sides = [
            jnp.concatenate([ffn_w[:, i * part : (i + 1) * part], ffn_far[:, i * part : (i + 1) * part]], 1)
            for i in range(2)
        ]
    else:
        ffn_sides = [ffn_w, ffn_far]
    rows_pair = half * 2 * block_l
    outs, scratch = exchange(2 * block_l)
    hidden, pre_grad, *parts = call(
        partial(ffn_kernel, half),
        [((rows_pair, 2 * part), BF, "h")] * 2 + outs,
        "h" * (2 * half + 2),
        [
            pltpu.VMEM((rows_pair, width), BF),
            pltpu.VMEM((rows_pair, width), BF),
            pltpu.VMEM((width, 2 * part), BF),
            pltpu.VMEM((width, 2 * part), BF),
            pltpu.VMEM((rows_pair, 2 * part), BF),
            pltpu.VMEM((rows_pair, 2 * part), BF),
            sems((2 * half + 4,)),
            sems((2,)),
            *scratch,
        ],
        cost=9,
    )(*in_kind, *cot_kind, *ffn_sides)

    def ffn_weight_grad(rows, right, *first):
        shape = (width, part * (2 if first else 1))
        return call(
            partial(ffn_weight_grad_kernel, half),
            [(shape, BF, "d")] * 2,
            "h" * half + "d" * (1 + len(first)),
            [pltpu.VMEM((rows_pair, width), BF), sems((half,))],
            cost=4,
        )(*rows, right, *first)

    def total(left, right):
        return call(total_kernel, [(left.shape, BF, "d")], "dd", cost=1)(left, right)[0]

    made = {}

    def beside_first(sent):
        made["down"] = ffn_weight_grad(cot_kind, after(hidden, sent))
        return made["down"]

    def beside_second(sent):
        outs, scratch = exchange(2 * block_l)
        made["parts"] = call(
            partial(down_kernel, half),
            outs,
            "dhh",
            [pltpu.VMEM((width, 2 * part), BF), sems((2,)), *scratch],
            cost=4,
        )(after(hidden, sent), *ffn_sides)
        return made["parts"]

    pair_total = total(*scatter(parts, [beside_first, beside_second]))
    grads_own, grads_far = ffn_weight_grad(in_kind, after(pre_grad, pair_total), *made["down"])
    pair_got = swap(pair_total[block_l:], 1, "dp")
    mixed_grad, branch = call(
        ffn_back_kernel, [((block_l, width), F32, "d"), ((block_l, width), BF, "d")], "dddd"
    )(
        pair_total[:block_l],
        after(pair_got, grads_far),
        mixed,
        cot_flat,
    )
    branch_slots = gather_all(branch)
    ffn_grads = total(after(grads_own, branch), swap(grads_far, 1)).reshape(nd, plane, 2 * part)
    ffn_planes = lax.all_to_all(ffn_grads, "dp", 0, 0, tiled=True)

    def keep_second(sent):
        made["second"] = sent
        return ()

    down_terms = scatter(made["parts"], [lambda sent: (), keep_second])

    dkv, dlat, dkv_odd, dlat_odd = call(
        partial(backward_kernel, nb, lay, ring, len(out_w)),
        [
            (kv_shape, BF, "d"),
            ((all_l, lay.width), BF, "d"),
            ((half, *kv_shape[1:]), BF, "d"),
            ((half, block_l, lay.width), BF, "d"),
        ],
        "ss" + "h" * (nb + len(out_w) + 4),
        [
            pltpu.VMEM((all_l, width), BF),
            pltpu.VMEM(kv_shape, BF),
            pltpu.VMEM(lat_shape, F32),
            pltpu.VMEM((nd * ring * own, width), BF),
            pltpu.VMEM((lay.block, width), BF),
            pltpu.VMEM(att_shape, F32),
            pltpu.VMEM(lse_shape, F32),
            pltpu.VMEM(lat_shape, F32),
            pltpu.VMEM(att_shape, F32),
            sems((nb + 2 * nd + 4,)),
        ],
        cost=9,
    )(place, media_lengths, *branch_slots, *out_w, kv, lat_proj, after(attended, ffn_grads), totals)

    attn_grads, out_keep, out_send = call(
        partial(attn_weight_grad_kernel, nb, lay, ring),
        [
            ((width, lay.width), BF, "d"),
            ((per_ring, own, width), BF, "d"),
            ((ring - 1, per_ring, own, width), BF, "d"),
        ],
        "s" + "h" * (2 * nb) + "dddd",
        [
            pltpu.VMEM((all_m, width), BF),
            pltpu.VMEM((all_l, width), BF),
            pltpu.VMEM((all_l, width), BF),
            pltpu.VMEM((per_ring * ring, own, width), BF),
            sems((3 * nb,)),
        ],
        cost=11,
    )(place, *slots, *branch_slots, after(dkv, made["second"]), dlat, attn_w, attended)
    attn_sum = lax.psum_scatter(attn_grads, "dp", scatter_dimension=0, tiled=True)

    outs, scratch = exchange(block)
    parts = call(
        partial(input_grad_kernel, lay),
        outs,
        "hhhhhh",
        [
            pltpu.VMEM((half, *kv_shape[1:]), BF),
            pltpu.VMEM((half * block_l, lay.width), BF),
            pltpu.VMEM((half, *kv_shape[1:]), BF),
            pltpu.VMEM((half, block_l, lay.width), BF),
            pltpu.VMEM((width, lay.width), BF),
            pltpu.VMEM((width, lay.width), BF),
            sems((10,)),
            *scratch,
        ],
        cost=9,
    )(
        after(dkv, attn_grads, *down_terms),
        dlat,
        swap(dkv_odd, 1),
        swap(dlat_odd, 1),
        attn_w,
        swap(attn_w, 1),
    )
    def keep_last(sent):
        made["last"] = sent
        return ()

    media_grad, latents_grad = call(
        final_kernel, [((block_m, width), F32, "d"), ((block_l, width), F32, "d")], "ddddd", cost=5
    )(*scatter(parts, [lambda sent: (), keep_last]), media_flat, lat_flat, mixed_grad)

    down_total = total(*down_terms)
    (resampled,) = call(resampled_kernel, [((block_l, width), BF, "d")], "ddd")(
        down_total[:block_l], swap(down_total[block_l:], 1, "dp"), mixed
    )

    (ffn_rows,) = call(sum_planes_kernel, [((plane, 4 * part), BF, "d")], "d", cost=3)(
        after(ffn_planes, made["last"])
    )
    ffn_slots = lax.all_to_all(ffn_rows.reshape(nb, own, 4 * part), "blk", 0, 0, tiled=True)

    in_grad, down_grad, ffn_gain_grad = call(
        finish_ffn_kernel,
        [((own, hidden_width), F32, "d")] * 2 + [((own, 128), F32, "d")],
        "ddd",
        cost=3,
    )(ffn_slots, in_weight, gains)

    attn_slots = lax.all_to_all(after(attn_sum, made["last"]).reshape(nb, own, -1), "blk", 0, 0, tiled=True)
    query_grad, kv_grad, gain_grads = call(
        partial(finish_attn_kernel, lay, ring, per_ring),
        [((own, width), F32, "d"), ((own, 2 * width), F32, "d"), ((own, 128), F32, "d")],
        "ddd",
    )(attn_slots, query_weight, gains)

    out_send = after(out_send, made["last"])
    pieces = [out_keep] + [swap(out_send[r - 1], r) for r in range(1, ring)]
    pieces = jnp.stack(pieces)
    rank = lax.axis_index("blk") % ring
    pieces = [lax.dynamic_index_in_dim(pieces, rank ^ r, 0, False) for r in range(ring)]
    out_rows = jnp.concatenate(pieces, 0).reshape(nd * own, width)
    out_grad = lax.psum_scatter(out_rows, "dp", scatter_dimension=0, tiled=True).astype(F32)
    return (
        resampled.reshape(latents.shape),
        latents_grad.reshape(latents.shape),
        media_grad.reshape(media.shape),
        query_grad,
        kv_grad,
        out_grad,
        in_grad,
        down_grad,
        gain_grads[:, 0],
        gain_grads[:, 1],
        ffn_gain_grad[:, 0],
    )


def solution(mesh):
    rows = P("dp", "blk", None)
    weight = P(("dp", "blk"), None)
    gain = P(("dp", "blk"))
    return jax.shard_map(
        body,
        mesh=mesh,
        in_specs=(rows, rows, P("dp"), rows) + (weight,) * 5 + (gain,) * 3,
        out_specs=(rows,) * 3 + (weight,) * 5 + (gain,) * 3,
        check_vma=False,
    )
```

```python
from functools import partial
import math

import jax
import jax.numpy as jnp
from jax import lax
from jax.experimental import pallas as pl
from jax.experimental.pallas import tpu as pltpu
from jax.sharding import PartitionSpec as P

HEADS = 16
NORM_EPS = 1e-05
MASKED = -1e30
GAUSS_DENSITY = 0.3989422804014327
BF = jnp.bfloat16
F32 = jnp.float32
MIB = 1 << 20
VMEM_MIB = 63
NT = ((1,), (1,))
TN = ((0,), (0,))


def chip_bits():
    return lax.axis_size("blk").bit_length() - 2


def hop_bit(j, core):
    return 2 << ((j + core) % chip_bits())


def hop(array, j):
    return lax.ppermute(
        array, "blk", [(i, i ^ hop_bit(j, i % 2)) for i in range(lax.axis_size("blk"))]
    )


def swap(array, bit, axis="blk"):
    return lax.ppermute(array, axis, [(i, i ^ bit) for i in range(lax.axis_size(axis))])


def gather_kind(block):
    blocks = [block]
    for j in range(chip_bits()):
        blocks = blocks + [hop(b, j) for b in blocks]
    return blocks


def gather_all(block):
    return with_other(gather_kind(block))


def with_other(blocks):
    return blocks + [swap(b, 1) for b in blocks]


def owners(me):
    tables = []
    for core in range(2):
        steps = [hop_bit(j, core) for j in range(chip_bits())]
        tables.append(
            [sum(s for j, s in enumerate(steps) if m >> j & 1) for m in range(1 << len(steps))]
        )
    both = [tables[c] + [1 ^ k for k in tables[1 - c]] for c in range(2)]
    return me ^ jnp.where(me % 2 == 0, jnp.array(both[0]), jnp.array(both[1])).astype(jnp.int32)


def after(array, *others):
    return lax.optimization_barrier((array, *others))[0]


def dot(left, right, dims=((1,), (0,))):
    return lax.dot_general(left, right, (dims, ((), ())), preferred_element_type=F32)


def padded_bytes(shape, kind):
    item = jnp.dtype(kind).itemsize
    *lead, rows, lanes = (1, *shape) if len(shape) == 1 else shape
    tile = 32 // item
    return math.prod(lead) * (-(-rows // tile) * tile) * (-(-lanes // 128) * 128) * item


def begin(pairs, sems, first=0):
    copies = [pltpu.make_async_copy(s, d, sems.at[first + i]) for i, (s, d) in enumerate(pairs)]
    for copy in copies:
        copy.start()
    return copies


def call(kernel, outs, spaces, scratch=(), cost=2, big=False):
    fetched = [i for i, letter in enumerate(spaces) if letter == "d"]
    stored = [i for i, out in enumerate(outs) if out[2] == "d"]
    first = len(spaces)
    last = first + len(outs)
    sems = pltpu.SemaphoreType.DMA

    def run(*operands):
        held = [pltpu.VMEM(operands[i].shape, operands[i].dtype) for i in fetched]
        made = [pltpu.VMEM(outs[i][0], outs[i][1]) for i in stored]
        size = sum(
            padded_bytes(b.shape, b.dtype)
            for b in (*scratch, *held, *made)
            if b.memory_space == pltpu.VMEM
        )

        def whole(*refs):
            at = last + len(scratch)
            own, extra = list(refs[:at]), list(refs[at:])
            out_sems, in_sems = extra.pop(), extra.pop()
            held_refs, made_refs = extra[: len(fetched)], extra[len(fetched) :]
            copies = begin([(own[i], r) for i, r in zip(fetched, held_refs)], in_sems)
            results = [(r, own[first + i]) for i, r in zip(stored, made_refs)]
            for i, r in zip(fetched, held_refs):
                own[i] = r
            for i, r in zip(stored, made_refs):
                own[first + i] = r
            for copy in copies:
                copy.wait()
            kernel(*own)
            for copy in begin(results, out_sems):
                copy.wait()

        return pl.pallas_call(
            whole,
            out_shape=[jax.ShapeDtypeStruct(shape, kind) for shape, kind, _ in outs],
            in_specs=[
                pl.BlockSpec(memory_space=pltpu.SMEM if s == "s" else pltpu.HBM) for s in spaces
            ],
            out_specs=[pl.BlockSpec(memory_space=pltpu.HBM)] * len(outs),
            scratch_shapes=[
                *scratch,
                *held,
                *made,
                sems((max(1, len(fetched)),)),
                sems((max(1, len(stored)),)),
            ],
            compiler_params=pltpu.CompilerParams(vmem_limit_bytes=VMEM_MIB * MIB if big else size + 6 * MIB),
            cost_estimate=pl.CostEstimate(
                flops=int(cost * 1.15e9), bytes_accessed=int(cost * 3.6e6), transcendentals=0
            ),
        )(*operands)

    return run


def column_steps(width, steps=3):
    step = width // steps if width % (128 * steps) == 0 else width
    return [(at, step) for at in range(0, width, step)]


def kept_and_sent(shape):
    return [(shape, BF, "h")] * 2, [
        pltpu.VMEM(shape, BF),
        pltpu.VMEM(shape, BF),
        pltpu.SemaphoreType.DMA((6,)),
    ]


def put_slots(parts, outs, at, step, values, written):
    kept, sent, sems = parts
    half = kept.shape[0]
    for m, value in enumerate(values):
        (sent if m // half else kept)[m % half, :, at : at + step] = value.astype(BF)
    for source, target in ((kept, outs[0]), (sent, outs[1])):
        cols = pl.ds(at, step)
        copy = pltpu.make_async_copy(
            source.at[:, :, cols], target.at[:, :, cols], sems.at[len(written)]
        )
        copy.start()
        written.append(copy)


def fold_kernel(kept, got, keep, send, left, right, low, high, sems):
    slots = left.shape[0]
    half = slots // 2
    order = [m for i in range(half) for m in (i + half, i)]
    pairs = [(r.at[m], h.at[m]) for m in order for r, h in ((kept, left), (got, right))]
    copies = begin(pairs, sems)
    written = []
    for i, m in enumerate(order):
        copies[2 * i].wait()
        copies[2 * i + 1].wait()
        total = (left[m].astype(F32) + right[m].astype(F32)).astype(BF)
        held, out = (high, send) if m >= half else (low, keep)
        held[m % half] = total
        copy = pltpu.make_async_copy(held.at[m % half], out.at[m % half], sems.at[2 * slots + i])
        copy.start()
        written.append(copy)
    for copy in written:
        copy.wait()


def fold(kept, got):
    slots, rows, width = kept.shape
    half = (slots // 2, rows, width)
    return call(
        fold_kernel,
        [(half, BF, "h")] * 2,
        "hh",
        [
            pltpu.VMEM(kept.shape, BF),
            pltpu.VMEM(kept.shape, BF),
            pltpu.VMEM(half, BF),
            pltpu.VMEM(half, BF),
            pltpu.SemaphoreType.DMA((3 * slots,)),
        ],
        cost=2,
    )(kept, got)


def scatter(parts, hooks=()):
    kept, sent = parts
    hooks = list(hooks)
    for j in reversed(range(chip_bits())):
        got = hop(sent, j)
        if hooks:
            got = after(got, *hooks.pop(0)(sent))
        if j:
            kept, sent = fold(kept, got)
    return kept[0], got[0]


def normalize(values):
    center = values - jnp.mean(values, -1, keepdims=True)
    inverse = lax.rsqrt(jnp.mean(center * center, -1, keepdims=True) + NORM_EPS)
    return (center * inverse, inverse)


def norm_back(grad_norm, normed, inverse):
    return inverse * (
        grad_norm
        - jnp.mean(grad_norm, -1, keepdims=True)
        - normed * jnp.mean(grad_norm * normed, -1, keepdims=True)
    )


class Layout:
    def __init__(self, span, size):
        self.span, self.size = span, size
        pad = -(-span // 128) * 128
        if (2 * span) % 128 == 0:
            self.step, self.v_at = span, span // 128 * 128
        else:
            self.step, self.v_at = pad, pad
        self.block = pad
        self.v_off = self.step - self.v_at
        self.q_at = 2 * self.step
        self.gain_at = self.q_at + span if self.step == span else 3 * pad
        self.width = -(-(self.gain_at + 2) // 128) * 128
        self.heads = span // size

    def keys(self, values):
        return values[..., : self.block]

    def values(self, values):
        return values[..., self.v_at : self.v_at + self.block]

    def queries(self, values):
        return values[..., self.q_at : self.q_at + self.block]

    def pack(self, keys, values):
        shared = self.block - self.v_at
        if not shared:
            return jnp.concatenate([keys, values], 1)
        return jnp.concatenate(
            [keys[:, : self.v_at], keys[:, self.v_at :] + values[:, :shared], values[:, shared:]], 1
        )

    def masks(self, rows, offset):
        lane = lax.broadcasted_iota(jnp.int32, (rows, self.block), 1) - offset
        return [
            (lane >= h * self.size) & (lane < (h + 1) * self.size) for h in range(self.heads)
        ]


def owned_heads(count, ring, per_ring, b):
    groups = count // ring
    return [((b % ring) * per_ring + j) * groups + b // ring for j in range(per_ring)]


def split_attn_kernel(lay, ring, per_ring, kv, query, gains, out):
    count, own, _ = out.shape
    width = query.shape[1]
    size = lay.size
    scaled = (query[...].astype(F32) * gains[:, 1:2]).astype(BF)
    both = kv[...]
    lane = lax.broadcasted_iota(jnp.int32, (own, lay.width - lay.gain_at), 1)
    tail = jnp.where(lane == 0, gains[:, 0:1], jnp.where(lane == 1, gains[:, 1:2], 0.0))
    tail = tail.astype(BF)
    for b in range(count):
        heads = owned_heads(count, ring, per_ring, b)
        pieces = []
        for source, base in ((both, 0), (both, width), (scaled, 0)):
            pieces += [source[:, base + h * size : base + (h + 1) * size] for h in heads]
            if lay.step > lay.span:
                pieces.append(jnp.zeros((own, lay.step - lay.span), BF))
        out[b] = jnp.concatenate(pieces + [tail], 1)


def split_ffn_kernel(w_in, w_down, gains, out):
    count, _, four = out.shape
    part = four // 4
    for b in range(count):
        for p in range(2):
            cols = slice((2 * b + p) * part, (2 * b + p + 1) * part)
            scaled = (w_in[:, cols].astype(F32) * gains[:, 2:3]).astype(BF)
            out[b, :, 2 * p * part : (2 * p + 1) * part] = scaled
            out[b, :, (2 * p + 1) * part : (2 * p + 2) * part] = w_down[:, cols]


def prepare_kernel(media, lats, out):
    rows = media.shape[0]
    out[:rows, :] = normalize(media[...].astype(F32))[0].astype(BF)
    out[rows:, :] = normalize(lats[...].astype(F32))[0].astype(BF)


def stacked(values, masks):
    return jnp.concatenate([jnp.where(m, values, jnp.zeros_like(values)) for m in masks], 0)


def unstacked(values, masks):
    rows = values.shape[0] // len(masks)
    total = jnp.zeros((rows, values.shape[1]), F32)
    for h, m in enumerate(masks):
        total = jnp.where(m, values[h * rows : (h + 1) * rows], total)
    return total


def patch_index(place_ref, count, media_rows, rows):
    column = lax.broadcasted_iota(jnp.int32, (rows, count * media_rows), 1)
    slot, row = column // media_rows, column % media_rows
    index = row
    for k in range(count):
        index = jnp.where(slot == k, place_ref[2 + k] * media_rows + row, index)
    return index


def scaled_columns(lay, w):
    row_media = w[:, lay.gain_at : lay.gain_at + 1].astype(F32)
    row_lat = w[:, lay.gain_at + 1 : lay.gain_at + 2].astype(F32)
    base = w[:, : lay.q_at].astype(F32)
    rest = w[:, lay.q_at :]
    return (base * row_media).astype(BF), jnp.concatenate([(base * row_lat).astype(BF), rest], 1)


def row_copies(slots, block_m, block_l, xm, xl):
    pairs = []
    for k, slot in enumerate(slots):
        pairs.append((slot.at[pl.ds(0, block_m)], xm.at[pl.ds(k * block_m, block_m)]))
        pairs.append((slot.at[pl.ds(block_m, block_l)], xl.at[pl.ds(k * block_l, block_l)]))
    return pairs


def out_copies(me, dz, near, far, held):
    planes, own, _ = near.shape
    core = me % 2
    pairs = []
    for source, which in ((near, core), (far, 1 - core)):
        for k in range(planes):
            at = pl.multiple_of(((dz ^ k) * 2 + which) * own, own)
            pairs.append((source.at[k], held.at[pl.ds(at, own)]))
    return pairs


def rows_of_heads(lay, member, wo_all, wo):
    at = pl.multiple_of(member * lay.span, lay.span)
    wo[...] = jnp.zeros(wo.shape, wo.dtype)
    wo[lay.v_off : lay.v_off + lay.span, :] = wo_all[pl.ds(at, lay.span), :]


def weight_copies(place_ref, weights, held):
    if len(weights) == 1:
        return [(weights[0], held)]
    return out_copies(place_ref[0], place_ref[1], *weights, held)


def forward_kernel(count, lay, place_ref, len_ref, *refs):
    slots, refs = refs[:count], refs[count:]
    w_hbm, kv_out, lat_out, att_out, lse_out, odd_out, low_out = refs[:7]
    xm, xl, w, wm, wl, kv_ref, lat_ref, att_ref, lse_ref, odd, low, sems, out_sems = refs[7:]
    images, media_rows = kv_ref.shape[1:3]
    lat_rows = lat_ref.shape[2]
    rows = count * lat_rows
    block_m, block_l = images * media_rows, images * lat_rows
    copies = begin([(w_hbm, w)] + row_copies(slots, block_m, block_l, xm, xl), sems)
    copies[0].wait()
    wm[...], wl[...] = scaled_columns(lay, w[...])
    step = max(1, count // 4)
    for k in range(0, count, step):
        for i in range(k, k + step):
            copies[1 + 2 * i].wait()
        proj = dot(xm[k * block_m : (k + step) * block_m, :], wm[...]).astype(BF)
        kv_ref[k : k + step] = proj.reshape(step, images, media_rows, lay.q_at)
    for k in range(count):
        copies[2 + 2 * k].wait()
    lat_ref[...] = dot(xl[...], wl[...]).reshape(lat_ref.shape)
    written = begin([(kv_ref, kv_out), (lat_ref, lat_out)], out_sems)

    scale = 1.0 / math.sqrt(lay.size)
    q_masks, v_masks = lay.masks(rows, 0), lay.masks(rows, lay.v_off)
    index = patch_index(place_ref, count, media_rows, lay.heads * rows)
    for i in range(images):
        kv = kv_ref[:, i].reshape(count * media_rows, lay.q_at)
        lat = lat_ref[:, i].reshape(rows, lay.width).astype(BF)
        queries = stacked(lay.queries(lat), q_masks)
        allowed = index < len_ref[i]
        scores = jnp.where(allowed, dot(queries, lay.keys(kv), NT) * scale, MASKED)
        lat_scores = dot(queries, lay.keys(lat), NT) * scale
        top = jnp.maximum(
            jnp.max(scores, -1, keepdims=True), jnp.max(lat_scores, -1, keepdims=True)
        )
        probs = jnp.where(allowed, jnp.exp(scores - top), 0.0)
        lat_probs = jnp.exp(lat_scores - top)
        denominator = jnp.sum(probs, -1, keepdims=True) + jnp.sum(lat_probs, -1, keepdims=True)
        weighted = dot(probs.astype(BF), lay.values(kv)) + dot(
            lat_probs.astype(BF), lay.values(lat)
        )
        attended = unstacked(weighted / denominator, v_masks)
        att_ref[:, i] = attended.reshape(count, lat_rows, lay.block)
        lse_ref[i] = jnp.broadcast_to(top + jnp.log(denominator), (lay.heads * rows, 128))
    half = count // 2
    for k in range(count):
        rounded = att_ref[k].reshape(block_l, lay.block).astype(BF)
        low[k] = rounded
        if k >= half:
            odd[k - half] = rounded
    pairs = [(odd, odd_out), (low, low_out), (att_ref, att_out), (lse_ref, lse_out)]
    written += begin(pairs, out_sems, 2)
    for copy in written:
        copy.wait()


def out_kernel(lay, ring, weights, place_ref, att_hbm, got, *refs):
    sources, outs, refs = refs[:weights], refs[weights : weights + 2], refs[weights + 2 :]
    wo_all, wo, wo_far, att, sems, *parts = refs
    half, rows = got.shape[:2]
    pairs = weight_copies(place_ref, sources, wo_all) + [(att_hbm.at[pl.ds(0, half)], att)]
    copies = begin(pairs, sems)
    for copy in copies:
        copy.wait()
    here = att[...].reshape(half * rows, lay.block)
    there = got[...].reshape(half * rows, lay.block)
    member = place_ref[0] % ring
    rows_of_heads(lay, member, wo_all, wo)
    rows_of_heads(lay, member ^ 1, wo_all, wo_far)
    written = []
    for at, step in column_steps(wo.shape[1]):
        cols = slice(at, at + step)
        total = dot(here, wo[:, cols]) + dot(there, wo_far[:, cols])
        values = [total[m * rows : (m + 1) * rows] for m in range(half)]
        put_slots(parts, outs, at, step, values, written)
    for copy in written:
        copy.wait()


def backward_kernel(count, lay, ring, weights, place_ref, len_ref, *refs):
    branch, sources, refs = refs[:count], refs[count : count + weights], refs[count + weights :]
    kv_hbm, lat_hbm, att_hbm, lse_hbm, dkv_ref, dlat_ref, dkv_odd, dlat_odd = refs[:8]
    br, kv_ref, lat_ref, wo_all, wo, att_ref, lse_ref, dwide, datt, sems = refs[8:]
    images, media_rows = kv_ref.shape[1:3]
    lat_rows = lat_ref.shape[2]
    rows = count * lat_rows
    block_m, block_l = images * media_rows, images * lat_rows
    pairs = weight_copies(place_ref, sources, wo_all)
    pairs += [(branch[k], br.at[pl.ds(k * block_l, block_l)]) for k in range(count)]
    ready = len(pairs)
    pairs += [(lat_hbm, lat_ref), (att_hbm, att_ref), (lse_hbm, lse_ref), (kv_hbm, kv_ref)]
    copies = begin(pairs, sems)
    for copy in copies[:ready]:
        copy.wait()
    rows_of_heads(lay, place_ref[0] % ring, wo_all, wo)
    datt[...] = dot(br[...], wo[...], NT).reshape(datt.shape)
    for copy in copies[ready:]:
        copy.wait()

    scale = 1.0 / math.sqrt(lay.size)
    q_masks, v_masks = lay.masks(rows, 0), lay.masks(rows, lay.v_off)
    index = patch_index(place_ref, count, media_rows, lay.heads * rows)
    for i in range(images):
        kv = kv_ref[:, i].reshape(count * media_rows, lay.q_at)
        lat = lat_ref[:, i].reshape(rows, lay.width).astype(BF)
        queries = stacked(lay.queries(lat), q_masks)
        grads = datt[:, i].reshape(rows, lay.block).astype(BF)
        attended = att_ref[:, i].reshape(rows, lay.block)
        grad_heads = stacked(grads, v_masks)
        delta = jnp.sum(stacked(grads.astype(F32) * attended, v_masks), -1, keepdims=True)
        total = lse_ref[i][:, :1]
        allowed = index < len_ref[i]
        scores = jnp.where(allowed, dot(queries, lay.keys(kv), NT) * scale, MASKED)
        lat_scores = dot(queries, lay.keys(lat), NT) * scale
        probs = jnp.where(allowed, jnp.exp(scores - total), 0.0)
        lat_probs = jnp.exp(lat_scores - total)
        score_grad = (probs * (dot(grad_heads, lay.values(kv), NT) - delta)).astype(BF)
        lat_score_grad = (lat_probs * (dot(grad_heads, lay.values(lat), NT) - delta)).astype(BF)
        query_grad = scale * unstacked(
            dot(score_grad, lay.keys(kv)) + dot(lat_score_grad, lay.keys(lat)), q_masks
        )
        dkv_ref[:, i] = (
            lay.pack(scale * dot(score_grad, queries, TN), dot(probs.astype(BF), grad_heads, TN))
            .astype(BF)
            .reshape(count, media_rows, lay.q_at)
        )
        dlat = jnp.concatenate(
            [
                lay.pack(
                    scale * dot(lat_score_grad, queries, TN),
                    dot(lat_probs.astype(BF), grad_heads, TN),
                ),
                query_grad,
            ],
            1,
        )
        dwide[:, i] = jnp.pad(dlat, ((0, 0), (0, lay.width - dlat.shape[1]))).reshape(
            count, lat_rows, lay.width
        )
    dlat_ref[...] = dwide[...].reshape(count * block_l, lay.width).astype(BF)
    half = count // 2
    for k in range(half):
        dkv_odd[k] = dkv_ref[half + k]
        dlat_odd[k] = dlat_ref[(half + k) * block_l : (half + k + 1) * block_l, :]


def input_grad_kernel(lay, *refs):
    ins, outs, refs = refs[:6], refs[6:8], refs[8:]
    dkv, dlat, dkv_got, dlat_got, w, w_far, sems, *parts = refs
    half, block_l = dlat_got.shape[:2]
    block_m = dkv_got.shape[1] * dkv_got.shape[2]
    steps = column_steps(w.shape[0])
    pairs = [
        (ins[3], dlat_got),
        (ins[2], dkv_got),
        (ins[1].at[pl.ds(0, half * block_l)], dlat),
        (ins[0].at[pl.ds(0, half)], dkv),
    ]
    ready = len(pairs)
    for at, step in steps:
        here = pl.ds(at, step)
        pairs += [(ins[4].at[here], w.at[here]), (ins[5].at[here], w_far.at[here])]
    copies = begin(pairs, sems)
    for copy in copies[:ready]:
        copy.wait()
    media_near = dkv[...].reshape(half * block_m, lay.q_at)
    media_far = dkv_got[...].reshape(half * block_m, lay.q_at)
    lat_far = dlat_got[...].reshape(half * block_l, lay.width)
    written = []
    for i, (at, step) in enumerate(steps):
        here = slice(at, at + step)
        copies[ready + 2 * i].wait()
        copies[ready + 2 * i + 1].wait()
        wm, wl = scaled_columns(lay, w[here, :])
        wm_far, wl_far = scaled_columns(lay, w_far[here, :])
        back = dot(media_near, wm, NT) + dot(media_far, wm_far, NT)
        lat = dot(dlat[...], wl, NT) + dot(lat_far, wl_far, NT)
        values = []
        for m in range(half):
            rows = [back[m * block_m : (m + 1) * block_m], lat[m * block_l : (m + 1) * block_l]]
            values.append(jnp.concatenate(rows, 0))
        put_slots(parts, outs, at, step, values, written)
    for copy in written:
        copy.wait()


def attn_weight_grad_kernel(count, lay, ring, place_ref, *refs):
    slots, branch, refs = refs[:count], refs[count : 2 * count], refs[2 * count :]
    dkv_hbm, dlat_hbm, w_hbm, att_hbm, grads_out, out_keep, out_send = refs[:7]
    xm, xl, br, out_all, dkv, dlat, w, att, grads, sems, out_sems = refs[7:]
    images, media_rows = dkv.shape[1:3]
    block_m, block_l = images * media_rows, dlat.shape[0] // count
    pairs = [(branch[k], br.at[pl.ds(k * block_l, block_l)]) for k in range(count)]
    pairs += [(att_hbm, att), (dkv_hbm, dkv), (dlat_hbm, dlat)]
    ready = len(pairs)
    steps = column_steps(xm.shape[1])
    for at, step in steps:
        cols = pl.ds(at, step)
        pairs.append((w_hbm.at[cols], w.at[cols]))
        for source, target in row_copies(slots, block_m, block_l, xm, xl):
            pairs.append((source.at[:, cols], target.at[:, cols]))
    each = (len(pairs) - ready) // len(steps)
    copies = begin(pairs, sems)
    for copy in copies[: count + 1]:
        copy.wait()
    total = dot(att[...].reshape(count * block_l, lay.block), br[...], TN)
    total = total[lay.v_off : lay.v_off + lay.span]
    per_ring, own = out_keep.shape[0], out_keep.shape[1]
    for q in range(per_ring * ring):
        out_all[q] = total[q * own : (q + 1) * own].astype(BF)
    me = place_ref[0]
    for j in range(per_ring):
        for r in range(ring):
            piece = out_all[j * ring + ((me % ring) ^ r)]
            if r:
                out_send[r - 1, j] = piece
            else:
                out_keep[j] = piece
    for copy in copies[count + 1 : ready]:
        copy.wait()
    right = dkv[...].reshape(count * block_m, lay.q_at)
    written = []
    for i, (at, step) in enumerate(steps):
        for copy in copies[ready + i * each : ready + (i + 1) * each]:
            copy.wait()
        here = slice(at, at + step)
        g_media = dot(xm[:, here], right, TN)
        g_lat = dot(xl[:, here], dlat[...], TN)
        block = w[here, :].astype(F32)
        base = block[:, : lay.q_at]
        row_media = block[:, lay.gain_at : lay.gain_at + 1]
        row_lat = block[:, lay.gain_at + 1 : lay.gain_at + 2]
        gain_media = jnp.sum(g_media * base, 1, keepdims=True)
        gain_lat = jnp.sum(g_lat[:, : lay.q_at] * base, 1, keepdims=True)
        rest = g_lat[:, lay.q_at :]
        lane = lax.broadcasted_iota(jnp.int32, rest.shape, 1) + lay.q_at
        rest = jnp.where(lane == lay.gain_at, gain_media, rest)
        rest = jnp.where(lane == lay.gain_at + 1, gain_lat, rest)
        grads[here, : lay.q_at] = (
            g_media * row_media + g_lat[:, : lay.q_at] * row_lat
        ).astype(BF)
        grads[here, lay.q_at :] = rest.astype(BF)
        rows = pl.ds(at, step)
        written += begin([(grads.at[rows], grads_out.at[rows])], out_sems, i)
    for copy in written:
        copy.wait()


def mixed_kernel(keep, got, lats, mixed, normed):
    value = keep[...].astype(F32) + got[...].astype(F32) + lats[...].astype(F32)
    mixed[...] = value
    normed[...] = normalize(value)[0].astype(BF)


def erf_parts(values):
    cdf = 0.5 * (1.0 + lax.erf(values * 0.7071067811865476))
    return cdf, cdf + values * jnp.exp(-0.5 * values * values) * GAUSS_DENSITY


def side_copies(side, weights, held):
    part = held.shape[1] // 2
    if part % 128:
        return [(weights[side], held)]
    cols = pl.ds(side * part, part)
    return [(w.at[:, cols], held.at[:, pl.ds(i * part, part)]) for i, w in enumerate(weights)]


def ffn_kernel(half, *refs):
    rows_in, cots, weights = refs[:half], refs[half : 2 * half], refs[2 * half : 2 * half + 2]
    made, outs = refs[2 * half + 2 : 2 * half + 6], refs[2 * half + 6 : 2 * half + 8]
    x, c, w_in, w_down, hidden, pre_grad, sems, out_sems, *parts = refs[2 * half + 8 :]
    rows = rows_in[0].shape[0]
    pairs = [(r, x.at[pl.ds(k * rows, rows)]) for k, r in enumerate(rows_in)]
    pairs += side_copies(0, weights, w_in)
    ready = len(pairs)
    pairs += [(r, c.at[pl.ds(k * rows, rows)]) for k, r in enumerate(cots)]
    pairs += side_copies(1, weights, w_down)
    copies = begin(pairs, sems)
    for copy in copies[:ready]:
        copy.wait()
    pre = dot(x[...], w_in[...])
    cdf, slope = erf_parts(pre)
    hidden[...] = (pre * cdf).astype(BF)
    stored = begin(core_copies(hidden, made[:2]), out_sems)
    for copy in copies[ready:]:
        copy.wait()
    pre_grad[...] = (dot(c[...], w_down[...]) * slope).astype(BF)
    stored += begin(core_copies(pre_grad, made[2:]), out_sems, 2)
    back_through(pre_grad, w_in, half, outs, parts)
    for copy in stored:
        copy.wait()


def core_copies(held, outs):
    part = held.shape[1] // 2
    if part % 128:
        return [(held, outs[0])]
    return [(held.at[:, pl.ds(i * part, part)], out) for i, out in enumerate(outs)]


def back_through(left, w, half, outs, parts):
    rows = left.shape[0] // half
    written = []
    for at, step in column_steps(w.shape[0]):
        total = dot(left[...], w[at : at + step, :], NT)
        values = [total[m * rows : (m + 1) * rows] for m in range(half)]
        put_slots(parts, outs, at, step, values, written)
    for copy in written:
        copy.wait()


def down_kernel(half, own, far, w, w_far, keep, send, hidden, w_down, sems, *parts):
    part = hidden.shape[1] // 2
    pairs = side_copies(1, (w, w_far), w_down)
    if part % 128:
        pairs.append((own, hidden))
    else:
        pairs += [(r, hidden.at[:, pl.ds(i * part, part)]) for i, r in enumerate((own, far))]
    for copy in begin(pairs, sems):
        copy.wait()
    back_through(hidden, w_down, half, (keep, send), parts)


def ffn_weight_grad_kernel(count, *refs):
    rows_in, own, far, first = refs[:count], refs[count], refs[count + 1], refs[count + 2 : -4]
    out, x, right, sems = refs[-4:]
    part, deep = right.shape[1], own.shape[0]
    rows = rows_in[0].shape[0]
    pairs = [(own, right.at[pl.ds(0, deep)]), (far, right.at[pl.ds(deep, deep)])]
    pairs += [(r, x.at[pl.ds(k * rows, rows)]) for k, r in enumerate(rows_in)]
    for copy in begin(pairs, sems):
        copy.wait()
    for at, step in column_steps(x.shape[1], 2):
        here = slice(at, at + step)
        out[here, :part] = dot(x[:, here], right[...], TN).astype(BF)
    if first:
        out[:, part:] = first[0][...]


def total_kernel(at, left, right, out, a, b, sems):
    rows = pl.ds(at, a.shape[0])
    for copy in begin([(left.at[rows], a), (right.at[rows], b)], sems):
        copy.wait()
    out[...] = (a[...].astype(F32) + b[...].astype(F32)).astype(out.dtype)


def sum_planes_kernel(grads, out):
    planes, _, width = grads.shape
    for p in range(2):
        total = grads[p].astype(F32)
        for d in range(p + 2, planes, 2):
            total = total + grads[d].astype(F32)
        out[:, p * width : (p + 1) * width] = total.astype(BF)


def first_rows(keep, got, a, b, sems):
    rows = pl.ds(0, a.shape[0])
    for copy in begin([(keep.at[rows], a), (got.at[rows], b)], sems):
        copy.wait()
    return a[...].astype(F32) + b[...].astype(F32)


def resampled_kernel(keep, got, far, mixed, out, *held):
    total = mixed[...] + first_rows(keep, got, *held) + far[...].astype(F32)
    out[...] = total.astype(out.dtype)


def ffn_back_kernel(keep, got, far, mixed, cot, mixed_grad, branch, *held):
    normed, inverse = normalize(mixed[...])
    back = first_rows(keep, got, *held) + far[...].astype(F32)
    grad = cot[...].astype(F32) + norm_back(back, normed, inverse)
    mixed_grad[...] = grad
    branch[...] = grad.astype(BF)


def final_kernel(keep, got, media, lats, mixed_grad, media_grad, lat_grad):
    rows = media.shape[0]
    back = keep[...].astype(F32) + got[...].astype(F32)
    normed, inverse = normalize(media[...].astype(F32))
    media_grad[...] = norm_back(back[:rows], normed, inverse)
    normed, inverse = normalize(lats[...].astype(F32))
    lat_grad[...] = mixed_grad[...] + norm_back(back[rows:], normed, inverse)


def finish_ffn_kernel(grads, w_in, gains, in_grad, down_grad, gain_grad):
    part = in_grad.shape[1] // grads.shape[0] // 2
    total = jnp.zeros((w_in.shape[0], 1), F32)
    for b in range(grads.shape[0]):
        for p in range(2):
            cols = slice((2 * b + p) * part, (2 * b + p + 1) * part)
            at = 2 * p * part
            raw = grads[b, :, at : at + part].astype(F32)
            total = total + jnp.sum(raw * w_in[:, cols].astype(F32), 1, keepdims=True)
            in_grad[:, cols] = raw * gains[:, 2:3]
            down_grad[:, cols] = grads[b, :, at + part : at + 2 * part].astype(F32)
    gain_grad[...] = jnp.broadcast_to(total, gain_grad.shape)


def finish_attn_kernel(lay, ring, per_ring, rows, query, gains, q_grad, kv_grad, gain_grad):
    count, own, wide = rows.shape
    width = query.shape[1]
    size = lay.size
    slots = rows[:, :, wide - lay.width :]
    place = {}
    tail = jnp.zeros((own, lay.width - lay.gain_at), F32)
    for b in range(count):
        block = slots[b].astype(F32)
        for j, h in enumerate(owned_heads(count, ring, per_ring, b)):
            for i, at in enumerate((0, lay.step, lay.q_at)):
                place[i, h] = block[:, at + j * size : at + (j + 1) * size]
        tail = tail + block[:, lay.gain_at :]
    heads = width // size
    kv_grad[:, :width] = jnp.concatenate([place[0, h] for h in range(heads)], 1)
    kv_grad[:, width:] = jnp.concatenate([place[1, h] for h in range(heads)], 1)
    raw = jnp.concatenate([place[2, h] for h in range(heads)], 1)
    q_grad[...] = raw * gains[:, 1:2]
    of_query = jnp.sum(raw * query[...].astype(F32), 1, keepdims=True)
    lane = lax.broadcasted_iota(jnp.int32, gain_grad.shape, 1)
    gain_grad[...] = jnp.where(lane == 0, tail[:, 0:1], tail[:, 1:2] + of_query)


def body(
    latents,
    media,
    media_lengths,
    cotangent,
    query_weight,
    kv_weight,
    out_weight,
    in_weight,
    down_weight,
    media_gain,
    latent_gain,
    ffn_gain,
):
    images, lat_rows, width = latents.shape
    media_rows = media.shape[1]
    nb, nd = lax.axis_size("blk"), lax.axis_size("dp")
    half = nb // 2
    size = width // HEADS
    heads = HEADS // nb
    own = query_weight.shape[0]
    plane = nb * own
    span = heads * size
    lay = Layout(span, size)
    hidden_width = in_weight.shape[1]
    part = hidden_width // nb // 2
    me = lax.axis_index("blk").astype(jnp.int32)
    dz = lax.axis_index("dp").astype(jnp.int32)
    place = jnp.concatenate([jnp.stack([me, dz]), owners(me)])
    ring = size // own
    per_ring = nd // ring
    groups = nb // ring
    block_m, block_l = images * media_rows, images * lat_rows
    block = block_m + block_l
    all_m, all_l = nb * block_m, nb * block_l
    sems = pltpu.SemaphoreType.DMA

    gains = jnp.stack([media_gain, latent_gain, ffn_gain], 1).astype(F32)
    (attn_parts,) = call(
        partial(split_attn_kernel, lay, ring, per_ring), [((nb, own, lay.width), BF, "d")], "ddd"
    )(kv_weight, query_weight, gains)

    quick = ring == 2 and own % 16 == 0
    if quick:
        out_near = [out_weight] + [swap(out_weight, k, "dp") for k in range(1, nd)]
    else:
        ring_groups = [[g * ring + i for i in range(ring)] for g in range(groups)]
        out_w = lax.all_gather(out_weight, "dp", axis=0, tiled=False)
        out_w = lax.all_gather(out_w, "blk", axis=0, tiled=False, axis_index_groups=ring_groups)
        out_near = [out_w.transpose(1, 0, 2, 3).reshape(nd * ring * own, width)]

    mine = lax.all_to_all(attn_parts, "blk", 0, 0, tiled=True).reshape(plane, -1)
    attn_w = lax.all_gather(after(mine, *out_near), "dp", axis=0, tiled=True)

    media_flat = media.reshape(block_m, width)
    lat_flat = latents.reshape(block_l, width)
    cot_flat = cotangent.reshape(block_l, width)
    (normed,) = call(prepare_kernel, [((block, width), BF, "d")], "dd", cost=3)(
        after(media_flat, attn_parts), lat_flat
    )
    slots = gather_all(normed)
    cot_pair = jnp.concatenate([cot_flat, swap(cot_flat, 1, "dp")], 0)

    (ffn_parts,) = call(split_ffn_kernel, [((nb, own, 4 * part), BF, "d")], "ddd", cost=4, big=True)(
        after(in_weight, normed), down_weight, gains
    )
    ffn_mine = lax.all_to_all(after(ffn_parts, mine), "blk", 0, 0, tiled=True)
    ffn_mine = ffn_mine.reshape(plane, 4 * part)
    by_plane = jnp.stack(
        [ffn_mine[:, d % 2 * 2 * part : (d % 2 + 1) * 2 * part] for d in range(nd)]
    )
    ffn_w = lax.all_to_all(after(by_plane, *slots, attn_w, cot_pair), "dp", 0, 0, tiled=True)
    ffn_w = ffn_w.reshape(width, 2 * part)

    if quick:
        near = jnp.stack(out_near)
        out_w = [near, swap(near, 1)]
    else:
        out_w = out_near

    cot_kind = gather_kind(after(cot_pair, *slots))
    kv_shape = (nb, images, media_rows, lay.q_at)
    lat_shape = (nb, images, lat_rows, lay.width)
    att_shape = (nb, images, lat_rows, lay.block)
    lse_shape = (images, heads * nb * lat_rows, 128)
    odd_shape = (half, block_l, lay.block)
    low_shape = (nb, block_l, lay.block)
    shapes = [(kv_shape, BF), (lat_shape, F32), (att_shape, F32), (lse_shape, F32)]
    shapes += [(odd_shape, BF), (low_shape, BF)]
    kv, lat_proj, attended, totals, att_odd, att_low = call(
        partial(forward_kernel, nb, lay),
        [(shape, kind, "h") for shape, kind in shapes],
        "ss" + "h" * (nb + 1),
        [
            pltpu.VMEM((all_m, width), BF),
            pltpu.VMEM((all_l, width), BF),
            pltpu.VMEM((width, lay.width), BF),
            pltpu.VMEM((width, lay.q_at), BF),
            pltpu.VMEM((width, lay.width), BF),
        ]
        + [pltpu.VMEM(shape, kind) for shape, kind in shapes]
        + [sems((1 + 2 * nb,)), sems((6,))],
        big=True,
            cost=11,
    )(place, media_lengths, *slots, attn_w)

    def exchange(rows):
        return kept_and_sent((half // 2, rows, width))

    outs, scratch = exchange(block_l)
    parts = call(
        partial(out_kernel, lay, ring, len(out_w)),
        outs,
        "shd" + "h" * len(out_w),
        [
            pltpu.VMEM((nd * ring * own, width), BF),
            pltpu.VMEM((lay.block, width), BF),
            pltpu.VMEM((lay.block, width), BF),
            pltpu.VMEM(odd_shape, BF),
            sems((2 * nd + 1,)),
            *scratch,
        ],
        cost=3,
    )(place, att_low, swap(after(att_odd, *cot_kind[1:3]), 1), *out_w)
    mixed, ffn_in = call(
        mixed_kernel, [((block_l, width), F32, "d"), ((block_l, width), BF, "d")], "ddd"
    )(*scatter(parts, [lambda sent: cot_kind[3:]]), lat_flat)

    mid = block_l // 2
    in_kind = gather_kind(
        jnp.concatenate([ffn_in, swap(ffn_in[:mid], 1, "dp"), swap(ffn_in[mid:], 1, "dp")], 0)
    )
    ffn_far = swap(after(ffn_w, *in_kind[1:3]), 1)
    if part % 128:
        ffn_sides = [
            jnp.concatenate([ffn_w[:, i * part : (i + 1) * part], ffn_far[:, i * part : (i + 1) * part]], 1)
            for i in range(2)
        ]
    else:
        ffn_sides = [ffn_w, ffn_far]
    rows_pair = half * 2 * block_l
    outs, scratch = exchange(2 * block_l)
    cut = part % 128 == 0
    made_shape = (rows_pair, part if cut else 2 * part)
    spare_shape = made_shape if cut else (8, 128)
    hid_own, hid_far, pre_own, pre_far, *parts = call(
        partial(ffn_kernel, half),
        [(made_shape, BF, "h"), (spare_shape, BF, "h")] * 2 + outs,
        "h" * (2 * half + 2),
        [
            pltpu.VMEM((rows_pair, width), BF),
            pltpu.VMEM((rows_pair, width), BF),
            pltpu.VMEM((width, 2 * part), BF),
            pltpu.VMEM((width, 2 * part), BF),
            pltpu.VMEM((rows_pair, 2 * part), BF),
            pltpu.VMEM((rows_pair, 2 * part), BF),
            sems((2 * half + 4,)),
            sems((4,)),
            *scratch,
        ],
        big=True,
            cost=9,
    )(*in_kind, *cot_kind, *ffn_sides)

    def ffn_weight_grad(rows, own_rows, far_rows, *first):
        if not cut:
            own_rows, far_rows = own_rows[:, :part], own_rows[:, part:]
        return call(
            partial(ffn_weight_grad_kernel, nb),
            [((width, part * (1 + len(first))), BF, "d")],
            "h" * (nb + 2) + "d" * len(first),
            [
                pltpu.VMEM((2 * rows_pair, width), BF),
                pltpu.VMEM((2 * rows_pair, part), BF),
                sems((nb + 2,)),
            ],
            big=True,
            cost=4,
        )(*rows, own_rows, swap(far_rows, 1), *first)[0]

    few_rows = [pltpu.VMEM((block_l, width), BF)] * 2 + [sems((2,))]

    def total_far(left, right):
        return call(
            partial(total_kernel, block_l), [((block_l, width), BF, "d")], "hh", few_rows, cost=1
        )(left, right)[0]

    made = {}

    def beside_first(sent):
        made["down"] = ffn_weight_grad(with_other(cot_kind), after(hid_own, sent), hid_far)
        made["both"] = ffn_weight_grad(with_other(in_kind), pre_own, pre_far, made["down"])
        return (made["both"],)

    def beside_second(sent):
        outs, scratch = exchange(2 * block_l)
        made["parts"] = call(
            partial(down_kernel, half),
            outs,
            "hhhh",
            [
                pltpu.VMEM((rows_pair, 2 * part), BF),
                pltpu.VMEM((width, 2 * part), BF),
                sems((4,)),
                *scratch,
            ],
            big=True,
            cost=4,
        )(after(hid_own, sent), hid_far, *ffn_sides)
        return made["parts"]

    terms = scatter(parts, [beside_first, beside_second])
    pair_got = swap(total_far(*terms), 1, "dp")
    mixed_grad, branch = call(
        ffn_back_kernel,
        [((block_l, width), F32, "d"), ((block_l, width), BF, "d")],
        "hhddd",
        few_rows,
    )(*terms, pair_got, mixed, cot_flat)
    branch_slots = gather_all(branch)
    ffn_planes = lax.all_to_all(
        after(made["both"], pair_got).reshape(nd, plane, 2 * part), "dp", 0, 0, tiled=True
    )

    (ffn_rows,) = call(sum_planes_kernel, [((plane, 4 * part), BF, "d")], "d", cost=3)(ffn_planes)
    ffn_slots = lax.all_to_all(ffn_rows.reshape(nb, own, 4 * part), "blk", 0, 0, tiled=True)

    def keep_second(sent):
        made["second"] = sent
        return ()

    down_terms = scatter(made["parts"], [lambda sent: (), keep_second])

    dkv, dlat, dkv_odd, dlat_odd = call(
        partial(backward_kernel, nb, lay, ring, len(out_w)),
        [
            (kv_shape, BF, "d"),
            ((all_l, lay.width), BF, "d"),
            ((half, *kv_shape[1:]), BF, "d"),
            ((half, block_l, lay.width), BF, "d"),
        ],
        "ss" + "h" * (nb + len(out_w) + 4),
        [
            pltpu.VMEM((all_l, width), BF),
            pltpu.VMEM(kv_shape, BF),
            pltpu.VMEM(lat_shape, F32),
            pltpu.VMEM((nd * ring * own, width), BF),
            pltpu.VMEM((lay.block, width), BF),
            pltpu.VMEM(att_shape, F32),
            pltpu.VMEM(lse_shape, F32),
            pltpu.VMEM(lat_shape, F32),
            pltpu.VMEM(att_shape, F32),
            sems((nb + 2 * nd + 4,)),
        ],
        big=True,
            cost=1,
    )(place, media_lengths, *branch_slots, *out_w, kv, lat_proj, attended, totals)

    attn_grads, out_keep, out_send = call(
        partial(attn_weight_grad_kernel, nb, lay, ring),
        [
            ((width, lay.width), BF, "h"),
            ((per_ring, own, width), BF, "d"),
            ((ring - 1, per_ring, own, width), BF, "d"),
        ],
        "s" + "h" * (2 * nb + 4),
        [
            pltpu.VMEM((all_m, width), BF),
            pltpu.VMEM((all_l, width), BF),
            pltpu.VMEM((all_l, width), BF),
            pltpu.VMEM((per_ring * ring, own, width), BF),
            pltpu.VMEM(kv_shape, BF),
            pltpu.VMEM((all_l, lay.width), BF),
            pltpu.VMEM((width, lay.width), BF),
            pltpu.VMEM(low_shape, BF),
            pltpu.VMEM((width, lay.width), BF),
            sems((nb + 3 + 3 * (1 + 2 * nb),)),
            sems((3,)),
        ],
        big=True,
            cost=1,
    )(place, *slots, *branch_slots, after(dkv, *down_terms), dlat, attn_w, att_low)
    attn_sum = lax.psum_scatter(attn_grads, "dp", scatter_dimension=0, tiled=True)

    outs, scratch = exchange(block)
    parts = call(
        partial(input_grad_kernel, lay),
        outs,
        "hhhhhh",
        [
            pltpu.VMEM((half, *kv_shape[1:]), BF),
            pltpu.VMEM((half * block_l, lay.width), BF),
            pltpu.VMEM((half, *kv_shape[1:]), BF),
            pltpu.VMEM((half, block_l, lay.width), BF),
            pltpu.VMEM((width, lay.width), BF),
            pltpu.VMEM((width, lay.width), BF),
            sems((10,)),
            *scratch,
        ],
        big=True,
            cost=1,
    )(
        after(dkv, attn_grads),
        dlat,
        swap(dkv_odd, 1),
        swap(dlat_odd, 1),
        attn_w,
        swap(attn_w, 1),
    )
    media_grad, latents_grad = call(
        final_kernel, [((block_m, width), F32, "d"), ((block_l, width), F32, "d")], "ddddd", cost=5
    )(*scatter(parts, [lambda sent: (ffn_rows,), lambda sent: (ffn_slots,)]), media_flat, lat_flat, mixed_grad)

    (resampled,) = call(resampled_kernel, [((block_l, width), BF, "d")], "hhdd", few_rows)(
        *down_terms, swap(total_far(*down_terms), 1, "dp"), mixed
    )

    in_grad, down_grad, ffn_gain_grad = call(
        finish_ffn_kernel,
        [((own, hidden_width), F32, "d")] * 2 + [((own, 128), F32, "d")],
        "ddd",
        cost=3,
    )(ffn_slots, in_weight, gains)

    attn_slots = lax.all_to_all(attn_sum.reshape(nb, own, -1), "blk", 0, 0, tiled=True)
    query_grad, kv_grad, gain_grads = call(
        partial(finish_attn_kernel, lay, ring, per_ring),
        [((own, width), F32, "d"), ((own, 2 * width), F32, "d"), ((own, 128), F32, "d")],
        "ddd",
    )(attn_slots, query_weight, gains)

    pieces = [out_keep] + [swap(out_send[r - 1], r) for r in range(1, ring)]
    pieces = jnp.stack(pieces)
    rank = lax.axis_index("blk") % ring
    pieces = [lax.dynamic_index_in_dim(pieces, rank ^ r, 0, False) for r in range(ring)]
    out_rows = jnp.concatenate(pieces, 0).reshape(nd * own, width)
    out_rows = after(out_rows, attn_sum)
    out_grad = lax.psum_scatter(out_rows, "dp", scatter_dimension=0, tiled=True).astype(F32)
    return (
        resampled.reshape(latents.shape),
        latents_grad.reshape(latents.shape),
        media_grad.reshape(media.shape),
        query_grad,
        kv_grad,
        out_grad,
        in_grad,
        down_grad,
        gain_grads[:, 0],
        gain_grads[:, 1],
        ffn_gain_grad[:, 0],
    )


def solution(mesh):
    rows = P("dp", "blk", None)
    weight = P(("dp", "blk"), None)
    gain = P(("dp", "blk"))
    return jax.shard_map(
        body,
        mesh=mesh,
        in_specs=(rows, rows, P("dp"), rows) + (weight,) * 5 + (gain,) * 3,
        out_specs=(rows,) * 3 + (weight,) * 5 + (gain,) * 3,
        check_vma=False,
    )
```

```python
from functools import partial
import math

import jax
import jax.numpy as jnp
from jax import lax
from jax.experimental import pallas as pl
from jax.experimental.pallas import tpu as pltpu
from jax.sharding import PartitionSpec as P

HEADS = 16
NORM_EPS = 1e-05
MASKED = -1e30
GAUSS_DENSITY = 0.3989422804014327
BF = jnp.bfloat16
F32 = jnp.float32
MIB = 1 << 20
VMEM_MIB = 56
NT = ((1,), (1,))
TN = ((0,), (0,))


def chip_bits():
    return lax.axis_size("blk").bit_length() - 2


def hop_bit(j, core):
    return 2 << ((j + core) % chip_bits())


def hop(array, j):
    return lax.ppermute(
        array, "blk", [(i, i ^ hop_bit(j, i % 2)) for i in range(lax.axis_size("blk"))]
    )


def swap(array, bit, axis="blk"):
    return lax.ppermute(array, axis, [(i, i ^ bit) for i in range(lax.axis_size(axis))])


def gather_kind(block):
    blocks = [block]
    for j in range(chip_bits()):
        blocks = blocks + [hop(b, j) for b in blocks]
    return blocks


def gather_all(block):
    return with_other(gather_kind(block))


def with_other(blocks):
    return blocks + [swap(b, 1) for b in blocks]


def owners(me):
    tables = []
    for core in range(2):
        steps = [hop_bit(j, core) for j in range(chip_bits())]
        tables.append(
            [sum(s for j, s in enumerate(steps) if m >> j & 1) for m in range(1 << len(steps))]
        )
    both = [tables[c] + [1 ^ k for k in tables[1 - c]] for c in range(2)]
    return me ^ jnp.where(me % 2 == 0, jnp.array(both[0]), jnp.array(both[1])).astype(jnp.int32)


def after(array, *others):
    return lax.optimization_barrier((array, *others))[0]


def dot(left, right, dims=((1,), (0,))):
    return lax.dot_general(left, right, (dims, ((), ())), preferred_element_type=F32)


def padded_bytes(shape, kind):
    item = jnp.dtype(kind).itemsize
    *lead, rows, lanes = (1, *shape) if len(shape) == 1 else shape
    tile = 32 // item
    return math.prod(lead) * (-(-rows // tile) * tile) * (-(-lanes // 128) * 128) * item


def begin(pairs, sems, first=0):
    copies = [pltpu.make_async_copy(s, d, sems.at[first + i]) for i, (s, d) in enumerate(pairs)]
    for copy in copies:
        copy.start()
    return copies


def call(kernel, outs, spaces, scratch=(), cost=2, big=False, room=6):
    fetched = [i for i, letter in enumerate(spaces) if letter == "d"]
    stored = [i for i, out in enumerate(outs) if out[2] == "d"]
    first = len(spaces)
    last = first + len(outs)
    sems = pltpu.SemaphoreType.DMA

    def run(*operands):
        held = [pltpu.VMEM(operands[i].shape, operands[i].dtype) for i in fetched]
        made = [pltpu.VMEM(outs[i][0], outs[i][1]) for i in stored]
        size = sum(
            padded_bytes(b.shape, b.dtype)
            for b in (*scratch, *held, *made)
            if b.memory_space == pltpu.VMEM
        )

        def whole(*refs):
            at = last + len(scratch)
            own, extra = list(refs[:at]), list(refs[at:])
            out_sems, in_sems = extra.pop(), extra.pop()
            held_refs, made_refs = extra[: len(fetched)], extra[len(fetched) :]
            copies = begin([(own[i], r) for i, r in zip(fetched, held_refs)], in_sems)
            results = [(r, own[first + i]) for i, r in zip(stored, made_refs)]
            for i, r in zip(fetched, held_refs):
                own[i] = r
            for i, r in zip(stored, made_refs):
                own[first + i] = r
            for copy in copies:
                copy.wait()
            kernel(*own)
            for copy in begin(results, out_sems):
                copy.wait()

        return pl.pallas_call(
            whole,
            out_shape=[jax.ShapeDtypeStruct(shape, kind) for shape, kind, _ in outs],
            in_specs=[
                pl.BlockSpec(memory_space=pltpu.SMEM if s == "s" else pltpu.HBM) for s in spaces
            ],
            out_specs=[pl.BlockSpec(memory_space=pltpu.HBM)] * len(outs),
            scratch_shapes=[
                *scratch,
                *held,
                *made,
                sems((max(1, len(fetched)),)),
                sems((max(1, len(stored)),)),
            ],
            compiler_params=pltpu.CompilerParams(vmem_limit_bytes=VMEM_MIB * MIB if big else size + room * MIB),
            cost_estimate=pl.CostEstimate(
                flops=int(cost * 1.15e9), bytes_accessed=int(cost * 3.6e6), transcendentals=0
            ),
        )(*operands)

    return run


def column_steps(width, steps=3):
    step = width // steps if width % (128 * steps) == 0 else width
    return [(at, step) for at in range(0, width, step)]


def kept_and_sent(shape):
    return [(shape, BF, "h")] * 2, [
        pltpu.VMEM(shape, BF),
        pltpu.VMEM(shape, BF),
        pltpu.SemaphoreType.DMA((6,)),
    ]


def put_slots(parts, outs, at, step, values, written):
    kept, sent, sems = parts
    half = kept.shape[0]
    for m, value in enumerate(values):
        (sent if m // half else kept)[m % half, :, at : at + step] = value.astype(BF)
    for source, target in ((kept, outs[0]), (sent, outs[1])):
        cols = pl.ds(at, step)
        copy = pltpu.make_async_copy(
            source.at[:, :, cols], target.at[:, :, cols], sems.at[len(written)]
        )
        copy.start()
        written.append(copy)


def fold_kernel(kept, got, keep, send, left, right, low, high, sems):
    slots = left.shape[0]
    half = slots // 2
    order = [m for i in range(half) for m in (i + half, i)]
    pairs = [(r.at[m], h.at[m]) for m in order for r, h in ((kept, left), (got, right))]
    copies = begin(pairs, sems)
    written = []
    for i, m in enumerate(order):
        copies[2 * i].wait()
        copies[2 * i + 1].wait()
        total = (left[m].astype(F32) + right[m].astype(F32)).astype(BF)
        held, out = (high, send) if m >= half else (low, keep)
        held[m % half] = total
        copy = pltpu.make_async_copy(held.at[m % half], out.at[m % half], sems.at[2 * slots + i])
        copy.start()
        written.append(copy)
    for copy in written:
        copy.wait()


def fold(kept, got):
    slots, rows, width = kept.shape
    half = (slots // 2, rows, width)
    return call(
        fold_kernel,
        [(half, BF, "h")] * 2,
        "hh",
        [
            pltpu.VMEM(kept.shape, BF),
            pltpu.VMEM(kept.shape, BF),
            pltpu.VMEM(half, BF),
            pltpu.VMEM(half, BF),
            pltpu.SemaphoreType.DMA((3 * slots,)),
        ],
        cost=2,
    )(kept, got)


def scatter(parts, hooks=()):
    kept, sent = parts
    hooks = list(hooks)
    for j in reversed(range(chip_bits())):
        got = hop(sent, j)
        if hooks:
            got = after(got, *hooks.pop(0)(sent))
        if j:
            kept, sent = fold(kept, got)
    return kept[0], got[0]


def normalize(values):
    center = values - jnp.mean(values, -1, keepdims=True)
    inverse = lax.rsqrt(jnp.mean(center * center, -1, keepdims=True) + NORM_EPS)
    return (center * inverse, inverse)


def norm_back(grad_norm, normed, inverse):
    return inverse * (
        grad_norm
        - jnp.mean(grad_norm, -1, keepdims=True)
        - normed * jnp.mean(grad_norm * normed, -1, keepdims=True)
    )


class Layout:
    def __init__(self, span, size):
        self.span, self.size = span, size
        pad = -(-span // 128) * 128
        if (2 * span) % 128 == 0:
            self.step, self.v_at = span, span // 128 * 128
        else:
            self.step, self.v_at = pad, pad
        self.block = pad
        self.v_off = self.step - self.v_at
        self.q_at = 2 * self.step
        self.gain_at = self.q_at + span if self.step == span else 3 * pad
        self.width = -(-(self.gain_at + 2) // 128) * 128
        self.heads = span // size

    def keys(self, values):
        return values[..., : self.block]

    def values(self, values):
        return values[..., self.v_at : self.v_at + self.block]

    def queries(self, values):
        return values[..., self.q_at : self.q_at + self.block]

    def pack(self, keys, values):
        shared = self.block - self.v_at
        if not shared:
            return jnp.concatenate([keys, values], 1)
        return jnp.concatenate(
            [keys[:, : self.v_at], keys[:, self.v_at :] + values[:, :shared], values[:, shared:]], 1
        )

    def masks(self, rows, offset):
        lane = lax.broadcasted_iota(jnp.int32, (rows, self.block), 1) - offset
        return [
            (lane >= h * self.size) & (lane < (h + 1) * self.size) for h in range(self.heads)
        ]


def owned_heads(count, ring, per_ring, b):
    groups = count // ring
    return [((b % ring) * per_ring + j) * groups + b // ring for j in range(per_ring)]


def split_attn_kernel(lay, ring, per_ring, kv, query, gains, out):
    count, own, _ = out.shape
    width = query.shape[1]
    size = lay.size
    scaled = (query[...].astype(F32) * gains[:, 1:2]).astype(BF)
    both = kv[...]
    lane = lax.broadcasted_iota(jnp.int32, (own, lay.width - lay.gain_at), 1)
    tail = jnp.where(lane == 0, gains[:, 0:1], jnp.where(lane == 1, gains[:, 1:2], 0.0))
    tail = tail.astype(BF)
    for b in range(count):
        heads = owned_heads(count, ring, per_ring, b)
        pieces = []
        for source, base in ((both, 0), (both, width), (scaled, 0)):
            pieces += [source[:, base + h * size : base + (h + 1) * size] for h in heads]
            if lay.step > lay.span:
                pieces.append(jnp.zeros((own, lay.step - lay.span), BF))
        out[b] = jnp.concatenate(pieces + [tail], 1)


def split_ffn_kernel(w_in, w_down, gains, out):
    count, _, four = out.shape
    part = four // 4
    for b in range(count):
        for p in range(2):
            cols = slice((2 * b + p) * part, (2 * b + p + 1) * part)
            scaled = (w_in[:, cols].astype(F32) * gains[:, 2:3]).astype(BF)
            out[b, :, 2 * p * part : (2 * p + 1) * part] = scaled
            out[b, :, (2 * p + 1) * part : (2 * p + 2) * part] = w_down[:, cols]


def prepare_kernel(media, lats, out):
    rows = media.shape[0]
    out[:rows, :] = normalize(media[...].astype(F32))[0].astype(BF)
    out[rows:, :] = normalize(lats[...].astype(F32))[0].astype(BF)


def stacked(values, masks):
    return jnp.concatenate([jnp.where(m, values, jnp.zeros_like(values)) for m in masks], 0)


def unstacked(values, masks):
    rows = values.shape[0] // len(masks)
    total = jnp.zeros((rows, values.shape[1]), F32)
    for h, m in enumerate(masks):
        total = jnp.where(m, values[h * rows : (h + 1) * rows], total)
    return total


def patch_index(place_ref, count, media_rows, rows):
    column = lax.broadcasted_iota(jnp.int32, (rows, count * media_rows), 1)
    slot, row = column // media_rows, column % media_rows
    index = row
    for k in range(count):
        index = jnp.where(slot == k, place_ref[2 + k] * media_rows + row, index)
    return index


def scaled_columns(lay, w):
    row_media = w[:, lay.gain_at : lay.gain_at + 1].astype(F32)
    row_lat = w[:, lay.gain_at + 1 : lay.gain_at + 2].astype(F32)
    base = w[:, : lay.q_at].astype(F32)
    rest = w[:, lay.q_at :]
    return (base * row_media).astype(BF), jnp.concatenate([(base * row_lat).astype(BF), rest], 1)


def row_copies(slots, block_m, block_l, xm, xl):
    pairs = []
    for k, slot in enumerate(slots):
        pairs.append((slot.at[pl.ds(0, block_m)], xm.at[pl.ds(k * block_m, block_m)]))
        pairs.append((slot.at[pl.ds(block_m, block_l)], xl.at[pl.ds(k * block_l, block_l)]))
    return pairs


def out_copies(me, dz, near, far, held):
    planes, own, _ = near.shape
    core = me % 2
    pairs = []
    for source, which in ((near, core), (far, 1 - core)):
        for k in range(planes):
            at = pl.multiple_of(((dz ^ k) * 2 + which) * own, own)
            pairs.append((source.at[k], held.at[pl.ds(at, own)]))
    return pairs


def rows_of_heads(lay, member, wo_all, wo):
    at = pl.multiple_of(member * lay.span, lay.span)
    wo[...] = jnp.zeros(wo.shape, wo.dtype)
    wo[lay.v_off : lay.v_off + lay.span, :] = wo_all[pl.ds(at, lay.span), :]


def weight_copies(place_ref, weights, held):
    if len(weights) == 1:
        return [(weights[0], held)]
    return out_copies(place_ref[0], place_ref[1], *weights, held)


def forward_kernel(count, lay, place_ref, len_ref, *refs):
    slots, refs = refs[:count], refs[count:]
    w_hbm, kv_out, lat_out, att_out, lse_out, odd_out, low_out = refs[:7]
    xm, xl, w, wm, wl, kv_ref, lat_ref, att_ref, lse_ref, odd, low, sems, out_sems = refs[7:]
    images, media_rows = kv_ref.shape[1:3]
    lat_rows = lat_ref.shape[2]
    rows = count * lat_rows
    block_m, block_l = images * media_rows, images * lat_rows
    copies = begin([(w_hbm, w)] + row_copies(slots, block_m, block_l, xm, xl), sems)
    copies[0].wait()
    wm[...], wl[...] = scaled_columns(lay, w[...])
    step = max(1, count // 4)
    for k in range(0, count, step):
        for i in range(k, k + step):
            copies[1 + 2 * i].wait()
        proj = dot(xm[k * block_m : (k + step) * block_m, :], wm[...]).astype(BF)
        kv_ref[k : k + step] = proj.reshape(step, images, media_rows, lay.q_at)
    for k in range(count):
        copies[2 + 2 * k].wait()
    lat_ref[...] = dot(xl[...], wl[...]).reshape(lat_ref.shape)
    written = begin([(kv_ref, kv_out), (lat_ref, lat_out)], out_sems)

    scale = 1.0 / math.sqrt(lay.size)
    q_masks, v_masks = lay.masks(rows, 0), lay.masks(rows, lay.v_off)
    index = patch_index(place_ref, count, media_rows, lay.heads * rows)
    for i in range(images):
        kv = kv_ref[:, i].reshape(count * media_rows, lay.q_at)
        lat = lat_ref[:, i].reshape(rows, lay.width).astype(BF)
        queries = stacked(lay.queries(lat), q_masks)
        allowed = index < len_ref[i]
        scores = jnp.where(allowed, dot(queries, lay.keys(kv), NT) * scale, MASKED)
        lat_scores = dot(queries, lay.keys(lat), NT) * scale
        top = jnp.maximum(
            jnp.max(scores, -1, keepdims=True), jnp.max(lat_scores, -1, keepdims=True)
        )
        probs = jnp.where(allowed, jnp.exp(scores - top), 0.0)
        lat_probs = jnp.exp(lat_scores - top)
        denominator = jnp.sum(probs, -1, keepdims=True) + jnp.sum(lat_probs, -1, keepdims=True)
        weighted = dot(probs.astype(BF), lay.values(kv)) + dot(
            lat_probs.astype(BF), lay.values(lat)
        )
        attended = unstacked(weighted / denominator, v_masks)
        att_ref[:, i] = attended.reshape(count, lat_rows, lay.block)
        lse_ref[i] = jnp.broadcast_to(top + jnp.log(denominator), (lay.heads * rows, 128))
    half = count // 2
    for k in range(count):
        rounded = att_ref[k].reshape(block_l, lay.block).astype(BF)
        low[k] = rounded
        if k >= half:
            odd[k - half] = rounded
    pairs = [(odd, odd_out), (low, low_out), (att_ref, att_out), (lse_ref, lse_out)]
    written += begin(pairs, out_sems, 2)
    for copy in written:
        copy.wait()


def out_kernel(lay, ring, weights, place_ref, att_hbm, got, *refs):
    sources, outs, refs = refs[:weights], refs[weights : weights + 2], refs[weights + 2 :]
    wo_all, wo, wo_far, att, sems, *parts = refs
    half, rows = got.shape[:2]
    pairs = weight_copies(place_ref, sources, wo_all) + [(att_hbm.at[pl.ds(0, half)], att)]
    copies = begin(pairs, sems)
    for copy in copies:
        copy.wait()
    here = att[...].reshape(half * rows, lay.block)
    there = got[...].reshape(half * rows, lay.block)
    member = place_ref[0] % ring
    rows_of_heads(lay, member, wo_all, wo)
    rows_of_heads(lay, member ^ 1, wo_all, wo_far)
    written = []
    for at, step in column_steps(wo.shape[1]):
        cols = slice(at, at + step)
        total = dot(here, wo[:, cols]) + dot(there, wo_far[:, cols])
        values = [total[m * rows : (m + 1) * rows] for m in range(half)]
        put_slots(parts, outs, at, step, values, written)
    for copy in written:
        copy.wait()


def backward_kernel(count, lay, ring, weights, place_ref, len_ref, *refs):
    branch, sources, refs = refs[:count], refs[count : count + weights], refs[count + weights :]
    kv_hbm, lat_hbm, att_hbm, lse_hbm, dkv_ref, dlat_ref, dkv_odd, dlat_odd = refs[:8]
    br, kv_ref, lat_ref, wo_all, wo, att_ref, lse_ref, dwide, datt, sems = refs[8:]
    images, media_rows = kv_ref.shape[1:3]
    lat_rows = lat_ref.shape[2]
    rows = count * lat_rows
    block_m, block_l = images * media_rows, images * lat_rows
    pairs = weight_copies(place_ref, sources, wo_all)
    pairs += [(branch[k], br.at[pl.ds(k * block_l, block_l)]) for k in range(count)]
    ready = len(pairs)
    pairs += [(lat_hbm, lat_ref), (att_hbm, att_ref), (lse_hbm, lse_ref), (kv_hbm, kv_ref)]
    copies = begin(pairs, sems)
    for copy in copies[:ready]:
        copy.wait()
    rows_of_heads(lay, place_ref[0] % ring, wo_all, wo)
    datt[...] = dot(br[...], wo[...], NT).reshape(datt.shape)
    for copy in copies[ready:]:
        copy.wait()

    scale = 1.0 / math.sqrt(lay.size)
    q_masks, v_masks = lay.masks(rows, 0), lay.masks(rows, lay.v_off)
    index = patch_index(place_ref, count, media_rows, lay.heads * rows)
    for i in range(images):
        kv = kv_ref[:, i].reshape(count * media_rows, lay.q_at)
        lat = lat_ref[:, i].reshape(rows, lay.width).astype(BF)
        queries = stacked(lay.queries(lat), q_masks)
        grads = datt[:, i].reshape(rows, lay.block).astype(BF)
        attended = att_ref[:, i].reshape(rows, lay.block)
        grad_heads = stacked(grads, v_masks)
        delta = jnp.sum(stacked(grads.astype(F32) * attended, v_masks), -1, keepdims=True)
        total = lse_ref[i][:, :1]
        allowed = index < len_ref[i]
        scores = jnp.where(allowed, dot(queries, lay.keys(kv), NT) * scale, MASKED)
        lat_scores = dot(queries, lay.keys(lat), NT) * scale
        probs = jnp.where(allowed, jnp.exp(scores - total), 0.0)
        lat_probs = jnp.exp(lat_scores - total)
        score_grad = (probs * (dot(grad_heads, lay.values(kv), NT) - delta)).astype(BF)
        lat_score_grad = (lat_probs * (dot(grad_heads, lay.values(lat), NT) - delta)).astype(BF)
        query_grad = scale * unstacked(
            dot(score_grad, lay.keys(kv)) + dot(lat_score_grad, lay.keys(lat)), q_masks
        )
        dkv_ref[:, i] = (
            lay.pack(scale * dot(score_grad, queries, TN), dot(probs.astype(BF), grad_heads, TN))
            .astype(BF)
            .reshape(count, media_rows, lay.q_at)
        )
        dlat = jnp.concatenate(
            [
                lay.pack(
                    scale * dot(lat_score_grad, queries, TN),
                    dot(lat_probs.astype(BF), grad_heads, TN),
                ),
                query_grad,
            ],
            1,
        )
        dwide[:, i] = jnp.pad(dlat, ((0, 0), (0, lay.width - dlat.shape[1]))).reshape(
            count, lat_rows, lay.width
        )
    dlat_ref[...] = dwide[...].reshape(count * block_l, lay.width).astype(BF)
    half = count // 2
    for k in range(half):
        dkv_odd[k] = dkv_ref[half + k]
        dlat_odd[k] = dlat_ref[(half + k) * block_l : (half + k + 1) * block_l, :]


def input_grad_kernel(lay, *refs):
    ins, outs, refs = refs[:6], refs[6:8], refs[8:]
    dkv, dlat, w, w_far, sems, *parts = refs
    count, width, block_l = dkv.shape[0], dkv.shape[-1] // 2, dlat.shape[0] // dkv.shape[0]
    block_m = dkv.shape[1] * dkv.shape[2]
    steps = column_steps(w.shape[0])
    pairs = []
    for c, (media, lat) in enumerate(((ins[0], ins[1]), (ins[2], ins[3]))):
        pairs.append((lat.at[pl.ds(0, count * block_l)], dlat.at[:, pl.ds(c * lay.width, lay.width)]))
        pairs.append((media.at[pl.ds(0, count)], dkv.at[:, :, :, pl.ds(c * width, width)]))
    ready = len(pairs)
    for at, step in steps:
        here = pl.ds(at, step)
        pairs += [(ins[4].at[here], w.at[here]), (ins[5].at[here], w_far.at[here])]
    copies = begin(pairs, sems)
    for copy in copies[:ready]:
        copy.wait()
    media_rows = dkv[...].reshape(count * block_m, 2 * width)
    written = []
    for i, (at, step) in enumerate(steps):
        here = slice(at, at + step)
        copies[ready + 2 * i].wait()
        copies[ready + 2 * i + 1].wait()
        near, far = scaled_columns(lay, w[here, :]), scaled_columns(lay, w_far[here, :])
        back = dot(media_rows, jnp.concatenate([near[0], far[0]], 1), NT)
        lat = dot(dlat[...], jnp.concatenate([near[1], far[1]], 1), NT)
        values = []
        for m in range(count):
            rows = [back[m * block_m : (m + 1) * block_m], lat[m * block_l : (m + 1) * block_l]]
            values.append(jnp.concatenate(rows, 0))
        put_slots(parts, outs, at, step, values, written)
    for copy in written:
        copy.wait()


def attn_weight_grad_kernel(count, lay, ring, place_ref, *refs):
    slots, branch, refs = refs[:count], refs[count : 2 * count], refs[2 * count :]
    dkv_hbm, dlat_hbm, w_hbm, att_hbm, grads_out, out_keep, out_send = refs[:7]
    xm, xl, br, out_all, dkv, dlat, w, att, grads, sems, out_sems = refs[7:]
    images, media_rows = dkv.shape[1:3]
    block_m, block_l = images * media_rows, dlat.shape[0] // count
    pairs = [(branch[k], br.at[pl.ds(k * block_l, block_l)]) for k in range(count)]
    pairs += [(att_hbm, att), (dkv_hbm, dkv), (dlat_hbm, dlat)]
    ready = len(pairs)
    steps = column_steps(xm.shape[1])
    for at, step in steps:
        cols = pl.ds(at, step)
        pairs.append((w_hbm.at[cols], w.at[cols]))
        for source, target in row_copies(slots, block_m, block_l, xm, xl):
            pairs.append((source.at[:, cols], target.at[:, cols]))
    each = (len(pairs) - ready) // len(steps)
    copies = begin(pairs, sems)
    for copy in copies[: count + 1]:
        copy.wait()
    total = dot(att[...].reshape(count * block_l, lay.block), br[...], TN)
    total = total[lay.v_off : lay.v_off + lay.span]
    per_ring, own = out_keep.shape[0], out_keep.shape[1]
    for q in range(per_ring * ring):
        out_all[q] = total[q * own : (q + 1) * own].astype(BF)
    me = place_ref[0]
    for j in range(per_ring):
        for r in range(ring):
            piece = out_all[j * ring + ((me % ring) ^ r)]
            if r:
                out_send[r - 1, j] = piece
            else:
                out_keep[j] = piece
    for copy in copies[count + 1 : ready]:
        copy.wait()
    right = dkv[...].reshape(count * block_m, lay.q_at)
    written = []
    for i, (at, step) in enumerate(steps):
        for copy in copies[ready + i * each : ready + (i + 1) * each]:
            copy.wait()
        here = slice(at, at + step)
        g_media = dot(xm[:, here], right, TN)
        g_lat = dot(xl[:, here], dlat[...], TN)
        block = w[here, :].astype(F32)
        base = block[:, : lay.q_at]
        row_media = block[:, lay.gain_at : lay.gain_at + 1]
        row_lat = block[:, lay.gain_at + 1 : lay.gain_at + 2]
        gain_media = jnp.sum(g_media * base, 1, keepdims=True)
        gain_lat = jnp.sum(g_lat[:, : lay.q_at] * base, 1, keepdims=True)
        rest = g_lat[:, lay.q_at :]
        lane = lax.broadcasted_iota(jnp.int32, rest.shape, 1) + lay.q_at
        rest = jnp.where(lane == lay.gain_at, gain_media, rest)
        rest = jnp.where(lane == lay.gain_at + 1, gain_lat, rest)
        grads[here, : lay.q_at] = (
            g_media * row_media + g_lat[:, : lay.q_at] * row_lat
        ).astype(BF)
        grads[here, lay.q_at :] = rest.astype(BF)
        rows = pl.ds(at, step)
        written += begin([(grads.at[rows], grads_out.at[rows])], out_sems, i)
    for copy in written:
        copy.wait()


def mixed_kernel(keep, got, lats, mixed, normed):
    value = keep[...].astype(F32) + got[...].astype(F32) + lats[...].astype(F32)
    mixed[...] = value
    normed[...] = normalize(value)[0].astype(BF)


def erf_parts(values):
    cdf = 0.5 * (1.0 + lax.erf(values * 0.7071067811865476))
    return cdf, cdf + values * jnp.exp(-0.5 * values * values) * GAUSS_DENSITY


def side_copies(side, weights, held):
    part = held.shape[1] // 2
    if part % 128:
        return [(weights[side], held)]
    cols = pl.ds(side * part, part)
    return [(w.at[:, cols], held.at[:, pl.ds(i * part, part)]) for i, w in enumerate(weights)]


def ffn_kernel(half, *refs):
    rows_in, cots, weights = refs[:half], refs[half : 2 * half], refs[2 * half : 2 * half + 2]
    made, outs = refs[2 * half + 2 : 2 * half + 6], refs[2 * half + 6 : 2 * half + 8]
    x, c, w_in, w_down, hidden, pre_grad, sems, out_sems, *parts = refs[2 * half + 8 :]
    rows = rows_in[0].shape[0]
    pairs = [(r, x.at[pl.ds(k * rows, rows)]) for k, r in enumerate(rows_in)]
    pairs += side_copies(0, weights, w_in)
    ready = len(pairs)
    pairs += [(r, c.at[pl.ds(k * rows, rows)]) for k, r in enumerate(cots)]
    pairs += side_copies(1, weights, w_down)
    copies = begin(pairs, sems)
    for copy in copies[:ready]:
        copy.wait()
    pre = dot(x[...], w_in[...])
    cdf, slope = erf_parts(pre)
    hidden[...] = (pre * cdf).astype(BF)
    stored = begin(core_copies(hidden, made[:2]), out_sems)
    for copy in copies[ready:]:
        copy.wait()
    pre_grad[...] = (dot(c[...], w_down[...]) * slope).astype(BF)
    stored += begin(core_copies(pre_grad, made[2:]), out_sems, 2)
    back_through(pre_grad, w_in, half, outs, parts)
    for copy in stored:
        copy.wait()


def core_copies(held, outs):
    part = held.shape[1] // 2
    if part % 128:
        return [(held, outs[0])]
    return [(held.at[:, pl.ds(i * part, part)], out) for i, out in enumerate(outs)]


def back_through(left, w, half, outs, parts):
    rows = left.shape[0] // half
    written = []
    for at, step in column_steps(w.shape[0], 1):
        total = dot(left[...], w[at : at + step, :], NT)
        values = [total[m * rows : (m + 1) * rows] for m in range(half)]
        put_slots(parts, outs, at, step, values, written)
    for copy in written:
        copy.wait()


def down_kernel(half, own, far, w, w_far, keep, send, hidden, w_down, sems, *parts):
    part = hidden.shape[1] // 2
    pairs = side_copies(1, (w, w_far), w_down)
    if part % 128:
        pairs.append((own, hidden))
    else:
        pairs += [(r, hidden.at[:, pl.ds(i * part, part)]) for i, r in enumerate((own, far))]
    for copy in begin(pairs, sems):
        copy.wait()
    back_through(hidden, w_down, half, (keep, send), parts)


def ffn_weight_grad_kernel(count, *refs):
    rows_in, own, far, first = refs[:count], refs[count], refs[count + 1], refs[count + 2 : -4]
    out, x, right, sems = refs[-4:]
    part, deep = right.shape[1], own.shape[0]
    rows = rows_in[0].shape[0]
    pairs = [(own, right.at[pl.ds(0, deep)]), (far, right.at[pl.ds(deep, deep)])]
    pairs += [(r, x.at[pl.ds(k * rows, rows)]) for k, r in enumerate(rows_in)]
    for copy in begin(pairs, sems):
        copy.wait()
    for at, step in column_steps(x.shape[1], 2):
        here = slice(at, at + step)
        out[here, :part] = dot(x[:, here], right[...], TN).astype(BF)
    if first:
        out[:, part:] = first[0][...]


def total_kernel(at, left, right, out, a, b, sems):
    rows = pl.ds(at, a.shape[0])
    for copy in begin([(left.at[rows], a), (right.at[rows], b)], sems):
        copy.wait()
    out[...] = (a[...].astype(F32) + b[...].astype(F32)).astype(out.dtype)


def sum_planes_kernel(grads, out):
    planes, _, width = grads.shape
    for p in range(2):
        total = grads[p].astype(F32)
        for d in range(p + 2, planes, 2):
            total = total + grads[d].astype(F32)
        out[:, p * width : (p + 1) * width] = total.astype(BF)


def first_rows(keep, got, a, b, sems):
    rows = pl.ds(0, a.shape[0])
    for copy in begin([(keep.at[rows], a), (got.at[rows], b)], sems):
        copy.wait()
    return a[...].astype(F32) + b[...].astype(F32)


def resampled_kernel(keep, got, far, mixed, out, *held):
    total = mixed[...] + first_rows(keep, got, *held) + far[...].astype(F32)
    out[...] = total.astype(out.dtype)


def ffn_back_kernel(keep, got, far, mixed, cot, mixed_grad, branch, *held):
    normed, inverse = normalize(mixed[...])
    back = first_rows(keep, got, *held) + far[...].astype(F32)
    grad = cot[...].astype(F32) + norm_back(back, normed, inverse)
    mixed_grad[...] = grad
    branch[...] = grad.astype(BF)


def final_kernel(keep, got, media, lats, mixed_grad, media_grad, lat_grad):
    rows = media.shape[0]
    back = keep[...].astype(F32) + got[...].astype(F32)
    normed, inverse = normalize(media[...].astype(F32))
    media_grad[...] = norm_back(back[:rows], normed, inverse)
    normed, inverse = normalize(lats[...].astype(F32))
    lat_grad[...] = mixed_grad[...] + norm_back(back[rows:], normed, inverse)


def finish_ffn_kernel(grads, w_in, gains, in_grad, down_grad, gain_grad):
    part = in_grad.shape[1] // grads.shape[0] // 2
    total = jnp.zeros((w_in.shape[0], 1), F32)
    for b in range(grads.shape[0]):
        for p in range(2):
            cols = slice((2 * b + p) * part, (2 * b + p + 1) * part)
            at = 2 * p * part
            raw = grads[b, :, at : at + part].astype(F32)
            total = total + jnp.sum(raw * w_in[:, cols].astype(F32), 1, keepdims=True)
            in_grad[:, cols] = raw * gains[:, 2:3]
            down_grad[:, cols] = grads[b, :, at + part : at + 2 * part].astype(F32)
    gain_grad[...] = jnp.broadcast_to(total, gain_grad.shape)


def finish_attn_kernel(lay, ring, per_ring, rows, query, gains, q_grad, kv_grad, gain_grad):
    count, own, wide = rows.shape
    width = query.shape[1]
    size = lay.size
    slots = rows[:, :, wide - lay.width :]
    place = {}
    tail = jnp.zeros((own, lay.width - lay.gain_at), F32)
    for b in range(count):
        block = slots[b].astype(F32)
        for j, h in enumerate(owned_heads(count, ring, per_ring, b)):
            for i, at in enumerate((0, lay.step, lay.q_at)):
                place[i, h] = block[:, at + j * size : at + (j + 1) * size]
        tail = tail + block[:, lay.gain_at :]
    heads = width // size
    kv_grad[:, :width] = jnp.concatenate([place[0, h] for h in range(heads)], 1)
    kv_grad[:, width:] = jnp.concatenate([place[1, h] for h in range(heads)], 1)
    raw = jnp.concatenate([place[2, h] for h in range(heads)], 1)
    q_grad[...] = raw * gains[:, 1:2]
    of_query = jnp.sum(raw * query[...].astype(F32), 1, keepdims=True)
    lane = lax.broadcasted_iota(jnp.int32, gain_grad.shape, 1)
    gain_grad[...] = jnp.where(lane == 0, tail[:, 0:1], tail[:, 1:2] + of_query)


def body(
    latents,
    media,
    media_lengths,
    cotangent,
    query_weight,
    kv_weight,
    out_weight,
    in_weight,
    down_weight,
    media_gain,
    latent_gain,
    ffn_gain,
):
    images, lat_rows, width = latents.shape
    media_rows = media.shape[1]
    nb, nd = lax.axis_size("blk"), lax.axis_size("dp")
    half = nb // 2
    size = width // HEADS
    heads = HEADS // nb
    own = query_weight.shape[0]
    plane = nb * own
    span = heads * size
    lay = Layout(span, size)
    hidden_width = in_weight.shape[1]
    part = hidden_width // nb // 2
    me = lax.axis_index("blk").astype(jnp.int32)
    dz = lax.axis_index("dp").astype(jnp.int32)
    place = jnp.concatenate([jnp.stack([me, dz]), owners(me)])
    ring = size // own
    per_ring = nd // ring
    groups = nb // ring
    block_m, block_l = images * media_rows, images * lat_rows
    block = block_m + block_l
    all_m, all_l = nb * block_m, nb * block_l
    sems = pltpu.SemaphoreType.DMA

    gains = jnp.stack([media_gain, latent_gain, ffn_gain], 1).astype(F32)
    (attn_parts,) = call(
        partial(split_attn_kernel, lay, ring, per_ring), [((nb, own, lay.width), BF, "d")], "ddd"
    )(kv_weight, query_weight, gains)

    quick = ring == 2 and own % 16 == 0
    if quick:
        out_near = [out_weight] + [swap(out_weight, k, "dp") for k in range(1, nd)]
    else:
        ring_groups = [[g * ring + i for i in range(ring)] for g in range(groups)]
        out_w = lax.all_gather(out_weight, "dp", axis=0, tiled=False)
        out_w = lax.all_gather(out_w, "blk", axis=0, tiled=False, axis_index_groups=ring_groups)
        out_near = [out_w.transpose(1, 0, 2, 3).reshape(nd * ring * own, width)]

    mine = lax.all_to_all(attn_parts, "blk", 0, 0, tiled=True).reshape(plane, -1)
    attn_w = lax.all_gather(after(mine, *out_near), "dp", axis=0, tiled=True)

    media_flat = media.reshape(block_m, width)
    lat_flat = latents.reshape(block_l, width)
    cot_flat = cotangent.reshape(block_l, width)
    (normed,) = call(prepare_kernel, [((block, width), BF, "d")], "dd", cost=3)(
        after(media_flat, attn_parts), lat_flat
    )
    slots = gather_all(normed)
    cot_pair = jnp.concatenate([cot_flat, swap(cot_flat, 1, "dp")], 0)

    (ffn_parts,) = call(split_ffn_kernel, [((nb, own, 4 * part), BF, "d")], "ddd", cost=4, big=True)(
        after(in_weight, normed), down_weight, gains
    )
    ffn_mine = lax.all_to_all(after(ffn_parts, mine), "blk", 0, 0, tiled=True)
    ffn_mine = ffn_mine.reshape(plane, 4 * part)
    by_plane = jnp.stack(
        [ffn_mine[:, d % 2 * 2 * part : (d % 2 + 1) * 2 * part] for d in range(nd)]
    )
    ffn_w = lax.all_to_all(after(by_plane, *slots, attn_w, cot_pair), "dp", 0, 0, tiled=True)
    ffn_w = ffn_w.reshape(width, 2 * part)

    if quick:
        near = jnp.stack(out_near)
        out_w = [near, swap(near, 1)]
    else:
        out_w = out_near

    cot_kind = gather_kind(after(cot_pair, *slots))
    kv_shape = (nb, images, media_rows, lay.q_at)
    lat_shape = (nb, images, lat_rows, lay.width)
    att_shape = (nb, images, lat_rows, lay.block)
    lse_shape = (images, heads * nb * lat_rows, 128)
    odd_shape = (half, block_l, lay.block)
    low_shape = (nb, block_l, lay.block)
    shapes = [(kv_shape, BF), (lat_shape, F32), (att_shape, F32), (lse_shape, F32)]
    shapes += [(odd_shape, BF), (low_shape, BF)]
    kv, lat_proj, attended, totals, att_odd, att_low = call(
        partial(forward_kernel, nb, lay),
        [(shape, kind, "h") for shape, kind in shapes],
        "ss" + "h" * (nb + 1),
        [
            pltpu.VMEM((all_m, width), BF),
            pltpu.VMEM((all_l, width), BF),
            pltpu.VMEM((width, lay.width), BF),
            pltpu.VMEM((width, lay.q_at), BF),
            pltpu.VMEM((width, lay.width), BF),
        ]
        + [pltpu.VMEM(shape, kind) for shape, kind in shapes]
        + [sems((1 + 2 * nb,)), sems((6,))],
        big=True,
            cost=11,
    )(place, media_lengths, *slots, attn_w)

    def exchange(rows):
        return kept_and_sent((half // 2, rows, width))

    outs, scratch = exchange(block_l)
    parts = call(
        partial(out_kernel, lay, ring, len(out_w)),
        outs,
        "shd" + "h" * len(out_w),
        [
            pltpu.VMEM((nd * ring * own, width), BF),
            pltpu.VMEM((lay.block, width), BF),
            pltpu.VMEM((lay.block, width), BF),
            pltpu.VMEM(odd_shape, BF),
            sems((2 * nd + 1,)),
            *scratch,
        ],
        cost=3,
    )(place, att_low, swap(after(att_odd, *cot_kind[1:3]), 1), *out_w)
    mixed, ffn_in = call(
        mixed_kernel, [((block_l, width), F32, "d"), ((block_l, width), BF, "d")], "ddd"
    )(*scatter(parts, [lambda sent: cot_kind[3:]]), lat_flat)

    mid = block_l // 2
    in_kind = gather_kind(
        jnp.concatenate([ffn_in, swap(ffn_in[:mid], 1, "dp"), swap(ffn_in[mid:], 1, "dp")], 0)
    )
    ffn_far = swap(after(ffn_w, *in_kind[1:3]), 1)
    if part % 128:
        ffn_sides = [
            jnp.concatenate([ffn_w[:, i * part : (i + 1) * part], ffn_far[:, i * part : (i + 1) * part]], 1)
            for i in range(2)
        ]
    else:
        ffn_sides = [ffn_w, ffn_far]
    rows_pair = half * 2 * block_l
    outs, scratch = exchange(2 * block_l)
    cut = part % 128 == 0
    made_shape = (rows_pair, part if cut else 2 * part)
    spare_shape = made_shape if cut else (8, 128)
    hid_own, hid_far, pre_own, pre_far, *parts = call(
        partial(ffn_kernel, half),
        [(made_shape, BF, "h"), (spare_shape, BF, "h")] * 2 + outs,
        "h" * (2 * half + 2),
        [
            pltpu.VMEM((rows_pair, width), BF),
            pltpu.VMEM((rows_pair, width), BF),
            pltpu.VMEM((width, 2 * part), BF),
            pltpu.VMEM((width, 2 * part), BF),
            pltpu.VMEM((rows_pair, 2 * part), BF),
            pltpu.VMEM((rows_pair, 2 * part), BF),
            sems((2 * half + 4,)),
            sems((4,)),
            *scratch,
        ],
        room=14,
            cost=1,
    )(*in_kind, *cot_kind, *ffn_sides)

    def ffn_weight_grad(rows, own_rows, far_rows, *first):
        if not cut:
            own_rows, far_rows = own_rows[:, :part], own_rows[:, part:]
        return call(
            partial(ffn_weight_grad_kernel, nb),
            [((width, part * (1 + len(first))), BF, "d")],
            "h" * (nb + 2) + "d" * len(first),
            [
                pltpu.VMEM((2 * rows_pair, width), BF),
                pltpu.VMEM((2 * rows_pair, part), BF),
                sems((nb + 2,)),
            ],
            room=14,
            cost=4,
        )(*rows, own_rows, swap(far_rows, 1), *first)[0]

    few_rows = [pltpu.VMEM((block_l, width), BF)] * 2 + [sems((2,))]

    def total_far(left, right):
        return call(
            partial(total_kernel, block_l), [((block_l, width), BF, "d")], "hh", few_rows, cost=1
        )(left, right)[0]

    made = {}

    def beside_first(sent):
        made["down"] = ffn_weight_grad(with_other(cot_kind), after(hid_own, sent), hid_far)
        made["both"] = ffn_weight_grad(with_other(in_kind), pre_own, pre_far, made["down"])
        return (made["both"],)

    def beside_second(sent):
        outs, scratch = exchange(2 * block_l)
        made["parts"] = call(
            partial(down_kernel, half),
            outs,
            "hhhh",
            [
                pltpu.VMEM((rows_pair, 2 * part), BF),
                pltpu.VMEM((width, 2 * part), BF),
                sems((4,)),
                *scratch,
            ],
            cost=4,
        )(after(hid_own, sent), hid_far, *ffn_sides)
        return made["parts"]

    terms = scatter(parts, [beside_first, beside_second])
    pair_got = swap(total_far(*terms), 1, "dp")
    mixed_grad, branch = call(
        ffn_back_kernel,
        [((block_l, width), F32, "d"), ((block_l, width), BF, "d")],
        "hhddd",
        few_rows,
    )(*terms, pair_got, mixed, cot_flat)
    branch_slots = gather_all(branch)
    ffn_planes = lax.all_to_all(
        after(made["both"], branch).reshape(nd, plane, 2 * part), "dp", 0, 0, tiled=True
    )

    (ffn_rows,) = call(sum_planes_kernel, [((plane, 4 * part), BF, "d")], "d", cost=3)(ffn_planes)
    ffn_slots = lax.all_to_all(ffn_rows.reshape(nb, own, 4 * part), "blk", 0, 0, tiled=True)

    def keep_second(sent):
        made["second"] = sent
        return ()

    down_terms = scatter(made["parts"], [lambda sent: (), keep_second])

    dkv, dlat, dkv_odd, dlat_odd = call(
        partial(backward_kernel, nb, lay, ring, len(out_w)),
        [
            (kv_shape, BF, "d"),
            ((all_l, lay.width), BF, "d"),
            ((half, *kv_shape[1:]), BF, "d"),
            ((half, block_l, lay.width), BF, "d"),
        ],
        "ss" + "h" * (nb + len(out_w) + 4),
        [
            pltpu.VMEM((all_l, width), BF),
            pltpu.VMEM(kv_shape, BF),
            pltpu.VMEM(lat_shape, F32),
            pltpu.VMEM((nd * ring * own, width), BF),
            pltpu.VMEM((lay.block, width), BF),
            pltpu.VMEM(att_shape, F32),
            pltpu.VMEM(lse_shape, F32),
            pltpu.VMEM(lat_shape, F32),
            pltpu.VMEM(att_shape, F32),
            sems((nb + 2 * nd + 4,)),
        ],
        big=True,
            cost=1,
    )(place, media_lengths, *branch_slots, *out_w, kv, lat_proj, attended, totals)

    attn_grads, out_keep, out_send = call(
        partial(attn_weight_grad_kernel, nb, lay, ring),
        [
            ((width, lay.width), BF, "h"),
            ((per_ring, own, width), BF, "d"),
            ((ring - 1, per_ring, own, width), BF, "d"),
        ],
        "s" + "h" * (2 * nb + 4),
        [
            pltpu.VMEM((all_m, width), BF),
            pltpu.VMEM((all_l, width), BF),
            pltpu.VMEM((all_l, width), BF),
            pltpu.VMEM((per_ring * ring, own, width), BF),
            pltpu.VMEM(kv_shape, BF),
            pltpu.VMEM((all_l, lay.width), BF),
            pltpu.VMEM((width, lay.width), BF),
            pltpu.VMEM(low_shape, BF),
            pltpu.VMEM((width, lay.width), BF),
            sems((nb + 3 + 3 * (1 + 2 * nb),)),
            sems((3,)),
        ],
        big=True,
            cost=1,
    )(place, *slots, *branch_slots, after(dkv, *down_terms), dlat, attn_w, att_low)
    attn_sum = lax.psum_scatter(attn_grads, "dp", scatter_dimension=0, tiled=True)

    outs, scratch = exchange(block)
    parts = call(
        partial(input_grad_kernel, lay),
        outs,
        "hhhhhh",
        [
            pltpu.VMEM((half, *kv_shape[1:-1], 2 * lay.q_at), BF),
            pltpu.VMEM((half * block_l, 2 * lay.width), BF),
            pltpu.VMEM((width, lay.width), BF),
            pltpu.VMEM((width, lay.width), BF),
            sems((10,)),
            *scratch,
        ],
        big=True,
            cost=1,
    )(
        after(dkv, attn_grads),
        dlat,
        swap(dkv_odd, 1),
        swap(dlat_odd, 1).reshape(half * block_l, lay.width),
        attn_w,
        swap(attn_w, 1),
    )
    (resampled,) = call(resampled_kernel, [((block_l, width), BF, "d")], "hhdd", few_rows)(
        *down_terms, swap(total_far(*down_terms), 1, "dp"), mixed
    )

    pieces = [out_keep] + [swap(out_send[r - 1], r) for r in range(1, ring)]
    pieces = jnp.stack(pieces)
    rank = lax.axis_index("blk") % ring
    pieces = [lax.dynamic_index_in_dim(pieces, rank ^ r, 0, False) for r in range(ring)]
    out_rows = jnp.concatenate(pieces, 0).reshape(nd * own, width)
    media_grad, latents_grad = call(
        final_kernel, [((block_m, width), F32, "d"), ((block_l, width), F32, "d")], "ddddd", cost=5
    )(*scatter(parts, [lambda sent: (ffn_rows, resampled), lambda sent: (ffn_slots, out_rows)]), media_flat, lat_flat, mixed_grad)

    in_grad, down_grad, ffn_gain_grad = call(
        finish_ffn_kernel,
        [((own, hidden_width), F32, "d")] * 2 + [((own, 128), F32, "d")],
        "ddd",
        cost=3,
    )(ffn_slots, in_weight, gains)

    attn_slots = lax.all_to_all(attn_sum.reshape(nb, own, -1), "blk", 0, 0, tiled=True)
    query_grad, kv_grad, gain_grads = call(
        partial(finish_attn_kernel, lay, ring, per_ring),
        [((own, width), F32, "d"), ((own, 2 * width), F32, "d"), ((own, 128), F32, "d")],
        "ddd",
    )(attn_slots, query_weight, gains)

    out_rows = after(out_rows, attn_sum)
    out_grad = lax.psum_scatter(out_rows, "dp", scatter_dimension=0, tiled=True).astype(F32)
    return (
        resampled.reshape(latents.shape),
        latents_grad.reshape(latents.shape),
        media_grad.reshape(media.shape),
        query_grad,
        kv_grad,
        out_grad,
        in_grad,
        down_grad,
        gain_grads[:, 0],
        gain_grads[:, 1],
        ffn_gain_grad[:, 0],
    )


def solution(mesh):
    rows = P("dp", "blk", None)
    weight = P(("dp", "blk"), None)
    gain = P(("dp", "blk"))
    return jax.shard_map(
        body,
        mesh=mesh,
        in_specs=(rows, rows, P("dp"), rows) + (weight,) * 5 + (gain,) * 3,
        out_specs=(rows,) * 3 + (weight,) * 5 + (gain,) * 3,
        check_vma=False,
    )
```

```python
from functools import partial
import math

import jax
import jax.numpy as jnp
from jax import lax
from jax.experimental import pallas as pl
from jax.experimental.pallas import tpu as pltpu
from jax.sharding import PartitionSpec as P

HEADS = 16
NORM_EPS = 1e-05
MASKED = -1e30
GAUSS_DENSITY = 0.3989422804014327
BF = jnp.bfloat16
F32 = jnp.float32
MIB = 1 << 20
VMEM_MIB = 56
NT = ((1,), (1,))
TN = ((0,), (0,))


def chip_bits():
    return lax.axis_size("blk").bit_length() - 2


def hop_bit(j, core):
    return 2 << ((j + core) % chip_bits())


def hop(array, j):
    return lax.ppermute(
        array, "blk", [(i, i ^ hop_bit(j, i % 2)) for i in range(lax.axis_size("blk"))]
    )


def swap(array, bit, axis="blk"):
    return lax.ppermute(array, axis, [(i, i ^ bit) for i in range(lax.axis_size(axis))])


def gather_kind(block):
    blocks = [block]
    for j in range(chip_bits()):
        blocks = blocks + [hop(b, j) for b in blocks]
    return blocks


def gather_all(block):
    return with_other(gather_kind(block))


def with_other(blocks):
    return blocks + [swap(b, 1) for b in blocks]


def owners(me):
    tables = []
    for core in range(2):
        steps = [hop_bit(j, core) for j in range(chip_bits())]
        tables.append(
            [sum(s for j, s in enumerate(steps) if m >> j & 1) for m in range(1 << len(steps))]
        )
    both = [tables[c] + [1 ^ k for k in tables[1 - c]] for c in range(2)]
    return me ^ jnp.where(me % 2 == 0, jnp.array(both[0]), jnp.array(both[1])).astype(jnp.int32)


def after(array, *others):
    return lax.optimization_barrier((array, *others))[0]


def dot(left, right, dims=((1,), (0,))):
    return lax.dot_general(left, right, (dims, ((), ())), preferred_element_type=F32)


def padded_bytes(shape, kind):
    item = jnp.dtype(kind).itemsize
    *lead, rows, lanes = (1, *shape) if len(shape) == 1 else shape
    tile = 32 // item
    return math.prod(lead) * (-(-rows // tile) * tile) * (-(-lanes // 128) * 128) * item


def begin(pairs, sems, first=0):
    copies = [pltpu.make_async_copy(s, d, sems.at[first + i]) for i, (s, d) in enumerate(pairs)]
    for copy in copies:
        copy.start()
    return copies


def call(kernel, outs, spaces, scratch=(), cost=2, big=False, room=6):
    fetched = [i for i, letter in enumerate(spaces) if letter == "d"]
    stored = [i for i, out in enumerate(outs) if out[2] == "d"]
    first = len(spaces)
    last = first + len(outs)
    sems = pltpu.SemaphoreType.DMA

    def run(*operands):
        held = [pltpu.VMEM(operands[i].shape, operands[i].dtype) for i in fetched]
        made = [pltpu.VMEM(outs[i][0], outs[i][1]) for i in stored]
        size = sum(
            padded_bytes(b.shape, b.dtype)
            for b in (*scratch, *held, *made)
            if b.memory_space == pltpu.VMEM
        )

        def whole(*refs):
            at = last + len(scratch)
            own, extra = list(refs[:at]), list(refs[at:])
            out_sems, in_sems = extra.pop(), extra.pop()
            held_refs, made_refs = extra[: len(fetched)], extra[len(fetched) :]
            copies = begin([(own[i], r) for i, r in zip(fetched, held_refs)], in_sems)
            results = [(r, own[first + i]) for i, r in zip(stored, made_refs)]
            for i, r in zip(fetched, held_refs):
                own[i] = r
            for i, r in zip(stored, made_refs):
                own[first + i] = r
            for copy in copies:
                copy.wait()
            kernel(*own)
            for copy in begin(results, out_sems):
                copy.wait()

        return pl.pallas_call(
            whole,
            out_shape=[jax.ShapeDtypeStruct(shape, kind) for shape, kind, _ in outs],
            in_specs=[
                pl.BlockSpec(memory_space=pltpu.SMEM if s == "s" else pltpu.HBM) for s in spaces
            ],
            out_specs=[pl.BlockSpec(memory_space=pltpu.HBM)] * len(outs),
            scratch_shapes=[
                *scratch,
                *held,
                *made,
                sems((max(1, len(fetched)),)),
                sems((max(1, len(stored)),)),
            ],
            compiler_params=pltpu.CompilerParams(vmem_limit_bytes=VMEM_MIB * MIB if big else size + room * MIB),
            cost_estimate=pl.CostEstimate(
                flops=int(cost * 1.15e9), bytes_accessed=int(cost * 3.6e6), transcendentals=0
            ),
        )(*operands)

    return run


def column_steps(width, steps=3):
    step = width // steps if width % (128 * steps) == 0 else width
    return [(at, step) for at in range(0, width, step)]


def kept_and_sent(shape):
    return [(shape, BF, "h")] * 2, [
        pltpu.VMEM(shape, BF),
        pltpu.VMEM(shape, BF),
        pltpu.SemaphoreType.DMA((6,)),
    ]


def put_slots(parts, outs, at, step, values, written):
    kept, sent, sems = parts
    half = kept.shape[0]
    for m, value in enumerate(values):
        (sent if m // half else kept)[m % half, :, at : at + step] = value.astype(BF)
    for source, target in ((kept, outs[0]), (sent, outs[1])):
        cols = pl.ds(at, step)
        copy = pltpu.make_async_copy(
            source.at[:, :, cols], target.at[:, :, cols], sems.at[len(written)]
        )
        copy.start()
        written.append(copy)


def fold_kernel(kept, got, keep, send, left, right, low, high, sems):
    slots = left.shape[0]
    half = slots // 2
    order = [m for i in range(half) for m in (i + half, i)]
    pairs = [(r.at[m], h.at[m]) for m in order for r, h in ((kept, left), (got, right))]
    copies = begin(pairs, sems)
    written = []
    for i, m in enumerate(order):
        copies[2 * i].wait()
        copies[2 * i + 1].wait()
        total = (left[m].astype(F32) + right[m].astype(F32)).astype(BF)
        held, out = (high, send) if m >= half else (low, keep)
        held[m % half] = total
        copy = pltpu.make_async_copy(held.at[m % half], out.at[m % half], sems.at[2 * slots + i])
        copy.start()
        written.append(copy)
    for copy in written:
        copy.wait()


def fold(kept, got):
    slots, rows, width = kept.shape
    half = (slots // 2, rows, width)
    return call(
        fold_kernel,
        [(half, BF, "h")] * 2,
        "hh",
        [
            pltpu.VMEM(kept.shape, BF),
            pltpu.VMEM(kept.shape, BF),
            pltpu.VMEM(half, BF),
            pltpu.VMEM(half, BF),
            pltpu.SemaphoreType.DMA((3 * slots,)),
        ],
        cost=2,
    )(kept, got)


def scatter(parts, hooks=()):
    kept, sent = parts
    hooks = list(hooks)
    for j in reversed(range(chip_bits())):
        got = hop(sent, j)
        if hooks:
            got = after(got, *hooks.pop(0)(sent))
        if j:
            kept, sent = fold(kept, got)
    return kept[0], got[0]


def normalize(values):
    center = values - jnp.mean(values, -1, keepdims=True)
    inverse = lax.rsqrt(jnp.mean(center * center, -1, keepdims=True) + NORM_EPS)
    return (center * inverse, inverse)


def norm_back(grad_norm, normed, inverse):
    return inverse * (
        grad_norm
        - jnp.mean(grad_norm, -1, keepdims=True)
        - normed * jnp.mean(grad_norm * normed, -1, keepdims=True)
    )


class Layout:
    def __init__(self, span, size):
        self.span, self.size = span, size
        pad = -(-span // 128) * 128
        if (2 * span) % 128 == 0:
            self.step, self.v_at = span, span // 128 * 128
        else:
            self.step, self.v_at = pad, pad
        self.block = pad
        self.v_off = self.step - self.v_at
        self.q_at = 2 * self.step
        self.gain_at = self.q_at + span if self.step == span else 3 * pad
        self.width = -(-(self.gain_at + 2) // 128) * 128
        self.heads = span // size

    def keys(self, values):
        return values[..., : self.block]

    def values(self, values):
        return values[..., self.v_at : self.v_at + self.block]

    def queries(self, values):
        return values[..., self.q_at : self.q_at + self.block]

    def pack(self, keys, values):
        shared = self.block - self.v_at
        if not shared:
            return jnp.concatenate([keys, values], 1)
        return jnp.concatenate(
            [keys[:, : self.v_at], keys[:, self.v_at :] + values[:, :shared], values[:, shared:]], 1
        )

    def masks(self, rows, offset):
        lane = lax.broadcasted_iota(jnp.int32, (rows, self.block), 1) - offset
        return [
            (lane >= h * self.size) & (lane < (h + 1) * self.size) for h in range(self.heads)
        ]


def owned_heads(count, ring, per_ring, b):
    groups = count // ring
    return [((b % ring) * per_ring + j) * groups + b // ring for j in range(per_ring)]


def split_attn_kernel(lay, ring, per_ring, kv, query, gains, out):
    count, own, _ = out.shape
    width = query.shape[1]
    size = lay.size
    scaled = (query[...].astype(F32) * gains[:, 1:2]).astype(BF)
    both = kv[...]
    lane = lax.broadcasted_iota(jnp.int32, (own, lay.width - lay.gain_at), 1)
    tail = jnp.where(lane == 0, gains[:, 0:1], jnp.where(lane == 1, gains[:, 1:2], 0.0))
    tail = tail.astype(BF)
    for b in range(count):
        heads = owned_heads(count, ring, per_ring, b)
        pieces = []
        for source, base in ((both, 0), (both, width), (scaled, 0)):
            pieces += [source[:, base + h * size : base + (h + 1) * size] for h in heads]
            if lay.step > lay.span:
                pieces.append(jnp.zeros((own, lay.step - lay.span), BF))
        out[b] = jnp.concatenate(pieces + [tail], 1)


def split_ffn_kernel(w_in, w_down, gains, out):
    count, _, four = out.shape
    part = four // 4
    for b in range(count):
        for p in range(2):
            cols = slice((2 * b + p) * part, (2 * b + p + 1) * part)
            scaled = (w_in[:, cols].astype(F32) * gains[:, 2:3]).astype(BF)
            out[b, :, 2 * p * part : (2 * p + 1) * part] = scaled
            out[b, :, (2 * p + 1) * part : (2 * p + 2) * part] = w_down[:, cols]


def prepare_kernel(media, lats, out):
    rows = media.shape[0]
    out[:rows, :] = normalize(media[...].astype(F32))[0].astype(BF)
    out[rows:, :] = normalize(lats[...].astype(F32))[0].astype(BF)


def stacked(values, masks):
    return jnp.concatenate([jnp.where(m, values, jnp.zeros_like(values)) for m in masks], 0)


def unstacked(values, masks):
    rows = values.shape[0] // len(masks)
    total = jnp.zeros((rows, values.shape[1]), F32)
    for h, m in enumerate(masks):
        total = jnp.where(m, values[h * rows : (h + 1) * rows], total)
    return total


def patch_index(place_ref, count, media_rows, rows):
    column = lax.broadcasted_iota(jnp.int32, (rows, count * media_rows), 1)
    slot, row = column // media_rows, column % media_rows
    index = row
    for k in range(count):
        index = jnp.where(slot == k, place_ref[2 + k] * media_rows + row, index)
    return index


def scaled_columns(lay, w):
    row_media = w[:, lay.gain_at : lay.gain_at + 1].astype(F32)
    row_lat = w[:, lay.gain_at + 1 : lay.gain_at + 2].astype(F32)
    base = w[:, : lay.q_at].astype(F32)
    rest = w[:, lay.q_at :]
    return (base * row_media).astype(BF), jnp.concatenate([(base * row_lat).astype(BF), rest], 1)


def row_copies(slots, block_m, block_l, xm, xl):
    pairs = []
    for k, slot in enumerate(slots):
        pairs.append((slot.at[pl.ds(0, block_m)], xm.at[pl.ds(k * block_m, block_m)]))
        pairs.append((slot.at[pl.ds(block_m, block_l)], xl.at[pl.ds(k * block_l, block_l)]))
    return pairs


def out_copies(me, dz, near, far, held):
    planes, own, _ = near.shape
    core = me % 2
    pairs = []
    for source, which in ((near, core), (far, 1 - core)):
        for k in range(planes):
            at = pl.multiple_of(((dz ^ k) * 2 + which) * own, own)
            pairs.append((source.at[k], held.at[pl.ds(at, own)]))
    return pairs


def rows_of_heads(lay, member, wo_all, wo):
    at = pl.multiple_of(member * lay.span, lay.span)
    wo[...] = jnp.zeros(wo.shape, wo.dtype)
    wo[lay.v_off : lay.v_off + lay.span, :] = wo_all[pl.ds(at, lay.span), :]


def weight_copies(place_ref, weights, held):
    if len(weights) == 1:
        return [(weights[0], held)]
    return out_copies(place_ref[0], place_ref[1], *weights, held)


def forward_kernel(count, lay, place_ref, len_ref, *refs):
    slots, refs = refs[:count], refs[count:]
    w_hbm, kv_out, lat_out, att_out, lse_out, odd_out, low_out = refs[:7]
    xm, xl, w, wm, wl, kv_ref, lat_ref, att_ref, lse_ref, odd, low, sems, out_sems = refs[7:]
    images, media_rows = kv_ref.shape[1:3]
    lat_rows = lat_ref.shape[2]
    rows = count * lat_rows
    block_m, block_l = images * media_rows, images * lat_rows
    copies = begin([(w_hbm, w)] + row_copies(slots, block_m, block_l, xm, xl), sems)
    copies[0].wait()
    wm[...], wl[...] = scaled_columns(lay, w[...])
    step = max(1, count // 4)
    for k in range(0, count, step):
        for i in range(k, k + step):
            copies[1 + 2 * i].wait()
        proj = dot(xm[k * block_m : (k + step) * block_m, :], wm[...]).astype(BF)
        kv_ref[k : k + step] = proj.reshape(step, images, media_rows, lay.q_at)
    for k in range(count):
        copies[2 + 2 * k].wait()
    lat_ref[...] = dot(xl[...], wl[...]).reshape(lat_ref.shape)
    written = begin([(kv_ref, kv_out), (lat_ref, lat_out)], out_sems)

    scale = 1.0 / math.sqrt(lay.size)
    q_masks, v_masks = lay.masks(rows, 0), lay.masks(rows, lay.v_off)
    index = patch_index(place_ref, count, media_rows, lay.heads * rows)
    for i in range(images):
        kv = kv_ref[:, i].reshape(count * media_rows, lay.q_at)
        lat = lat_ref[:, i].reshape(rows, lay.width).astype(BF)
        queries = stacked(lay.queries(lat), q_masks)
        allowed = index < len_ref[i]
        scores = jnp.where(allowed, dot(queries, lay.keys(kv), NT) * scale, MASKED)
        lat_scores = dot(queries, lay.keys(lat), NT) * scale
        top = jnp.maximum(
            jnp.max(scores, -1, keepdims=True), jnp.max(lat_scores, -1, keepdims=True)
        )
        probs = jnp.where(allowed, jnp.exp(scores - top), 0.0)
        lat_probs = jnp.exp(lat_scores - top)
        denominator = jnp.sum(probs, -1, keepdims=True) + jnp.sum(lat_probs, -1, keepdims=True)
        weighted = dot(probs.astype(BF), lay.values(kv)) + dot(
            lat_probs.astype(BF), lay.values(lat)
        )
        attended = unstacked(weighted / denominator, v_masks)
        att_ref[:, i] = attended.reshape(count, lat_rows, lay.block)
        lse_ref[i] = jnp.broadcast_to(top + jnp.log(denominator), (lay.heads * rows, 128))
    half = count // 2
    for k in range(count):
        rounded = att_ref[k].reshape(block_l, lay.block).astype(BF)
        low[k] = rounded
        if k >= half:
            odd[k - half] = rounded
    pairs = [(odd, odd_out), (low, low_out), (att_ref, att_out), (lse_ref, lse_out)]
    written += begin(pairs, out_sems, 2)
    for copy in written:
        copy.wait()


def out_kernel(lay, ring, weights, place_ref, att_hbm, got, *refs):
    sources, outs, refs = refs[:weights], refs[weights : weights + 2], refs[weights + 2 :]
    wo_all, wo, wo_far, att, sems, *parts = refs
    half, rows = got.shape[:2]
    pairs = weight_copies(place_ref, sources, wo_all) + [(att_hbm.at[pl.ds(0, half)], att)]
    copies = begin(pairs, sems)
    for copy in copies:
        copy.wait()
    here = att[...].reshape(half * rows, lay.block)
    there = got[...].reshape(half * rows, lay.block)
    member = place_ref[0] % ring
    rows_of_heads(lay, member, wo_all, wo)
    rows_of_heads(lay, member ^ 1, wo_all, wo_far)
    written = []
    for at, step in column_steps(wo.shape[1]):
        cols = slice(at, at + step)
        total = dot(here, wo[:, cols]) + dot(there, wo_far[:, cols])
        values = [total[m * rows : (m + 1) * rows] for m in range(half)]
        put_slots(parts, outs, at, step, values, written)
    for copy in written:
        copy.wait()


def backward_kernel(count, lay, ring, weights, place_ref, len_ref, *refs):
    branch, sources, refs = refs[:count], refs[count : count + weights], refs[count + weights :]
    kv_hbm, lat_hbm, att_hbm, lse_hbm, dkv_ref, dlat_ref, dkv_odd, dlat_odd = refs[:8]
    br, kv_ref, lat_ref, wo_all, wo, att_ref, lse_ref, dwide, datt, sems = refs[8:]
    images, media_rows = kv_ref.shape[1:3]
    lat_rows = lat_ref.shape[2]
    rows = count * lat_rows
    block_m, block_l = images * media_rows, images * lat_rows
    pairs = weight_copies(place_ref, sources, wo_all)
    pairs += [(branch[k], br.at[pl.ds(k * block_l, block_l)]) for k in range(count)]
    ready = len(pairs)
    pairs += [(lat_hbm, lat_ref), (att_hbm, att_ref), (lse_hbm, lse_ref), (kv_hbm, kv_ref)]
    copies = begin(pairs, sems)
    for copy in copies[:ready]:
        copy.wait()
    rows_of_heads(lay, place_ref[0] % ring, wo_all, wo)
    datt[...] = dot(br[...], wo[...], NT).reshape(datt.shape)
    for copy in copies[ready:]:
        copy.wait()

    scale = 1.0 / math.sqrt(lay.size)
    q_masks, v_masks = lay.masks(rows, 0), lay.masks(rows, lay.v_off)
    index = patch_index(place_ref, count, media_rows, lay.heads * rows)
    for i in range(images):
        kv = kv_ref[:, i].reshape(count * media_rows, lay.q_at)
        lat = lat_ref[:, i].reshape(rows, lay.width).astype(BF)
        queries = stacked(lay.queries(lat), q_masks)
        grads = datt[:, i].reshape(rows, lay.block).astype(BF)
        attended = att_ref[:, i].reshape(rows, lay.block)
        grad_heads = stacked(grads, v_masks)
        delta = jnp.sum(stacked(grads.astype(F32) * attended, v_masks), -1, keepdims=True)
        total = lse_ref[i][:, :1]
        allowed = index < len_ref[i]
        scores = jnp.where(allowed, dot(queries, lay.keys(kv), NT) * scale, MASKED)
        lat_scores = dot(queries, lay.keys(lat), NT) * scale
        probs = jnp.where(allowed, jnp.exp(scores - total), 0.0)
        lat_probs = jnp.exp(lat_scores - total)
        score_grad = (probs * (dot(grad_heads, lay.values(kv), NT) - delta)).astype(BF)
        lat_score_grad = (lat_probs * (dot(grad_heads, lay.values(lat), NT) - delta)).astype(BF)
        query_grad = scale * unstacked(
            dot(score_grad, lay.keys(kv)) + dot(lat_score_grad, lay.keys(lat)), q_masks
        )
        dkv_ref[:, i] = (
            lay.pack(scale * dot(score_grad, queries, TN), dot(probs.astype(BF), grad_heads, TN))
            .astype(BF)
            .reshape(count, media_rows, lay.q_at)
        )
        dlat = jnp.concatenate(
            [
                lay.pack(
                    scale * dot(lat_score_grad, queries, TN),
                    dot(lat_probs.astype(BF), grad_heads, TN),
                ),
                query_grad,
            ],
            1,
        )
        dwide[:, i] = jnp.pad(dlat, ((0, 0), (0, lay.width - dlat.shape[1]))).reshape(
            count, lat_rows, lay.width
        )
    dlat_ref[...] = dwide[...].reshape(count * block_l, lay.width).astype(BF)
    half = count // 2
    for k in range(half):
        dkv_odd[k] = dkv_ref[half + k]
        dlat_odd[k] = dlat_ref[(half + k) * block_l : (half + k + 1) * block_l, :]


def input_grad_kernel(lay, *refs):
    ins, outs, refs = refs[:6], refs[6:8], refs[8:]
    dkv, dlat, w, w_far, sems, *parts = refs
    count, width, block_l = dkv.shape[0], dkv.shape[-1] // 2, dlat.shape[0] // dkv.shape[0]
    block_m = dkv.shape[1] * dkv.shape[2]
    steps = column_steps(w.shape[0])
    pairs = []
    for c, (media, lat) in enumerate(((ins[0], ins[1]), (ins[2], ins[3]))):
        pairs.append((lat.at[pl.ds(0, count * block_l)], dlat.at[:, pl.ds(c * lay.width, lay.width)]))
        pairs.append((media.at[pl.ds(0, count)], dkv.at[:, :, :, pl.ds(c * width, width)]))
    ready = len(pairs)
    for at, step in steps:
        here = pl.ds(at, step)
        pairs += [(ins[4].at[here], w.at[here]), (ins[5].at[here], w_far.at[here])]
    copies = begin(pairs, sems)
    for copy in copies[:ready]:
        copy.wait()
    media_rows = dkv[...].reshape(count * block_m, 2 * width)
    written = []
    for i, (at, step) in enumerate(steps):
        here = slice(at, at + step)
        copies[ready + 2 * i].wait()
        copies[ready + 2 * i + 1].wait()
        near, far = scaled_columns(lay, w[here, :]), scaled_columns(lay, w_far[here, :])
        back = dot(media_rows, jnp.concatenate([near[0], far[0]], 1), NT)
        lat = dot(dlat[...], jnp.concatenate([near[1], far[1]], 1), NT)
        values = []
        for m in range(count):
            rows = [back[m * block_m : (m + 1) * block_m], lat[m * block_l : (m + 1) * block_l]]
            values.append(jnp.concatenate(rows, 0))
        put_slots(parts, outs, at, step, values, written)
    for copy in written:
        copy.wait()


def attn_weight_grad_kernel(count, lay, ring, place_ref, *refs):
    slots, branch, refs = refs[:count], refs[count : 2 * count], refs[2 * count :]
    dkv_hbm, dlat_hbm, w_hbm, att_hbm, grads_out, out_keep, out_send = refs[:7]
    xm, xl, br, out_all, dkv, dlat, w, att, grads, sems, out_sems = refs[7:]
    images, media_rows = dkv.shape[1:3]
    block_m, block_l = images * media_rows, dlat.shape[0] // count
    pairs = [(branch[k], br.at[pl.ds(k * block_l, block_l)]) for k in range(count)]
    pairs += [(att_hbm, att), (dkv_hbm, dkv), (dlat_hbm, dlat)]
    ready = len(pairs)
    steps = column_steps(xm.shape[1])
    for at, step in steps:
        cols = pl.ds(at, step)
        pairs.append((w_hbm.at[cols], w.at[cols]))
        for source, target in row_copies(slots, block_m, block_l, xm, xl):
            pairs.append((source.at[:, cols], target.at[:, cols]))
    each = (len(pairs) - ready) // len(steps)
    copies = begin(pairs, sems)
    for copy in copies[: count + 1]:
        copy.wait()
    total = dot(att[...].reshape(count * block_l, lay.block), br[...], TN)
    total = total[lay.v_off : lay.v_off + lay.span]
    per_ring, own = out_keep.shape[0], out_keep.shape[1]
    for q in range(per_ring * ring):
        out_all[q] = total[q * own : (q + 1) * own].astype(BF)
    me = place_ref[0]
    for j in range(per_ring):
        for r in range(ring):
            piece = out_all[j * ring + ((me % ring) ^ r)]
            if r:
                out_send[r - 1, j] = piece
            else:
                out_keep[j] = piece
    for copy in copies[count + 1 : ready]:
        copy.wait()
    right = dkv[...].reshape(count * block_m, lay.q_at)
    written = []
    for i, (at, step) in enumerate(steps):
        for copy in copies[ready + i * each : ready + (i + 1) * each]:
            copy.wait()
        here = slice(at, at + step)
        g_media = dot(xm[:, here], right, TN)
        g_lat = dot(xl[:, here], dlat[...], TN)
        block = w[here, :].astype(F32)
        base = block[:, : lay.q_at]
        row_media = block[:, lay.gain_at : lay.gain_at + 1]
        row_lat = block[:, lay.gain_at + 1 : lay.gain_at + 2]
        gain_media = jnp.sum(g_media * base, 1, keepdims=True)
        gain_lat = jnp.sum(g_lat[:, : lay.q_at] * base, 1, keepdims=True)
        rest = g_lat[:, lay.q_at :]
        lane = lax.broadcasted_iota(jnp.int32, rest.shape, 1) + lay.q_at
        rest = jnp.where(lane == lay.gain_at, gain_media, rest)
        rest = jnp.where(lane == lay.gain_at + 1, gain_lat, rest)
        grads[here, : lay.q_at] = (
            g_media * row_media + g_lat[:, : lay.q_at] * row_lat
        ).astype(BF)
        grads[here, lay.q_at :] = rest.astype(BF)
        rows = pl.ds(at, step)
        written += begin([(grads.at[rows], grads_out.at[rows])], out_sems, i)
    for copy in written:
        copy.wait()


def mixed_kernel(keep, got, lats, mixed, normed):
    value = keep[...].astype(F32) + got[...].astype(F32) + lats[...].astype(F32)
    mixed[...] = value
    normed[...] = normalize(value)[0].astype(BF)


def erf_parts(values):
    cdf = 0.5 * (1.0 + lax.erf(values * 0.7071067811865476))
    return cdf, cdf + values * jnp.exp(-0.5 * values * values) * GAUSS_DENSITY


def side_copies(side, weights, held):
    part = held.shape[1] // 2
    if part % 128:
        return [(weights[side], held)]
    cols = pl.ds(side * part, part)
    return [(w.at[:, cols], held.at[:, pl.ds(i * part, part)]) for i, w in enumerate(weights)]


def ffn_kernel(half, *refs):
    rows_in, cots, weights = refs[:half], refs[half : 2 * half], refs[2 * half : 2 * half + 2]
    made, outs = refs[2 * half + 2 : 2 * half + 6], refs[2 * half + 6 : 2 * half + 8]
    x, c, w_in, w_down, hidden, pre_grad, sems, out_sems, *parts = refs[2 * half + 8 :]
    rows = rows_in[0].shape[0]
    pairs = [(r, x.at[pl.ds(k * rows, rows)]) for k, r in enumerate(rows_in)]
    pairs += side_copies(0, weights, w_in)
    ready = len(pairs)
    pairs += [(r, c.at[pl.ds(k * rows, rows)]) for k, r in enumerate(cots)]
    pairs += side_copies(1, weights, w_down)
    copies = begin(pairs, sems)
    for copy in copies[:ready]:
        copy.wait()
    pre = dot(x[...], w_in[...])
    cdf, slope = erf_parts(pre)
    hidden[...] = (pre * cdf).astype(BF)
    stored = begin(core_copies(hidden, made[:2]), out_sems)
    for copy in copies[ready:]:
        copy.wait()
    pre_grad[...] = (dot(c[...], w_down[...]) * slope).astype(BF)
    stored += begin(core_copies(pre_grad, made[2:]), out_sems, 2)
    back_through(pre_grad, w_in, half, outs, parts)
    for copy in stored:
        copy.wait()


def core_copies(held, outs):
    part = held.shape[1] // 2
    if part % 128:
        return [(held, outs[0])]
    return [(held.at[:, pl.ds(i * part, part)], out) for i, out in enumerate(outs)]


def back_through(left, w, half, outs, parts):
    rows = left.shape[0] // half
    written = []
    for at, step in column_steps(w.shape[0], 1):
        total = dot(left[...], w[at : at + step, :], NT)
        values = [total[m * rows : (m + 1) * rows] for m in range(half)]
        put_slots(parts, outs, at, step, values, written)
    for copy in written:
        copy.wait()


def down_kernel(half, own, far, w, w_far, keep, send, hidden, w_down, sems, *parts):
    part = hidden.shape[1] // 2
    pairs = side_copies(1, (w, w_far), w_down)
    if part % 128:
        pairs.append((own, hidden))
    else:
        pairs += [(r, hidden.at[:, pl.ds(i * part, part)]) for i, r in enumerate((own, far))]
    for copy in begin(pairs, sems):
        copy.wait()
    back_through(hidden, w_down, half, (keep, send), parts)


def ffn_weight_grad_kernel(count, *refs):
    rows_in, own, far, first = refs[:count], refs[count], refs[count + 1], refs[count + 2 : -4]
    out, x, right, sems = refs[-4:]
    part, deep = right.shape[1], own.shape[0]
    rows = rows_in[0].shape[0]
    pairs = [(own, right.at[pl.ds(0, deep)]), (far, right.at[pl.ds(deep, deep)])]
    pairs += [(r, x.at[pl.ds(k * rows, rows)]) for k, r in enumerate(rows_in)]
    for copy in begin(pairs, sems):
        copy.wait()
    for at, step in column_steps(x.shape[1], 2):
        here = slice(at, at + step)
        out[here, :part] = dot(x[:, here], right[...], TN).astype(BF)
    if first:
        out[:, part:] = first[0][...]


def total_kernel(at, left, right, out, a, b, sems):
    rows = pl.ds(at, a.shape[0])
    for copy in begin([(left.at[rows], a), (right.at[rows], b)], sems):
        copy.wait()
    out[...] = (a[...].astype(F32) + b[...].astype(F32)).astype(out.dtype)


def sum_planes_kernel(grads, out):
    planes, _, width = grads.shape
    for p in range(2):
        total = grads[p].astype(F32)
        for d in range(p + 2, planes, 2):
            total = total + grads[d].astype(F32)
        out[:, p * width : (p + 1) * width] = total.astype(BF)


def first_rows(keep, got, a, b, sems):
    rows = pl.ds(0, a.shape[0])
    for copy in begin([(keep.at[rows], a), (got.at[rows], b)], sems):
        copy.wait()
    return a[...].astype(F32) + b[...].astype(F32)


def resampled_kernel(keep, got, far, mixed, out, *held):
    total = mixed[...] + first_rows(keep, got, *held) + far[...].astype(F32)
    out[...] = total.astype(out.dtype)


def ffn_back_kernel(keep, got, far, mixed, cot, mixed_grad, branch, *held):
    normed, inverse = normalize(mixed[...])
    back = first_rows(keep, got, *held) + far[...].astype(F32)
    grad = cot[...].astype(F32) + norm_back(back, normed, inverse)
    mixed_grad[...] = grad
    branch[...] = grad.astype(BF)


def final_kernel(keep, got, media, lats, mixed_grad, media_grad, lat_grad):
    rows = media.shape[0]
    back = keep[...].astype(F32) + got[...].astype(F32)
    normed, inverse = normalize(media[...].astype(F32))
    media_grad[...] = norm_back(back[:rows], normed, inverse)
    normed, inverse = normalize(lats[...].astype(F32))
    lat_grad[...] = mixed_grad[...] + norm_back(back[rows:], normed, inverse)


def finish_ffn_kernel(grads, w_in, gains, in_grad, down_grad, gain_grad):
    part = in_grad.shape[1] // grads.shape[0] // 2
    total = jnp.zeros((w_in.shape[0], 1), F32)
    for b in range(grads.shape[0]):
        for p in range(2):
            cols = slice((2 * b + p) * part, (2 * b + p + 1) * part)
            at = 2 * p * part
            raw = grads[b, :, at : at + part].astype(F32)
            total = total + jnp.sum(raw * w_in[:, cols].astype(F32), 1, keepdims=True)
            in_grad[:, cols] = raw * gains[:, 2:3]
            down_grad[:, cols] = grads[b, :, at + part : at + 2 * part].astype(F32)
    gain_grad[...] = jnp.broadcast_to(total, gain_grad.shape)


def finish_attn_kernel(lay, ring, per_ring, rows, query, gains, q_grad, kv_grad, gain_grad):
    count, own, wide = rows.shape
    width = query.shape[1]
    size = lay.size
    slots = rows[:, :, wide - lay.width :]
    place = {}
    tail = jnp.zeros((own, lay.width - lay.gain_at), F32)
    for b in range(count):
        block = slots[b].astype(F32)
        for j, h in enumerate(owned_heads(count, ring, per_ring, b)):
            for i, at in enumerate((0, lay.step, lay.q_at)):
                place[i, h] = block[:, at + j * size : at + (j + 1) * size]
        tail = tail + block[:, lay.gain_at :]
    heads = width // size
    kv_grad[:, :width] = jnp.concatenate([place[0, h] for h in range(heads)], 1)
    kv_grad[:, width:] = jnp.concatenate([place[1, h] for h in range(heads)], 1)
    raw = jnp.concatenate([place[2, h] for h in range(heads)], 1)
    q_grad[...] = raw * gains[:, 1:2]
    of_query = jnp.sum(raw * query[...].astype(F32), 1, keepdims=True)
    lane = lax.broadcasted_iota(jnp.int32, gain_grad.shape, 1)
    gain_grad[...] = jnp.where(lane == 0, tail[:, 0:1], tail[:, 1:2] + of_query)


def body(
    latents,
    media,
    media_lengths,
    cotangent,
    query_weight,
    kv_weight,
    out_weight,
    in_weight,
    down_weight,
    media_gain,
    latent_gain,
    ffn_gain,
):
    images, lat_rows, width = latents.shape
    media_rows = media.shape[1]
    nb, nd = lax.axis_size("blk"), lax.axis_size("dp")
    half = nb // 2
    size = width // HEADS
    heads = HEADS // nb
    own = query_weight.shape[0]
    plane = nb * own
    span = heads * size
    lay = Layout(span, size)
    hidden_width = in_weight.shape[1]
    part = hidden_width // nb // 2
    me = lax.axis_index("blk").astype(jnp.int32)
    dz = lax.axis_index("dp").astype(jnp.int32)
    place = jnp.concatenate([jnp.stack([me, dz]), owners(me)])
    ring = size // own
    per_ring = nd // ring
    groups = nb // ring
    block_m, block_l = images * media_rows, images * lat_rows
    block = block_m + block_l
    all_m, all_l = nb * block_m, nb * block_l
    sems = pltpu.SemaphoreType.DMA

    gains = jnp.stack([media_gain, latent_gain, ffn_gain], 1).astype(F32)
    (attn_parts,) = call(
        partial(split_attn_kernel, lay, ring, per_ring), [((nb, own, lay.width), BF, "d")], "ddd"
    )(kv_weight, query_weight, gains)

    quick = ring == 2 and own % 16 == 0
    if quick:
        out_near = [out_weight] + [swap(out_weight, k, "dp") for k in range(1, nd)]
    else:
        ring_groups = [[g * ring + i for i in range(ring)] for g in range(groups)]
        out_w = lax.all_gather(out_weight, "dp", axis=0, tiled=False)
        out_w = lax.all_gather(out_w, "blk", axis=0, tiled=False, axis_index_groups=ring_groups)
        out_near = [out_w.transpose(1, 0, 2, 3).reshape(nd * ring * own, width)]

    mine = lax.all_to_all(attn_parts, "blk", 0, 0, tiled=True).reshape(plane, -1)
    attn_w = lax.all_gather(after(mine, *out_near), "dp", axis=0, tiled=True)

    media_flat = media.reshape(block_m, width)
    lat_flat = latents.reshape(block_l, width)
    cot_flat = cotangent.reshape(block_l, width)
    (normed,) = call(prepare_kernel, [((block, width), BF, "d")], "dd", cost=3)(
        after(media_flat, attn_parts), lat_flat
    )
    slots = gather_all(normed)
    cot_pair = jnp.concatenate([cot_flat, swap(cot_flat, 1, "dp")], 0)

    (ffn_parts,) = call(split_ffn_kernel, [((nb, own, 4 * part), BF, "d")], "ddd", cost=4, big=True)(
        after(in_weight, normed), down_weight, gains
    )
    ffn_mine = lax.all_to_all(after(ffn_parts, mine), "blk", 0, 0, tiled=True)
    ffn_mine = ffn_mine.reshape(plane, 4 * part)
    by_plane = jnp.stack(
        [ffn_mine[:, d % 2 * 2 * part : (d % 2 + 1) * 2 * part] for d in range(nd)]
    )
    ffn_w = lax.all_to_all(after(by_plane, *slots, attn_w, cot_pair), "dp", 0, 0, tiled=True)
    ffn_w = ffn_w.reshape(width, 2 * part)

    if quick:
        near = jnp.stack(out_near)
        out_w = [near, swap(near, 1)]
    else:
        out_w = out_near

    cot_kind = gather_kind(after(cot_pair, *slots))
    kv_shape = (nb, images, media_rows, lay.q_at)
    lat_shape = (nb, images, lat_rows, lay.width)
    att_shape = (nb, images, lat_rows, lay.block)
    lse_shape = (images, heads * nb * lat_rows, 128)
    odd_shape = (half, block_l, lay.block)
    low_shape = (nb, block_l, lay.block)
    shapes = [(kv_shape, BF), (lat_shape, F32), (att_shape, F32), (lse_shape, F32)]
    shapes += [(odd_shape, BF), (low_shape, BF)]
    kv, lat_proj, attended, totals, att_odd, att_low = call(
        partial(forward_kernel, nb, lay),
        [(shape, kind, "h") for shape, kind in shapes],
        "ss" + "h" * (nb + 1),
        [
            pltpu.VMEM((all_m, width), BF),
            pltpu.VMEM((all_l, width), BF),
            pltpu.VMEM((width, lay.width), BF),
            pltpu.VMEM((width, lay.q_at), BF),
            pltpu.VMEM((width, lay.width), BF),
        ]
        + [pltpu.VMEM(shape, kind) for shape, kind in shapes]
        + [sems((1 + 2 * nb,)), sems((6,))],
        big=True,
            cost=11,
    )(place, media_lengths, *slots, attn_w)

    def exchange(rows):
        return kept_and_sent((half // 2, rows, width))

    outs, scratch = exchange(block_l)
    parts = call(
        partial(out_kernel, lay, ring, len(out_w)),
        outs,
        "shd" + "h" * len(out_w),
        [
            pltpu.VMEM((nd * ring * own, width), BF),
            pltpu.VMEM((lay.block, width), BF),
            pltpu.VMEM((lay.block, width), BF),
            pltpu.VMEM(odd_shape, BF),
            sems((2 * nd + 1,)),
            *scratch,
        ],
        cost=3,
    )(place, att_low, swap(after(att_odd, *cot_kind[1:3]), 1), *out_w)
    mixed, ffn_in = call(
        mixed_kernel, [((block_l, width), F32, "d"), ((block_l, width), BF, "d")], "ddd"
    )(*scatter(parts, [lambda sent: cot_kind[3:]]), lat_flat)

    mid = block_l // 2
    in_kind = gather_kind(
        jnp.concatenate([ffn_in, swap(ffn_in[:mid], 1, "dp"), swap(ffn_in[mid:], 1, "dp")], 0)
    )
    ffn_far = swap(after(ffn_w, *in_kind[1:3]), 1)
    if part % 128:
        ffn_sides = [
            jnp.concatenate([ffn_w[:, i * part : (i + 1) * part], ffn_far[:, i * part : (i + 1) * part]], 1)
            for i in range(2)
        ]
    else:
        ffn_sides = [ffn_w, ffn_far]
    rows_pair = half * 2 * block_l
    outs, scratch = exchange(2 * block_l)
    cut = part % 128 == 0
    made_shape = (rows_pair, part if cut else 2 * part)
    spare_shape = made_shape if cut else (8, 128)
    hid_own, hid_far, pre_own, pre_far, *parts = call(
        partial(ffn_kernel, half),
        [(made_shape, BF, "h"), (spare_shape, BF, "h")] * 2 + outs,
        "h" * (2 * half + 2),
        [
            pltpu.VMEM((rows_pair, width), BF),
            pltpu.VMEM((rows_pair, width), BF),
            pltpu.VMEM((width, 2 * part), BF),
            pltpu.VMEM((width, 2 * part), BF),
            pltpu.VMEM((rows_pair, 2 * part), BF),
            pltpu.VMEM((rows_pair, 2 * part), BF),
            sems((2 * half + 4,)),
            sems((4,)),
            *scratch,
        ],
        room=14,
            cost=1,
    )(*in_kind, *cot_kind, *ffn_sides)

    def ffn_weight_grad(rows, own_rows, far_rows, *first):
        if not cut:
            own_rows, far_rows = own_rows[:, :part], own_rows[:, part:]
        return call(
            partial(ffn_weight_grad_kernel, nb),
            [((width, part * (1 + len(first))), BF, "d")],
            "h" * (nb + 2) + "d" * len(first),
            [
                pltpu.VMEM((2 * rows_pair, width), BF),
                pltpu.VMEM((2 * rows_pair, part), BF),
                sems((nb + 2,)),
            ],
            room=14,
            cost=4,
        )(*rows, own_rows, swap(far_rows, 1), *first)[0]

    few_rows = [pltpu.VMEM((block_l, width), BF)] * 2 + [sems((2,))]

    def total_far(left, right):
        return call(
            partial(total_kernel, block_l), [((block_l, width), BF, "d")], "hh", few_rows, cost=1
        )(left, right)[0]

    made = {}

    def beside_first(sent):
        made["down"] = ffn_weight_grad(with_other(cot_kind), after(hid_own, sent), hid_far)
        made["both"] = ffn_weight_grad(with_other(in_kind), pre_own, pre_far, made["down"])
        return (made["both"],)

    def beside_second(sent):
        outs, scratch = exchange(2 * block_l)
        made["parts"] = call(
            partial(down_kernel, half),
            outs,
            "hhhh",
            [
                pltpu.VMEM((rows_pair, 2 * part), BF),
                pltpu.VMEM((width, 2 * part), BF),
                sems((4,)),
                *scratch,
            ],
            cost=4,
        )(after(hid_own, sent), hid_far, *ffn_sides)
        return made["parts"]

    terms = scatter(parts, [beside_first, beside_second])
    pair_got = swap(total_far(*terms), 1, "dp")
    mixed_grad, branch = call(
        ffn_back_kernel,
        [((block_l, width), F32, "d"), ((block_l, width), BF, "d")],
        "hhddd",
        few_rows,
    )(*terms, pair_got, mixed, cot_flat)
    branch_slots = gather_all(branch)
    ffn_planes = lax.all_to_all(
        after(made["both"], branch).reshape(nd, plane, 2 * part), "dp", 0, 0, tiled=True
    )

    (ffn_rows,) = call(sum_planes_kernel, [((plane, 4 * part), BF, "d")], "d", cost=3)(ffn_planes)
    ffn_slots = lax.all_to_all(ffn_rows.reshape(nb, own, 4 * part), "blk", 0, 0, tiled=True)

    def keep_second(sent):
        made["second"] = sent
        return ()

    down_terms = scatter(made["parts"], [lambda sent: (), keep_second])

    dkv, dlat, dkv_odd, dlat_odd = call(
        partial(backward_kernel, nb, lay, ring, len(out_w)),
        [
            (kv_shape, BF, "d"),
            ((all_l, lay.width), BF, "d"),
            ((half, *kv_shape[1:]), BF, "d"),
            ((half, block_l, lay.width), BF, "d"),
        ],
        "ss" + "h" * (nb + len(out_w) + 4),
        [
            pltpu.VMEM((all_l, width), BF),
            pltpu.VMEM(kv_shape, BF),
            pltpu.VMEM(lat_shape, F32),
            pltpu.VMEM((nd * ring * own, width), BF),
            pltpu.VMEM((lay.block, width), BF),
            pltpu.VMEM(att_shape, F32),
            pltpu.VMEM(lse_shape, F32),
            pltpu.VMEM(lat_shape, F32),
            pltpu.VMEM(att_shape, F32),
            sems((nb + 2 * nd + 4,)),
        ],
        big=True,
            cost=1,
    )(place, media_lengths, *branch_slots, *out_w, kv, lat_proj, attended, totals)

    attn_grads, out_keep, out_send = call(
        partial(attn_weight_grad_kernel, nb, lay, ring),
        [
            ((width, lay.width), BF, "h"),
            ((per_ring, own, width), BF, "d"),
            ((ring - 1, per_ring, own, width), BF, "d"),
        ],
        "s" + "h" * (2 * nb + 4),
        [
            pltpu.VMEM((all_m, width), BF),
            pltpu.VMEM((all_l, width), BF),
            pltpu.VMEM((all_l, width), BF),
            pltpu.VMEM((per_ring * ring, own, width), BF),
            pltpu.VMEM(kv_shape, BF),
            pltpu.VMEM((all_l, lay.width), BF),
            pltpu.VMEM((width, lay.width), BF),
            pltpu.VMEM(low_shape, BF),
            pltpu.VMEM((width, lay.width), BF),
            sems((nb + 3 + 3 * (1 + 2 * nb),)),
            sems((3,)),
        ],
        big=True,
            cost=1,
    )(place, *slots, *branch_slots, after(dkv, *down_terms), dlat, attn_w, att_low)
    attn_sum = lax.psum_scatter(attn_grads, "dp", scatter_dimension=0, tiled=True)

    outs, scratch = exchange(block)
    parts = call(
        partial(input_grad_kernel, lay),
        outs,
        "hhhhhh",
        [
            pltpu.VMEM((half, *kv_shape[1:-1], 2 * lay.q_at), BF),
            pltpu.VMEM((half * block_l, 2 * lay.width), BF),
            pltpu.VMEM((width, lay.width), BF),
            pltpu.VMEM((width, lay.width), BF),
            sems((10,)),
            *scratch,
        ],
        big=True,
            cost=1,
    )(
        after(dkv, attn_grads),
        dlat,
        swap(dkv_odd, 1),
        swap(dlat_odd, 1).reshape(half * block_l, lay.width),
        attn_w,
        swap(attn_w, 1),
    )
    (resampled,) = call(resampled_kernel, [((block_l, width), BF, "d")], "hhdd", few_rows)(
        *down_terms, swap(total_far(*down_terms), 1, "dp"), mixed
    )

    pieces = [out_keep] + [swap(out_send[r - 1], r) for r in range(1, ring)]
    pieces = jnp.stack(pieces)
    rank = lax.axis_index("blk") % ring
    pieces = [lax.dynamic_index_in_dim(pieces, rank ^ r, 0, False) for r in range(ring)]
    out_rows = jnp.concatenate(pieces, 0).reshape(nd * own, width)
    in_grad, down_grad, ffn_gain_grad = call(
        finish_ffn_kernel,
        [((own, hidden_width), F32, "d")] * 2 + [((own, 128), F32, "d")],
        "ddd",
        cost=3,
    )(ffn_slots, in_weight, gains)

    media_grad, latents_grad = call(
        final_kernel, [((block_m, width), F32, "d"), ((block_l, width), F32, "d")], "ddddd", cost=5
    )(*scatter(parts, [lambda sent: (ffn_rows, resampled), lambda sent: (ffn_slots, out_rows)]), after(media_flat, in_grad), lat_flat, mixed_grad)

    attn_slots = lax.all_to_all(attn_sum.reshape(nb, own, -1), "blk", 0, 0, tiled=True)
    query_grad, kv_grad, gain_grads = call(
        partial(finish_attn_kernel, lay, ring, per_ring),
        [((own, width), F32, "d"), ((own, 2 * width), F32, "d"), ((own, 128), F32, "d")],
        "ddd",
    )(attn_slots, query_weight, gains)

    out_rows = after(out_rows, attn_sum)
    out_grad = lax.psum_scatter(out_rows, "dp", scatter_dimension=0, tiled=True).astype(F32)
    return (
        resampled.reshape(latents.shape),
        latents_grad.reshape(latents.shape),
        media_grad.reshape(media.shape),
        query_grad,
        kv_grad,
        out_grad,
        in_grad,
        down_grad,
        gain_grads[:, 0],
        gain_grads[:, 1],
        ffn_gain_grad[:, 0],
    )


def solution(mesh):
    rows = P("dp", "blk", None)
    weight = P(("dp", "blk"), None)
    gain = P(("dp", "blk"))
    return jax.shard_map(
        body,
        mesh=mesh,
        in_specs=(rows, rows, P("dp"), rows) + (weight,) * 5 + (gain,) * 3,
        out_specs=(rows,) * 3 + (weight,) * 5 + (gain,) * 3,
        check_vma=False,
    )
```

```python
from functools import partial
import math

import jax
import jax.numpy as jnp
from jax import lax
from jax.experimental import pallas as pl
from jax.experimental.pallas import tpu as pltpu
from jax.sharding import PartitionSpec as P

HEADS = 16
NORM_EPS = 1e-05
MASKED = -1e30
GAUSS_DENSITY = 0.3989422804014327
BF = jnp.bfloat16
F32 = jnp.float32
MIB = 1 << 20
VMEM_MIB = 56
NT = ((1,), (1,))
TN = ((0,), (0,))


def chip_bits():
    return lax.axis_size("blk").bit_length() - 2


def hop_bit(j, core):
    return 2 << ((j + core) % chip_bits())


def hop(array, j):
    return lax.ppermute(
        array, "blk", [(i, i ^ hop_bit(j, i % 2)) for i in range(lax.axis_size("blk"))]
    )


def swap(array, bit, axis="blk"):
    return lax.ppermute(array, axis, [(i, i ^ bit) for i in range(lax.axis_size(axis))])


def gather_kind(block):
    blocks = [block]
    for j in range(chip_bits()):
        blocks = blocks + [hop(b, j) for b in blocks]
    return blocks


def gather_all(block):
    return with_other(gather_kind(block))


def with_other(blocks):
    return blocks + [swap(b, 1) for b in blocks]


def owners(me):
    tables = []
    for core in range(2):
        steps = [hop_bit(j, core) for j in range(chip_bits())]
        tables.append(
            [sum(s for j, s in enumerate(steps) if m >> j & 1) for m in range(1 << len(steps))]
        )
    both = [tables[c] + [1 ^ k for k in tables[1 - c]] for c in range(2)]
    return me ^ jnp.where(me % 2 == 0, jnp.array(both[0]), jnp.array(both[1])).astype(jnp.int32)


def after(array, *others):
    return lax.optimization_barrier((array, *others))[0]


def dot(left, right, dims=((1,), (0,))):
    return lax.dot_general(left, right, (dims, ((), ())), preferred_element_type=F32)


def padded_bytes(shape, kind):
    item = jnp.dtype(kind).itemsize
    *lead, rows, lanes = (1, *shape) if len(shape) == 1 else shape
    tile = 32 // item
    return math.prod(lead) * (-(-rows // tile) * tile) * (-(-lanes // 128) * 128) * item


def begin(pairs, sems, first=0):
    copies = [pltpu.make_async_copy(s, d, sems.at[first + i]) for i, (s, d) in enumerate(pairs)]
    for copy in copies:
        copy.start()
    return copies


def call(kernel, outs, spaces, scratch=(), cost=2, big=False, room=6):
    fetched = [i for i, letter in enumerate(spaces) if letter == "d"]
    stored = [i for i, out in enumerate(outs) if out[2] == "d"]
    first = len(spaces)
    last = first + len(outs)
    sems = pltpu.SemaphoreType.DMA

    def run(*operands):
        held = [pltpu.VMEM(operands[i].shape, operands[i].dtype) for i in fetched]
        made = [pltpu.VMEM(outs[i][0], outs[i][1]) for i in stored]
        size = sum(
            padded_bytes(b.shape, b.dtype)
            for b in (*scratch, *held, *made)
            if b.memory_space == pltpu.VMEM
        )

        def whole(*refs):
            at = last + len(scratch)
            own, extra = list(refs[:at]), list(refs[at:])
            out_sems, in_sems = extra.pop(), extra.pop()
            held_refs, made_refs = extra[: len(fetched)], extra[len(fetched) :]
            copies = begin([(own[i], r) for i, r in zip(fetched, held_refs)], in_sems)
            results = [(r, own[first + i]) for i, r in zip(stored, made_refs)]
            for i, r in zip(fetched, held_refs):
                own[i] = r
            for i, r in zip(stored, made_refs):
                own[first + i] = r
            for copy in copies:
                copy.wait()
            kernel(*own)
            for copy in begin(results, out_sems):
                copy.wait()

        return pl.pallas_call(
            whole,
            out_shape=[jax.ShapeDtypeStruct(shape, kind) for shape, kind, _ in outs],
            in_specs=[
                pl.BlockSpec(memory_space=pltpu.SMEM if s == "s" else pltpu.HBM) for s in spaces
            ],
            out_specs=[pl.BlockSpec(memory_space=pltpu.HBM)] * len(outs),
            scratch_shapes=[
                *scratch,
                *held,
                *made,
                sems((max(1, len(fetched)),)),
                sems((max(1, len(stored)),)),
            ],
            compiler_params=pltpu.CompilerParams(vmem_limit_bytes=VMEM_MIB * MIB if big else size + room * MIB),
            cost_estimate=pl.CostEstimate(
                flops=int(cost * 1.15e9), bytes_accessed=int(cost * 3.6e6), transcendentals=0
            ),
        )(*operands)

    return run


def column_steps(width, steps=3):
    step = width // steps if width % (128 * steps) == 0 else width
    return [(at, step) for at in range(0, width, step)]


def kept_and_sent(shape):
    return [(shape, BF, "h")] * 2, [
        pltpu.VMEM(shape, BF),
        pltpu.VMEM(shape, BF),
        pltpu.SemaphoreType.DMA((6,)),
    ]


def put_slots(parts, outs, at, step, values, written):
    kept, sent, sems = parts
    half = kept.shape[0]
    for m, value in enumerate(values):
        (sent if m // half else kept)[m % half, :, at : at + step] = value.astype(BF)
    for source, target in ((kept, outs[0]), (sent, outs[1])):
        cols = pl.ds(at, step)
        copy = pltpu.make_async_copy(
            source.at[:, :, cols], target.at[:, :, cols], sems.at[len(written)]
        )
        copy.start()
        written.append(copy)


def fold_kernel(kept, got, keep, send, left, right, low, high, sems):
    slots = left.shape[0]
    half = slots // 2
    order = [m for i in range(half) for m in (i + half, i)]
    pairs = [(r.at[m], h.at[m]) for m in order for r, h in ((kept, left), (got, right))]
    copies = begin(pairs, sems)
    written = []
    for i, m in enumerate(order):
        copies[2 * i].wait()
        copies[2 * i + 1].wait()
        total = (left[m].astype(F32) + right[m].astype(F32)).astype(BF)
        held, out = (high, send) if m >= half else (low, keep)
        held[m % half] = total
        copy = pltpu.make_async_copy(held.at[m % half], out.at[m % half], sems.at[2 * slots + i])
        copy.start()
        written.append(copy)
    for copy in written:
        copy.wait()


def fold(kept, got):
    slots, rows, width = kept.shape
    half = (slots // 2, rows, width)
    return call(
        fold_kernel,
        [(half, BF, "h")] * 2,
        "hh",
        [
            pltpu.VMEM(kept.shape, BF),
            pltpu.VMEM(kept.shape, BF),
            pltpu.VMEM(half, BF),
            pltpu.VMEM(half, BF),
            pltpu.SemaphoreType.DMA((3 * slots,)),
        ],
        cost=2,
    )(kept, got)


def scatter(parts, hooks=()):
    kept, sent = parts
    hooks = list(hooks)
    for j in reversed(range(chip_bits())):
        got = hop(sent, j)
        if hooks:
            got = after(got, *hooks.pop(0)(sent))
        if j:
            kept, sent = fold(kept, got)
    return kept[0], got[0]


def normalize(values):
    center = values - jnp.mean(values, -1, keepdims=True)
    inverse = lax.rsqrt(jnp.mean(center * center, -1, keepdims=True) + NORM_EPS)
    return (center * inverse, inverse)


def norm_back(grad_norm, normed, inverse):
    return inverse * (
        grad_norm
        - jnp.mean(grad_norm, -1, keepdims=True)
        - normed * jnp.mean(grad_norm * normed, -1, keepdims=True)
    )


class Layout:
    def __init__(self, span, size):
        self.span, self.size = span, size
        pad = -(-span // 128) * 128
        if (2 * span) % 128 == 0:
            self.step, self.v_at = span, span // 128 * 128
        else:
            self.step, self.v_at = pad, pad
        self.block = pad
        self.v_off = self.step - self.v_at
        self.q_at = 2 * self.step
        self.gain_at = self.q_at + span if self.step == span else 3 * pad
        self.width = -(-(self.gain_at + 2) // 128) * 128
        self.heads = span // size

    def keys(self, values):
        return values[..., : self.block]

    def values(self, values):
        return values[..., self.v_at : self.v_at + self.block]

    def queries(self, values):
        return values[..., self.q_at : self.q_at + self.block]

    def pack(self, keys, values):
        shared = self.block - self.v_at
        if not shared:
            return jnp.concatenate([keys, values], 1)
        return jnp.concatenate(
            [keys[:, : self.v_at], keys[:, self.v_at :] + values[:, :shared], values[:, shared:]], 1
        )

    def masks(self, rows, offset):
        lane = lax.broadcasted_iota(jnp.int32, (rows, self.block), 1) - offset
        return [
            (lane >= h * self.size) & (lane < (h + 1) * self.size) for h in range(self.heads)
        ]


def owned_heads(count, ring, per_ring, b):
    groups = count // ring
    return [((b % ring) * per_ring + j) * groups + b // ring for j in range(per_ring)]


def split_attn_kernel(lay, ring, per_ring, kv, query, gains, out):
    count, own, _ = out.shape
    width = query.shape[1]
    size = lay.size
    scaled = (query[...].astype(F32) * gains[:, 1:2]).astype(BF)
    both = kv[...]
    lane = lax.broadcasted_iota(jnp.int32, (own, lay.width - lay.gain_at), 1)
    tail = jnp.where(lane == 0, gains[:, 0:1], jnp.where(lane == 1, gains[:, 1:2], 0.0))
    tail = tail.astype(BF)
    for b in range(count):
        heads = owned_heads(count, ring, per_ring, b)
        pieces = []
        for source, base in ((both, 0), (both, width), (scaled, 0)):
            pieces += [source[:, base + h * size : base + (h + 1) * size] for h in heads]
            if lay.step > lay.span:
                pieces.append(jnp.zeros((own, lay.step - lay.span), BF))
        out[b] = jnp.concatenate(pieces + [tail], 1)


def split_ffn_kernel(w_in, w_down, gains, out):
    count, _, four = out.shape
    part = four // 4
    for b in range(count):
        for p in range(2):
            cols = slice((2 * b + p) * part, (2 * b + p + 1) * part)
            scaled = (w_in[:, cols].astype(F32) * gains[:, 2:3]).astype(BF)
            out[b, :, 2 * p * part : (2 * p + 1) * part] = scaled
            out[b, :, (2 * p + 1) * part : (2 * p + 2) * part] = w_down[:, cols]


def prepare_kernel(media, lats, out):
    rows = media.shape[0]
    out[:rows, :] = normalize(media[...].astype(F32))[0].astype(BF)
    out[rows:, :] = normalize(lats[...].astype(F32))[0].astype(BF)


def stacked(values, masks):
    return jnp.concatenate([jnp.where(m, values, jnp.zeros_like(values)) for m in masks], 0)


def unstacked(values, masks):
    rows = values.shape[0] // len(masks)
    total = jnp.zeros((rows, values.shape[1]), F32)
    for h, m in enumerate(masks):
        total = jnp.where(m, values[h * rows : (h + 1) * rows], total)
    return total


def patch_index(place_ref, count, media_rows, rows):
    column = lax.broadcasted_iota(jnp.int32, (rows, count * media_rows), 1)
    slot, row = column // media_rows, column % media_rows
    index = row
    for k in range(count):
        index = jnp.where(slot == k, place_ref[2 + k] * media_rows + row, index)
    return index


def scaled_columns(lay, w):
    row_media = w[:, lay.gain_at : lay.gain_at + 1].astype(F32)
    row_lat = w[:, lay.gain_at + 1 : lay.gain_at + 2].astype(F32)
    base = w[:, : lay.q_at].astype(F32)
    rest = w[:, lay.q_at :]
    return (base * row_media).astype(BF), jnp.concatenate([(base * row_lat).astype(BF), rest], 1)


def row_copies(slots, block_m, block_l, xm, xl):
    pairs = []
    for k, slot in enumerate(slots):
        pairs.append((slot.at[pl.ds(0, block_m)], xm.at[pl.ds(k * block_m, block_m)]))
        pairs.append((slot.at[pl.ds(block_m, block_l)], xl.at[pl.ds(k * block_l, block_l)]))
    return pairs


def out_copies(me, dz, near, far, held):
    planes, own, _ = near.shape
    core = me % 2
    pairs = []
    for source, which in ((near, core), (far, 1 - core)):
        for k in range(planes):
            at = pl.multiple_of(((dz ^ k) * 2 + which) * own, own)
            pairs.append((source.at[k], held.at[pl.ds(at, own)]))
    return pairs


def rows_of_heads(lay, member, wo_all, wo):
    at = pl.multiple_of(member * lay.span, lay.span)
    wo[...] = jnp.zeros(wo.shape, wo.dtype)
    wo[lay.v_off : lay.v_off + lay.span, :] = wo_all[pl.ds(at, lay.span), :]


def weight_copies(place_ref, weights, held):
    if len(weights) == 1:
        return [(weights[0], held)]
    return out_copies(place_ref[0], place_ref[1], *weights, held)


def forward_kernel(count, lay, place_ref, len_ref, *refs):
    slots, refs = refs[:count], refs[count:]
    w_hbm, kv_out, lat_out, att_out, lse_out, odd_out, low_out = refs[:7]
    xm, xl, w, wm, wl, kv_ref, lat_ref, att_ref, lse_ref, odd, low, sems, out_sems = refs[7:]
    images, media_rows = kv_ref.shape[1:3]
    lat_rows = lat_ref.shape[2]
    rows = count * lat_rows
    block_m, block_l = images * media_rows, images * lat_rows
    copies = begin([(w_hbm, w)] + row_copies(slots, block_m, block_l, xm, xl), sems)
    copies[0].wait()
    wm[...], wl[...] = scaled_columns(lay, w[...])
    step = max(1, count // 4)
    for k in range(0, count, step):
        for i in range(k, k + step):
            copies[1 + 2 * i].wait()
        proj = dot(xm[k * block_m : (k + step) * block_m, :], wm[...]).astype(BF)
        kv_ref[k : k + step] = proj.reshape(step, images, media_rows, lay.q_at)
    for k in range(count):
        copies[2 + 2 * k].wait()
    lat_ref[...] = dot(xl[...], wl[...]).reshape(lat_ref.shape)
    written = begin([(kv_ref, kv_out), (lat_ref, lat_out)], out_sems)

    scale = 1.0 / math.sqrt(lay.size)
    q_masks, v_masks = lay.masks(rows, 0), lay.masks(rows, lay.v_off)
    index = patch_index(place_ref, count, media_rows, lay.heads * rows)
    for i in range(images):
        kv = kv_ref[:, i].reshape(count * media_rows, lay.q_at)
        lat = lat_ref[:, i].reshape(rows, lay.width).astype(BF)
        queries = stacked(lay.queries(lat), q_masks)
        allowed = index < len_ref[i]
        scores = jnp.where(allowed, dot(queries, lay.keys(kv), NT) * scale, MASKED)
        lat_scores = dot(queries, lay.keys(lat), NT) * scale
        top = jnp.maximum(
            jnp.max(scores, -1, keepdims=True), jnp.max(lat_scores, -1, keepdims=True)
        )
        probs = jnp.where(allowed, jnp.exp(scores - top), 0.0)
        lat_probs = jnp.exp(lat_scores - top)
        denominator = jnp.sum(probs, -1, keepdims=True) + jnp.sum(lat_probs, -1, keepdims=True)
        weighted = dot(probs.astype(BF), lay.values(kv)) + dot(
            lat_probs.astype(BF), lay.values(lat)
        )
        attended = unstacked(weighted / denominator, v_masks)
        att_ref[:, i] = attended.reshape(count, lat_rows, lay.block)
        lse_ref[i] = jnp.broadcast_to(top + jnp.log(denominator), (lay.heads * rows, 128))
    half = count // 2
    for k in range(count):
        rounded = att_ref[k].reshape(block_l, lay.block).astype(BF)
        low[k] = rounded
        if k >= half:
            odd[k - half] = rounded
    pairs = [(odd, odd_out), (low, low_out), (att_ref, att_out), (lse_ref, lse_out)]
    written += begin(pairs, out_sems, 2)
    for copy in written:
        copy.wait()


def out_kernel(lay, ring, weights, place_ref, att_hbm, got, *refs):
    sources, outs, refs = refs[:weights], refs[weights : weights + 2], refs[weights + 2 :]
    wo_all, wo, wo_far, att, sems, *parts = refs
    half, rows = got.shape[:2]
    pairs = weight_copies(place_ref, sources, wo_all) + [(att_hbm.at[pl.ds(0, half)], att)]
    copies = begin(pairs, sems)
    for copy in copies:
        copy.wait()
    here = att[...].reshape(half * rows, lay.block)
    there = got[...].reshape(half * rows, lay.block)
    member = place_ref[0] % ring
    rows_of_heads(lay, member, wo_all, wo)
    rows_of_heads(lay, member ^ 1, wo_all, wo_far)
    written = []
    for at, step in column_steps(wo.shape[1]):
        cols = slice(at, at + step)
        total = dot(here, wo[:, cols]) + dot(there, wo_far[:, cols])
        values = [total[m * rows : (m + 1) * rows] for m in range(half)]
        put_slots(parts, outs, at, step, values, written)
    for copy in written:
        copy.wait()


def backward_kernel(count, lay, ring, weights, place_ref, len_ref, *refs):
    branch, sources, refs = refs[:count], refs[count : count + weights], refs[count + weights :]
    kv_hbm, lat_hbm, att_hbm, lse_hbm, dkv_ref, dlat_ref, dkv_odd, dlat_odd = refs[:8]
    br, kv_ref, lat_ref, wo_all, wo, att_ref, lse_ref, dwide, datt, sems = refs[8:]
    images, media_rows = kv_ref.shape[1:3]
    lat_rows = lat_ref.shape[2]
    rows = count * lat_rows
    block_m, block_l = images * media_rows, images * lat_rows
    pairs = weight_copies(place_ref, sources, wo_all)
    pairs += [(branch[k], br.at[pl.ds(k * block_l, block_l)]) for k in range(count)]
    ready = len(pairs)
    pairs += [(lat_hbm, lat_ref), (att_hbm, att_ref), (lse_hbm, lse_ref), (kv_hbm, kv_ref)]
    copies = begin(pairs, sems)
    for copy in copies[:ready]:
        copy.wait()
    rows_of_heads(lay, place_ref[0] % ring, wo_all, wo)
    datt[...] = dot(br[...], wo[...], NT).reshape(datt.shape)
    for copy in copies[ready:]:
        copy.wait()

    scale = 1.0 / math.sqrt(lay.size)
    q_masks, v_masks = lay.masks(rows, 0), lay.masks(rows, lay.v_off)
    index = patch_index(place_ref, count, media_rows, lay.heads * rows)
    for i in range(images):
        kv = kv_ref[:, i].reshape(count * media_rows, lay.q_at)
        lat = lat_ref[:, i].reshape(rows, lay.width).astype(BF)
        queries = stacked(lay.queries(lat), q_masks)
        grads = datt[:, i].reshape(rows, lay.block).astype(BF)
        attended = att_ref[:, i].reshape(rows, lay.block)
        grad_heads = stacked(grads, v_masks)
        delta = jnp.sum(stacked(grads.astype(F32) * attended, v_masks), -1, keepdims=True)
        total = lse_ref[i][:, :1]
        allowed = index < len_ref[i]
        scores = jnp.where(allowed, dot(queries, lay.keys(kv), NT) * scale, MASKED)
        lat_scores = dot(queries, lay.keys(lat), NT) * scale
        probs = jnp.where(allowed, jnp.exp(scores - total), 0.0)
        lat_probs = jnp.exp(lat_scores - total)
        score_grad = (probs * (dot(grad_heads, lay.values(kv), NT) - delta)).astype(BF)
        lat_score_grad = (lat_probs * (dot(grad_heads, lay.values(lat), NT) - delta)).astype(BF)
        query_grad = scale * unstacked(
            dot(score_grad, lay.keys(kv)) + dot(lat_score_grad, lay.keys(lat)), q_masks
        )
        dkv_ref[:, i] = (
            lay.pack(scale * dot(score_grad, queries, TN), dot(probs.astype(BF), grad_heads, TN))
            .astype(BF)
            .reshape(count, media_rows, lay.q_at)
        )
        dlat = jnp.concatenate(
            [
                lay.pack(
                    scale * dot(lat_score_grad, queries, TN),
                    dot(lat_probs.astype(BF), grad_heads, TN),
                ),
                query_grad,
            ],
            1,
        )
        dwide[:, i] = jnp.pad(dlat, ((0, 0), (0, lay.width - dlat.shape[1]))).reshape(
            count, lat_rows, lay.width
        )
    dlat_ref[...] = dwide[...].reshape(count * block_l, lay.width).astype(BF)
    half = count // 2
    for k in range(half):
        dkv_odd[k] = dkv_ref[half + k]
        dlat_odd[k] = dlat_ref[(half + k) * block_l : (half + k + 1) * block_l, :]


def input_grad_kernel(lay, *refs):
    ins, outs, refs = refs[:6], refs[6:8], refs[8:]
    dkv, dlat, w, w_far, sems, *parts = refs
    count, width, block_l = dkv.shape[0], dkv.shape[-1] // 2, dlat.shape[0] // dkv.shape[0]
    block_m = dkv.shape[1] * dkv.shape[2]
    steps = column_steps(w.shape[0])
    pairs = []
    for c, (media, lat) in enumerate(((ins[0], ins[1]), (ins[2], ins[3]))):
        pairs.append((lat.at[pl.ds(0, count * block_l)], dlat.at[:, pl.ds(c * lay.width, lay.width)]))
        pairs.append((media.at[pl.ds(0, count)], dkv.at[:, :, :, pl.ds(c * width, width)]))
    ready = len(pairs)
    for at, step in steps:
        here = pl.ds(at, step)
        pairs += [(ins[4].at[here], w.at[here]), (ins[5].at[here], w_far.at[here])]
    copies = begin(pairs, sems)
    for copy in copies[:ready]:
        copy.wait()
    media_rows = dkv[...].reshape(count * block_m, 2 * width)
    written = []
    for i, (at, step) in enumerate(steps):
        here = slice(at, at + step)
        copies[ready + 2 * i].wait()
        copies[ready + 2 * i + 1].wait()
        near, far = scaled_columns(lay, w[here, :]), scaled_columns(lay, w_far[here, :])
        back = dot(media_rows, jnp.concatenate([near[0], far[0]], 1), NT)
        lat = dot(dlat[...], jnp.concatenate([near[1], far[1]], 1), NT)
        values = []
        for m in range(count):
            rows = [back[m * block_m : (m + 1) * block_m], lat[m * block_l : (m + 1) * block_l]]
            values.append(jnp.concatenate(rows, 0))
        put_slots(parts, outs, at, step, values, written)
    for copy in written:
        copy.wait()


def attn_weight_grad_kernel(count, lay, ring, place_ref, *refs):
    slots, branch, refs = refs[:count], refs[count : 2 * count], refs[2 * count :]
    dkv_hbm, dlat_hbm, w_hbm, att_hbm, grads_out, out_keep, out_send = refs[:7]
    xm, xl, br, out_all, dkv, dlat, w, att, grads, sems, out_sems = refs[7:]
    images, media_rows = dkv.shape[1:3]
    block_m, block_l = images * media_rows, dlat.shape[0] // count
    pairs = [(branch[k], br.at[pl.ds(k * block_l, block_l)]) for k in range(count)]
    pairs += [(att_hbm, att), (dkv_hbm, dkv), (dlat_hbm, dlat)]
    ready = len(pairs)
    steps = column_steps(xm.shape[1])
    for at, step in steps:
        cols = pl.ds(at, step)
        pairs.append((w_hbm.at[cols], w.at[cols]))
        for source, target in row_copies(slots, block_m, block_l, xm, xl):
            pairs.append((source.at[:, cols], target.at[:, cols]))
    each = (len(pairs) - ready) // len(steps)
    copies = begin(pairs, sems)
    for copy in copies[: count + 1]:
        copy.wait()
    total = dot(att[...].reshape(count * block_l, lay.block), br[...], TN)
    total = total[lay.v_off : lay.v_off + lay.span]
    per_ring, own = out_keep.shape[0], out_keep.shape[1]
    for q in range(per_ring * ring):
        out_all[q] = total[q * own : (q + 1) * own].astype(BF)
    me = place_ref[0]
    for j in range(per_ring):
        for r in range(ring):
            piece = out_all[j * ring + ((me % ring) ^ r)]
            if r:
                out_send[r - 1, j] = piece
            else:
                out_keep[j] = piece
    for copy in copies[count + 1 : ready]:
        copy.wait()
    right = dkv[...].reshape(count * block_m, lay.q_at)
    written = []
    for i, (at, step) in enumerate(steps):
        for copy in copies[ready + i * each : ready + (i + 1) * each]:
            copy.wait()
        here = slice(at, at + step)
        g_media = dot(xm[:, here], right, TN)
        g_lat = dot(xl[:, here], dlat[...], TN)
        block = w[here, :].astype(F32)
        base = block[:, : lay.q_at]
        row_media = block[:, lay.gain_at : lay.gain_at + 1]
        row_lat = block[:, lay.gain_at + 1 : lay.gain_at + 2]
        gain_media = jnp.sum(g_media * base, 1, keepdims=True)
        gain_lat = jnp.sum(g_lat[:, : lay.q_at] * base, 1, keepdims=True)
        rest = g_lat[:, lay.q_at :]
        lane = lax.broadcasted_iota(jnp.int32, rest.shape, 1) + lay.q_at
        rest = jnp.where(lane == lay.gain_at, gain_media, rest)
        rest = jnp.where(lane == lay.gain_at + 1, gain_lat, rest)
        grads[here, : lay.q_at] = (
            g_media * row_media + g_lat[:, : lay.q_at] * row_lat
        ).astype(BF)
        grads[here, lay.q_at :] = rest.astype(BF)
        rows = pl.ds(at, step)
        written += begin([(grads.at[rows], grads_out.at[rows])], out_sems, i)
    for copy in written:
        copy.wait()


def mixed_kernel(keep, got, lats, mixed, normed):
    value = keep[...].astype(F32) + got[...].astype(F32) + lats[...].astype(F32)
    mixed[...] = value
    normed[...] = normalize(value)[0].astype(BF)


def erf_parts(values):
    cdf = 0.5 * (1.0 + lax.erf(values * 0.7071067811865476))
    return cdf, cdf + values * jnp.exp(-0.5 * values * values) * GAUSS_DENSITY


def side_copies(side, weights, held):
    part = held.shape[1] // 2
    if part % 128:
        return [(weights[side], held)]
    cols = pl.ds(side * part, part)
    return [(w.at[:, cols], held.at[:, pl.ds(i * part, part)]) for i, w in enumerate(weights)]


def ffn_kernel(half, *refs):
    rows_in, cots, weights = refs[:half], refs[half : 2 * half], refs[2 * half : 2 * half + 2]
    made, outs = refs[2 * half + 2 : 2 * half + 6], refs[2 * half + 6 : 2 * half + 8]
    x, c, w_in, w_down, hidden, pre_grad, sems, out_sems, *parts = refs[2 * half + 8 :]
    rows = rows_in[0].shape[0]
    pairs = [(r, x.at[pl.ds(k * rows, rows)]) for k, r in enumerate(rows_in)]
    pairs += side_copies(0, weights, w_in)
    ready = len(pairs)
    pairs += [(r, c.at[pl.ds(k * rows, rows)]) for k, r in enumerate(cots)]
    pairs += side_copies(1, weights, w_down)
    copies = begin(pairs, sems)
    for copy in copies[:ready]:
        copy.wait()
    pre = dot(x[...], w_in[...])
    cdf, slope = erf_parts(pre)
    hidden[...] = (pre * cdf).astype(BF)
    stored = begin(core_copies(hidden, made[:2]), out_sems)
    for copy in copies[ready:]:
        copy.wait()
    pre_grad[...] = (dot(c[...], w_down[...]) * slope).astype(BF)
    stored += begin(core_copies(pre_grad, made[2:]), out_sems, 2)
    back_through(pre_grad, w_in, half, outs, parts)
    for copy in stored:
        copy.wait()


def core_copies(held, outs):
    part = held.shape[1] // 2
    if part % 128:
        return [(held, outs[0])]
    return [(held.at[:, pl.ds(i * part, part)], out) for i, out in enumerate(outs)]


def back_through(left, w, half, outs, parts):
    rows = left.shape[0] // half
    written = []
    for at, step in column_steps(w.shape[0], 1):
        total = dot(left[...], w[at : at + step, :], NT)
        values = [total[m * rows : (m + 1) * rows] for m in range(half)]
        put_slots(parts, outs, at, step, values, written)
    for copy in written:
        copy.wait()


def down_kernel(half, own, far, w, w_far, keep, send, hidden, w_down, sems, *parts):
    part = hidden.shape[1] // 2
    pairs = side_copies(1, (w, w_far), w_down)
    if part % 128:
        pairs.append((own, hidden))
    else:
        pairs += [(r, hidden.at[:, pl.ds(i * part, part)]) for i, r in enumerate((own, far))]
    for copy in begin(pairs, sems):
        copy.wait()
    back_through(hidden, w_down, half, (keep, send), parts)


def ffn_weight_grad_kernel(count, *refs):
    rows_in, own, far, first = refs[:count], refs[count], refs[count + 1], refs[count + 2 : -4]
    out, x, right, sems = refs[-4:]
    part, deep = right.shape[1], own.shape[0]
    rows = rows_in[0].shape[0]
    pairs = [(own, right.at[pl.ds(0, deep)]), (far, right.at[pl.ds(deep, deep)])]
    pairs += [(r, x.at[pl.ds(k * rows, rows)]) for k, r in enumerate(rows_in)]
    for copy in begin(pairs, sems):
        copy.wait()
    for at, step in column_steps(x.shape[1], 2):
        here = slice(at, at + step)
        out[here, :part] = dot(x[:, here], right[...], TN).astype(BF)
    if first:
        out[:, part:] = first[0][...]


def total_kernel(at, left, right, out, a, b, sems):
    rows = pl.ds(at, a.shape[0])
    for copy in begin([(left.at[rows], a), (right.at[rows], b)], sems):
        copy.wait()
    out[...] = (a[...].astype(F32) + b[...].astype(F32)).astype(out.dtype)


def sum_planes_kernel(grads, out):
    planes, _, width = grads.shape
    for p in range(2):
        total = grads[p].astype(F32)
        for d in range(p + 2, planes, 2):
            total = total + grads[d].astype(F32)
        out[:, p * width : (p + 1) * width] = total.astype(BF)


def first_rows(keep, got, a, b, sems):
    rows = pl.ds(0, a.shape[0])
    for copy in begin([(keep.at[rows], a), (got.at[rows], b)], sems):
        copy.wait()
    return a[...].astype(F32) + b[...].astype(F32)


def resampled_kernel(keep, got, far, mixed, out, *held):
    total = mixed[...] + first_rows(keep, got, *held) + far[...].astype(F32)
    out[...] = total.astype(out.dtype)


def ffn_back_kernel(keep, got, far, mixed, cot, mixed_grad, branch, *held):
    normed, inverse = normalize(mixed[...])
    back = first_rows(keep, got, *held) + far[...].astype(F32)
    grad = cot[...].astype(F32) + norm_back(back, normed, inverse)
    mixed_grad[...] = grad
    branch[...] = grad.astype(BF)


def final_kernel(keep, got, media, lats, mixed_grad, media_grad, lat_grad):
    rows = media.shape[0]
    back = keep[...].astype(F32) + got[...].astype(F32)
    normed, inverse = normalize(media[...].astype(F32))
    media_grad[...] = norm_back(back[:rows], normed, inverse)
    normed, inverse = normalize(lats[...].astype(F32))
    lat_grad[...] = mixed_grad[...] + norm_back(back[rows:], normed, inverse)


def finish_ffn_kernel(grads, w_in, gains, in_grad, down_grad, gain_grad):
    part = in_grad.shape[1] // grads.shape[0] // 2
    total = jnp.zeros((w_in.shape[0], 1), F32)
    for b in range(grads.shape[0]):
        for p in range(2):
            cols = slice((2 * b + p) * part, (2 * b + p + 1) * part)
            at = 2 * p * part
            raw = grads[b, :, at : at + part].astype(F32)
            total = total + jnp.sum(raw * w_in[:, cols].astype(F32), 1, keepdims=True)
            in_grad[:, cols] = raw * gains[:, 2:3]
            down_grad[:, cols] = grads[b, :, at + part : at + 2 * part].astype(F32)
    gain_grad[...] = jnp.broadcast_to(total, gain_grad.shape)


def finish_attn_kernel(lay, ring, per_ring, rows, query, gains, q_grad, kv_grad, gain_grad):
    count, own, wide = rows.shape
    width = query.shape[1]
    size = lay.size
    slots = rows[:, :, wide - lay.width :]
    place = {}
    tail = jnp.zeros((own, lay.width - lay.gain_at), F32)
    for b in range(count):
        block = slots[b].astype(F32)
        for j, h in enumerate(owned_heads(count, ring, per_ring, b)):
            for i, at in enumerate((0, lay.step, lay.q_at)):
                place[i, h] = block[:, at + j * size : at + (j + 1) * size]
        tail = tail + block[:, lay.gain_at :]
    heads = width // size
    kv_grad[:, :width] = jnp.concatenate([place[0, h] for h in range(heads)], 1)
    kv_grad[:, width:] = jnp.concatenate([place[1, h] for h in range(heads)], 1)
    raw = jnp.concatenate([place[2, h] for h in range(heads)], 1)
    q_grad[...] = raw * gains[:, 1:2]
    of_query = jnp.sum(raw * query[...].astype(F32), 1, keepdims=True)
    lane = lax.broadcasted_iota(jnp.int32, gain_grad.shape, 1)
    gain_grad[...] = jnp.where(lane == 0, tail[:, 0:1], tail[:, 1:2] + of_query)


def body(
    latents,
    media,
    media_lengths,
    cotangent,
    query_weight,
    kv_weight,
    out_weight,
    in_weight,
    down_weight,
    media_gain,
    latent_gain,
    ffn_gain,
):
    images, lat_rows, width = latents.shape
    media_rows = media.shape[1]
    nb, nd = lax.axis_size("blk"), lax.axis_size("dp")
    half = nb // 2
    size = width // HEADS
    heads = HEADS // nb
    own = query_weight.shape[0]
    plane = nb * own
    span = heads * size
    lay = Layout(span, size)
    hidden_width = in_weight.shape[1]
    part = hidden_width // nb // 2
    me = lax.axis_index("blk").astype(jnp.int32)
    dz = lax.axis_index("dp").astype(jnp.int32)
    place = jnp.concatenate([jnp.stack([me, dz]), owners(me)])
    ring = size // own
    per_ring = nd // ring
    groups = nb // ring
    block_m, block_l = images * media_rows, images * lat_rows
    block = block_m + block_l
    all_m, all_l = nb * block_m, nb * block_l
    sems = pltpu.SemaphoreType.DMA

    gains = jnp.stack([media_gain, latent_gain, ffn_gain], 1).astype(F32)
    (attn_parts,) = call(
        partial(split_attn_kernel, lay, ring, per_ring), [((nb, own, lay.width), BF, "d")], "ddd"
    )(kv_weight, query_weight, gains)

    quick = ring == 2 and own % 16 == 0
    if quick:
        out_near = [out_weight] + [swap(out_weight, k, "dp") for k in range(1, nd)]
    else:
        ring_groups = [[g * ring + i for i in range(ring)] for g in range(groups)]
        out_w = lax.all_gather(out_weight, "dp", axis=0, tiled=False)
        out_w = lax.all_gather(out_w, "blk", axis=0, tiled=False, axis_index_groups=ring_groups)
        out_near = [out_w.transpose(1, 0, 2, 3).reshape(nd * ring * own, width)]

    mine = lax.all_to_all(attn_parts, "blk", 0, 0, tiled=True).reshape(plane, -1)
    attn_w = lax.all_gather(after(mine, *out_near), "dp", axis=0, tiled=True)

    media_flat = media.reshape(block_m, width)
    lat_flat = latents.reshape(block_l, width)
    cot_flat = cotangent.reshape(block_l, width)
    (normed,) = call(prepare_kernel, [((block, width), BF, "d")], "dd", cost=3)(
        after(media_flat, attn_parts), lat_flat
    )
    slots = gather_all(normed)
    cot_pair = jnp.concatenate([cot_flat, swap(cot_flat, 1, "dp")], 0)

    (ffn_parts,) = call(split_ffn_kernel, [((nb, own, 4 * part), BF, "d")], "ddd", cost=4, big=True)(
        after(in_weight, normed), down_weight, gains
    )
    ffn_mine = lax.all_to_all(after(ffn_parts, mine), "blk", 0, 0, tiled=True)
    ffn_mine = ffn_mine.reshape(plane, 4 * part)
    by_plane = jnp.stack(
        [ffn_mine[:, d % 2 * 2 * part : (d % 2 + 1) * 2 * part] for d in range(nd)]
    )
    ffn_w = lax.all_to_all(after(by_plane, *slots, cot_pair), "dp", 0, 0, tiled=True)
    ffn_w = ffn_w.reshape(width, 2 * part)

    if quick:
        near = jnp.stack(out_near)
        out_w = [near, swap(near, 1)]
    else:
        out_w = out_near

    cot_kind = gather_kind(after(cot_pair, *slots))
    kv_shape = (nb, images, media_rows, lay.q_at)
    lat_shape = (nb, images, lat_rows, lay.width)
    att_shape = (nb, images, lat_rows, lay.block)
    lse_shape = (images, heads * nb * lat_rows, 128)
    odd_shape = (half, block_l, lay.block)
    low_shape = (nb, block_l, lay.block)
    shapes = [(kv_shape, BF), (lat_shape, F32), (att_shape, F32), (lse_shape, F32)]
    shapes += [(odd_shape, BF), (low_shape, BF)]
    kv, lat_proj, attended, totals, att_odd, att_low = call(
        partial(forward_kernel, nb, lay),
        [(shape, kind, "h") for shape, kind in shapes],
        "ss" + "h" * (nb + 1),
        [
            pltpu.VMEM((all_m, width), BF),
            pltpu.VMEM((all_l, width), BF),
            pltpu.VMEM((width, lay.width), BF),
            pltpu.VMEM((width, lay.q_at), BF),
            pltpu.VMEM((width, lay.width), BF),
        ]
        + [pltpu.VMEM(shape, kind) for shape, kind in shapes]
        + [sems((1 + 2 * nb,)), sems((6,))],
        big=True,
            cost=11,
    )(place, media_lengths, *slots, attn_w)

    def exchange(rows):
        return kept_and_sent((half // 2, rows, width))

    outs, scratch = exchange(block_l)
    parts = call(
        partial(out_kernel, lay, ring, len(out_w)),
        outs,
        "shd" + "h" * len(out_w),
        [
            pltpu.VMEM((nd * ring * own, width), BF),
            pltpu.VMEM((lay.block, width), BF),
            pltpu.VMEM((lay.block, width), BF),
            pltpu.VMEM(odd_shape, BF),
            sems((2 * nd + 1,)),
            *scratch,
        ],
        cost=3,
    )(place, att_low, swap(after(att_odd, *cot_kind[1:3]), 1), *out_w)
    mixed, ffn_in = call(
        mixed_kernel, [((block_l, width), F32, "d"), ((block_l, width), BF, "d")], "ddd"
    )(*scatter(parts, [lambda sent: cot_kind[3:]]), lat_flat)

    mid = block_l // 2
    in_kind = gather_kind(
        jnp.concatenate([ffn_in, swap(ffn_in[:mid], 1, "dp"), swap(ffn_in[mid:], 1, "dp")], 0)
    )
    ffn_far = swap(after(ffn_w, *in_kind[1:2]), 1)
    if part % 128:
        ffn_sides = [
            jnp.concatenate([ffn_w[:, i * part : (i + 1) * part], ffn_far[:, i * part : (i + 1) * part]], 1)
            for i in range(2)
        ]
    else:
        ffn_sides = [ffn_w, ffn_far]
    rows_pair = half * 2 * block_l
    outs, scratch = exchange(2 * block_l)
    cut = part % 128 == 0
    made_shape = (rows_pair, part if cut else 2 * part)
    spare_shape = made_shape if cut else (8, 128)
    hid_own, hid_far, pre_own, pre_far, *parts = call(
        partial(ffn_kernel, half),
        [(made_shape, BF, "h"), (spare_shape, BF, "h")] * 2 + outs,
        "h" * (2 * half + 2),
        [
            pltpu.VMEM((rows_pair, width), BF),
            pltpu.VMEM((rows_pair, width), BF),
            pltpu.VMEM((width, 2 * part), BF),
            pltpu.VMEM((width, 2 * part), BF),
            pltpu.VMEM((rows_pair, 2 * part), BF),
            pltpu.VMEM((rows_pair, 2 * part), BF),
            sems((2 * half + 4,)),
            sems((4,)),
            *scratch,
        ],
        room=14,
            cost=1,
    )(*in_kind, *cot_kind, *ffn_sides)

    def ffn_weight_grad(rows, own_rows, far_rows, *first):
        if not cut:
            own_rows, far_rows = own_rows[:, :part], own_rows[:, part:]
        return call(
            partial(ffn_weight_grad_kernel, nb),
            [((width, part * (1 + len(first))), BF, "d")],
            "h" * (nb + 2) + "d" * len(first),
            [
                pltpu.VMEM((2 * rows_pair, width), BF),
                pltpu.VMEM((2 * rows_pair, part), BF),
                sems((nb + 2,)),
            ],
            room=14,
            cost=4,
        )(*rows, own_rows, swap(far_rows, 1), *first)[0]

    few_rows = [pltpu.VMEM((block_l, width), BF)] * 2 + [sems((2,))]

    def total_far(left, right):
        return call(
            partial(total_kernel, block_l), [((block_l, width), BF, "d")], "hh", few_rows, cost=1
        )(left, right)[0]

    made = {}

    def beside_first(sent):
        made["down"] = ffn_weight_grad(with_other(cot_kind), after(hid_own, sent), hid_far)
        made["both"] = ffn_weight_grad(with_other(in_kind), pre_own, pre_far, made["down"])
        return (made["both"],)

    def beside_second(sent):
        outs, scratch = exchange(2 * block_l)
        made["parts"] = call(
            partial(down_kernel, half),
            outs,
            "hhhh",
            [
                pltpu.VMEM((rows_pair, 2 * part), BF),
                pltpu.VMEM((width, 2 * part), BF),
                sems((4,)),
                *scratch,
            ],
            cost=4,
        )(after(hid_own, sent), hid_far, *ffn_sides)
        return made["parts"]

    terms = scatter(parts, [beside_first, beside_second])
    pair_got = swap(total_far(*terms), 1, "dp")
    mixed_grad, branch = call(
        ffn_back_kernel,
        [((block_l, width), F32, "d"), ((block_l, width), BF, "d")],
        "hhddd",
        few_rows,
    )(*terms, pair_got, mixed, cot_flat)
    branch_slots = gather_all(branch)
    ffn_planes = lax.all_to_all(
        after(made["both"], branch).reshape(nd, plane, 2 * part), "dp", 0, 0, tiled=True
    )

    (ffn_rows,) = call(sum_planes_kernel, [((plane, 4 * part), BF, "d")], "d", cost=3)(ffn_planes)
    ffn_slots = lax.all_to_all(ffn_rows.reshape(nb, own, 4 * part), "blk", 0, 0, tiled=True)

    def keep_second(sent):
        made["second"] = sent
        return ()

    down_terms = scatter(made["parts"], [lambda sent: (), keep_second])

    dkv, dlat, dkv_odd, dlat_odd = call(
        partial(backward_kernel, nb, lay, ring, len(out_w)),
        [
            (kv_shape, BF, "d"),
            ((all_l, lay.width), BF, "d"),
            ((half, *kv_shape[1:]), BF, "d"),
            ((half, block_l, lay.width), BF, "d"),
        ],
        "ss" + "h" * (nb + len(out_w) + 4),
        [
            pltpu.VMEM((all_l, width), BF),
            pltpu.VMEM(kv_shape, BF),
            pltpu.VMEM(lat_shape, F32),
            pltpu.VMEM((nd * ring * own, width), BF),
            pltpu.VMEM((lay.block, width), BF),
            pltpu.VMEM(att_shape, F32),
            pltpu.VMEM(lse_shape, F32),
            pltpu.VMEM(lat_shape, F32),
            pltpu.VMEM(att_shape, F32),
            sems((nb + 2 * nd + 4,)),
        ],
        big=True,
            cost=1,
    )(place, media_lengths, *branch_slots, *out_w, kv, lat_proj, attended, totals)

    attn_grads, out_keep, out_send = call(
        partial(attn_weight_grad_kernel, nb, lay, ring),
        [
            ((width, lay.width), BF, "h"),
            ((per_ring, own, width), BF, "d"),
            ((ring - 1, per_ring, own, width), BF, "d"),
        ],
        "s" + "h" * (2 * nb + 4),
        [
            pltpu.VMEM((all_m, width), BF),
            pltpu.VMEM((all_l, width), BF),
            pltpu.VMEM((all_l, width), BF),
            pltpu.VMEM((per_ring * ring, own, width), BF),
            pltpu.VMEM(kv_shape, BF),
            pltpu.VMEM((all_l, lay.width), BF),
            pltpu.VMEM((width, lay.width), BF),
            pltpu.VMEM(low_shape, BF),
            pltpu.VMEM((width, lay.width), BF),
            sems((nb + 3 + 3 * (1 + 2 * nb),)),
            sems((3,)),
        ],
        big=True,
            cost=1,
    )(place, *slots, *branch_slots, after(dkv, *down_terms), dlat, attn_w, att_low)
    attn_sum = lax.psum_scatter(attn_grads, "dp", scatter_dimension=0, tiled=True)

    outs, scratch = exchange(block)
    parts = call(
        partial(input_grad_kernel, lay),
        outs,
        "hhhhhh",
        [
            pltpu.VMEM((half, *kv_shape[1:-1], 2 * lay.q_at), BF),
            pltpu.VMEM((half * block_l, 2 * lay.width), BF),
            pltpu.VMEM((width, lay.width), BF),
            pltpu.VMEM((width, lay.width), BF),
            sems((10,)),
            *scratch,
        ],
        big=True,
            cost=1,
    )(
        after(dkv, attn_grads),
        dlat,
        swap(dkv_odd, 1),
        swap(dlat_odd, 1).reshape(half * block_l, lay.width),
        attn_w,
        swap(attn_w, 1),
    )
    (resampled,) = call(resampled_kernel, [((block_l, width), BF, "d")], "hhdd", few_rows)(
        *down_terms, swap(total_far(*down_terms), 1, "dp"), mixed
    )

    pieces = [out_keep] + [swap(out_send[r - 1], r) for r in range(1, ring)]
    pieces = jnp.stack(pieces)
    rank = lax.axis_index("blk") % ring
    pieces = [lax.dynamic_index_in_dim(pieces, rank ^ r, 0, False) for r in range(ring)]
    out_rows = jnp.concatenate(pieces, 0).reshape(nd * own, width)
    in_grad, down_grad, ffn_gain_grad = call(
        finish_ffn_kernel,
        [((own, hidden_width), F32, "d")] * 2 + [((own, 128), F32, "d")],
        "ddd",
        cost=8,
    )(ffn_slots, in_weight, gains)

    media_grad, latents_grad = call(
        final_kernel, [((block_m, width), F32, "d"), ((block_l, width), F32, "d")], "ddddd", cost=5
    )(*scatter(parts, [lambda sent: (ffn_rows, resampled), lambda sent: (ffn_slots, out_rows)]), after(media_flat, in_grad), lat_flat, mixed_grad)

    attn_slots = lax.all_to_all(attn_sum.reshape(nb, own, -1), "blk", 0, 0, tiled=True)
    query_grad, kv_grad, gain_grads = call(
        partial(finish_attn_kernel, lay, ring, per_ring),
        [((own, width), F32, "d"), ((own, 2 * width), F32, "d"), ((own, 128), F32, "d")],
        "ddd",
    )(attn_slots, query_weight, gains)

    out_rows = after(out_rows, attn_sum)
    out_grad = lax.psum_scatter(out_rows, "dp", scatter_dimension=0, tiled=True).astype(F32)
    return (
        resampled.reshape(latents.shape),
        latents_grad.reshape(latents.shape),
        media_grad.reshape(media.shape),
        query_grad,
        kv_grad,
        out_grad,
        in_grad,
        down_grad,
        gain_grads[:, 0],
        gain_grads[:, 1],
        ffn_gain_grad[:, 0],
    )


def solution(mesh):
    rows = P("dp", "blk", None)
    weight = P(("dp", "blk"), None)
    gain = P(("dp", "blk"))
    return jax.shard_map(
        body,
        mesh=mesh,
        in_specs=(rows, rows, P("dp"), rows) + (weight,) * 5 + (gain,) * 3,
        out_specs=(rows,) * 3 + (weight,) * 5 + (gain,) * 3,
        check_vma=False,
    )
```
